32 devices in a mesh: dp: 4 (over z), seq: 8 (over y, x, core).
Axes of the slice: x: 2, y: 2, z: 4, core: 2. Of those that a mesh axis runs over, the one named last changes fastest.
Arguments:
- tokens: bfloat16 [8, 512, 2048], P('dp', 'seq'), may hold values from -6 to 6
- segments: int32 [8, 512], P('dp', 'seq'), may hold values from 0 to 2, as said below
- ln1_gain: bfloat16 [2048], P(('dp', 'seq')), may hold values from 0.099609375 to 1.8984375
- ln1_bias: bfloat16 [2048], P(('dp', 'seq')), may hold values from -1.75 to 1.75
- qkv_weight: bfloat16 [2048, 6144], P(('dp', 'seq')), may hold values from -0.125 to 0.125
- qkv_bias: bfloat16 [6144], P(('dp', 'seq')), may hold values from -1.75 to 1.75
- out_weight: bfloat16 [2048, 2048], P(('dp', 'seq')), may hold values from -1 to 1
- out_bias: bfloat16 [2048], P(('dp', 'seq')), may hold values from -3 to 3
- ln2_gain: bfloat16 [2048], P(('dp', 'seq')), may hold values from 0.099609375 to 1.8984375
- ln2_bias: bfloat16 [2048], P(('dp', 'seq')), may hold values from -1.75 to 1.75
- fc1_weight: bfloat16 [2048, 8192], P(('dp', 'seq')), may hold values from -0.125 to 0.125
- fc1_bias: bfloat16 [8192], P(('dp', 'seq')), may hold values from -3 to 3
- fc2_weight: bfloat16 [8192, 2048], P(('dp', 'seq')), may hold values from -0.0625 to 0.0625
- fc2_bias: bfloat16 [2048], P(('dp', 'seq')), may hold values from -3 to 3
- cotangent: bfloat16 [8, 512, 2048], P('dp', 'seq'), may hold values from -8 to 8
Outputs:
- mixed: bfloat16 [8, 512, 2048], P('dp', 'seq')
- grad_tokens: bfloat16 [8, 512, 2048], P('dp', 'seq')
- grad_ln1_gain: float32 [2048], P(('dp', 'seq'))
- grad_ln1_bias: float32 [2048], P(('dp', 'seq'))
- grad_qkv_weight: float32 [2048, 6144], P(('dp', 'seq'))
- grad_qkv_bias: float32 [6144], P(('dp', 'seq'))
- grad_out_weight: float32 [2048, 2048], P(('dp', 'seq'))
- grad_out_bias: float32 [2048], P(('dp', 'seq'))
- grad_ln2_gain: float32 [2048], P(('dp', 'seq'))
- grad_ln2_bias: float32 [2048], P(('dp', 'seq'))
- grad_fc1_weight: float32 [2048, 8192], P(('dp', 'seq'))
- grad_fc1_bias: float32 [8192], P(('dp', 'seq'))
- grad_fc2_weight: float32 [8192, 2048], P(('dp', 'seq'))
- grad_fc2_bias: float32 [2048], P(('dp', 'seq'))
The draws below stay inside these ranges and needn't reach their ends.
Inputs may be any that keep to these rules, and one draw needn't show every extreme that they name: `segments`: within each sequence the segment numbers start at 0 and never fall; every document but a sequence's last has 200 to 2000 tokens; of the 2 sequences on each index of dp, one is a single document, and every other sequence holds two documents or more; some sequence may be packed with documents of equal length.
All inputs are finite; a program needn't handle non-finite values.
Results may differ from the reference program's by a relative error of at most 0.029.
Values may be sent and summed in bfloat16 or wider, within the bound.
No kernel may reach another device: no remote copies, remote signals or barrier semaphores. Data moves between devices by JAX's collectives and lax.ppermute only.
A program may use at most 384 MiB of HBM per device.

```python
import jax
import jax.numpy as jnp
from jax import lax

D = 2048
HEADS = 8
HD = 256
ROT = 64
FF = 8192
SEQ_GRP = 2
DOC_MIN = 200
DOC_MAX = 2000
SEQS = 8
LEN = 512


def draw_segments(key, part):
    key = jax.random.fold_in(key, 7)
    length_key, first_key, pick_key = jax.random.split(key, 3)
    doc_count = LEN // DOC_MIN + 1
    first_cap = min(DOC_MAX, LEN // 2)
    later = jax.random.randint(length_key, (SEQS, doc_count), DOC_MIN, DOC_MAX + 1)
    first = jax.random.randint(first_key, (SEQS, 1), DOC_MIN, first_cap + 1)
    lengths = jnp.concatenate([first, later[:, 1:]], axis=1)
    group_count = SEQS // SEQ_GRP
    chosen = jax.random.randint(pick_key, (group_count,), 0, SEQ_GRP)
    row_ids = jnp.arange(SEQS, dtype=jnp.int32)
    packed_row = (chosen[0] + 1) % SEQ_GRP
    lengths = jnp.where((row_ids == packed_row)[:, None], DOC_MIN, lengths)
    bounds = jnp.cumsum(lengths, axis=1)
    places = jnp.arange(LEN, dtype=jnp.int32)
    numbers = jnp.sum((bounds[:, None, :] <= places[None, :, None]).astype(jnp.int32), axis=2)
    rows_in_group = row_ids % SEQ_GRP
    single_doc = rows_in_group == jnp.repeat(chosen, SEQ_GRP)
    return jnp.where(single_doc[:, None], 0, numbers).astype(jnp.int32)


def with_spikes(array, key, source, target, parts, factor):
    owner, partner = [(jnp.arange(array.shape[axis_at]) // (array.shape[axis_at] // parts)).reshape([-1 if axis == axis_at else 1 for axis in range(array.ndim)]) for axis_at in (source, target)]
    chosen = jax.random.permutation(key, parts)[partner]
    strong = (owner == chosen) | (owner == (partner + parts // 2) % parts)
    return jnp.where(strong, factor * array, array)


def shard_levels(stream_key, shape, pieces, least, top_value):
    level, own = 1.0, jax.random.fold_in(stream_key, 6)
    for dim, blocks in pieces:
        steps = jnp.exp(jax.random.uniform(jax.random.fold_in(own, dim), (blocks,), jnp.float32, least / len(pieces), top_value / len(pieces)))
        level = level * jnp.repeat(steps, shape[dim] // blocks).reshape([-1 if axis == dim else 1 for axis in range(len(shape))])
    return level


def centred(own_key, shape, width, bound, shards=(), kind=jnp.bfloat16):
    array = width * jax.random.normal(own_key, shape, jnp.float32)
    if shards:
        array = array * shard_levels(own_key, shape, shards, -0.22, 0.18)
    return jnp.clip(array, -bound, bound).astype(kind)


def noise_with(own_key, dims, scale, reach, cuts, heavy, kind=jnp.bfloat16):
    drawn = scale * jax.random.normal(own_key, dims, jnp.float32)
    if cuts:
        drawn = drawn * shard_levels(own_key, dims, cuts, -0.22, 0.18)
    return jnp.clip(with_spikes(drawn, jax.random.fold_in(own_key, 3), *heavy), -reach, reach).astype(kind)


def setup_inputs(seed: int = 0) -> dict:
    keys = jax.random.split(jax.random.key(seed), 16)
    return {
        "tokens": centred(keys[0], (SEQS, LEN, D), 1.0, 6.0, ((0, 4), (1, 8))),
        "segments": draw_segments(jax.random.fold_in(keys[15], 71), 0),
        "ln1_gain": jnp.clip(1.0 + 0.18 * jax.random.normal(keys[2], (D,), jnp.float32), 0.099609375, 1.8984375).astype(jnp.bfloat16),
        "ln1_bias": centred(keys[3], (D,), 0.3, 1.75, ((0, 32),)),
        "qkv_weight": centred(keys[4], (D, 3 * D), D ** -0.5, 0.125, ((0, 32),)),
        "qkv_bias": centred(keys[5], (3 * D,), 0.3, 1.75, ((0, 32),)),
        "out_weight": centred(keys[6], (D, D), (D // 64) ** -0.5, 1.0, ((0, 32),)),
        "out_bias": centred(keys[7], (D,), 0.5, 3.0, ((0, 32),)),
        "ln2_gain": jnp.clip(1.0 + 0.18 * jax.random.normal(keys[8], (D,), jnp.float32), 0.099609375, 1.8984375).astype(jnp.bfloat16),
        "ln2_bias": centred(keys[9], (D,), 0.3, 1.75, ((0, 32),)),
        "fc1_weight": centred(keys[10], (D, FF), D ** -0.5, 0.125, ((0, 32),)),
        "fc1_bias": centred(keys[11], (FF,), 0.5, 3.0, ((0, 32),)),
        "fc2_weight": centred(keys[12], (FF, D), FF ** -0.5, 0.0625, ((0, 32),)),
        "fc2_bias": centred(keys[13], (D,), 0.5, 3.0, ((0, 32),)),
        "cotangent": noise_with(keys[14], (SEQS, LEN, D), 1.0, 8.0, ((0, 4), (1, 8)), (1, 2, 8, 2.0)),
    }


@jax.custom_vjp
def low(v):
    return lax.optimization_barrier(v.astype(jnp.bfloat16)).astype(jnp.float32)

@jax.custom_vjp
def low_back(v):
    return v

def low_keep(v):
    return (low(v), None)

def low_pass(kept, grad):
    return (grad,)

def back_keep(v):
    return (v, None)

def back_low(kept, grad):
    return (low(grad),)
low.defvjp(low_keep, low_pass)
low_back.defvjp(back_keep, back_low)
epsilon = 1e-05
masked_value = -1e+30

def layer_norm(values, gain, shift):
    average = lax.optimization_barrier(jnp.mean(values, axis=-1, keepdims=True))
    centered = values - average
    variance = lax.optimization_barrier(jnp.mean(centered * centered, axis=-1, keepdims=True))
    return centered * lax.rsqrt(variance + epsilon) * gain + shift

def product(left, right):
    return jnp.dot(left, right, precision=lax.Precision.HIGHEST)

def rotary_tables(places):
    half_rot = ROT // 2
    frequencies = 10000.0 ** (-(jnp.arange(half_rot, dtype=jnp.int32).astype(jnp.float32) * 2.0 / ROT))
    angles = places[:, None] * frequencies[None, :]
    return (jnp.cos(angles)[:, None, :], jnp.sin(angles)[:, None, :])

def rotate(values, cosines, sines):
    half_rot = ROT // 2
    first_half = values[..., :half_rot]
    second_half = values[..., half_rot:ROT]
    return jnp.concatenate([first_half * cosines - second_half * sines, second_half * cosines + first_half * sines, values[..., ROT:]], axis=-1)

def gelu_exact(values):
    return jax.nn.gelu(values, approximate=False)

def attend_block(query_block, offset, keys_all, values_all, seg_all):
    block_rows = query_block.shape[0]
    query_pos = offset + jnp.arange(block_rows, dtype=jnp.int32)
    key_pos = jnp.arange(keys_all.shape[0], dtype=jnp.int32)
    query_seg = lax.dynamic_slice_in_dim(seg_all, offset, block_rows)
    allowed = (key_pos[None, :] <= query_pos[:, None]) & (query_seg[:, None] == seg_all[None, :])
    logits = jnp.einsum('qhd,khd->qhk', query_block, keys_all, precision=lax.Precision.HIGHEST)
    logits = low_back(logits)
    logits = jnp.where(allowed[:, None, :], logits, masked_value)
    highest = lax.optimization_barrier(jnp.max(logits, axis=-1, keepdims=True))
    weights = jnp.exp(logits - highest)
    chances = low(weights / lax.optimization_barrier(jnp.sum(weights, axis=-1, keepdims=True)))
    return jnp.einsum('qhk,khd->qhd', chances, values_all, precision=lax.Precision.HIGHEST)

def reference(tokens, segments, ln1_gain, ln1_bias, qkv_weight, qkv_bias, out_weight, out_bias, ln2_gain, ln2_bias, fc1_weight, fc1_bias, fc2_weight, fc2_bias, cotangent):
    block_rows = min(512, LEN)
    block_count = LEN // block_rows
    cosines, sines = rotary_tables(jnp.arange(LEN, dtype=jnp.int32).astype(jnp.float32))
    checked_block = jax.checkpoint(attend_block)

    def one_sequence(items):
        query_seq, key_seq, value_seq, seg_seq = items
        blocks = query_seq.reshape(block_count, block_rows, HEADS, HD)
        offsets = jnp.arange(block_count, dtype=jnp.int32) * block_rows

        def one_block(block_items):
            return checked_block(block_items[0], block_items[1], key_seq, value_seq, seg_seq)
        return lax.map(one_block, (blocks, offsets)).reshape(LEN, HEADS, HD)

    def forward(inputs, gain_one, bias_one, weight_qkv, bias_qkv, weight_out, bias_out, gain_two, bias_two, weight_up, bias_up, weight_down, bias_down):
        flat_rows = inputs.reshape(SEQS * LEN, D)
        act_one = low(layer_norm(flat_rows, gain_one, bias_one))
        mixed_qkv = low_back(product(act_one, weight_qkv) + bias_qkv).reshape(SEQS, LEN, 3, HEADS, HD)
        query_low = low(rotate(mixed_qkv[:, :, 0], cosines, sines) * 0.0625)
        key_low = low(rotate(mixed_qkv[:, :, 1], cosines, sines))
        value_low = low(mixed_qkv[:, :, 2])
        attended = lax.map(one_sequence, (query_low, key_low, value_low, segments))
        attended = low_back(low(attended)).reshape(SEQS * LEN, D)
        attn_out = product(attended, weight_out) + bias_out
        act_two = low(layer_norm(flat_rows, gain_two, bias_two))
        hidden = low_back(product(act_two, weight_up) + bias_up)
        activated = low(gelu_exact(hidden))
        mlp_out = product(activated, weight_down) + bias_down
        return (flat_rows + attn_out + mlp_out).reshape(SEQS, LEN, D)
    arguments = tuple((tensor.astype(jnp.float32) for tensor in (tokens, ln1_gain, ln1_bias, qkv_weight, qkv_bias, out_weight, out_bias, ln2_gain, ln2_bias, fc1_weight, fc1_bias, fc2_weight, fc2_bias)))
    mixed, pull_back = jax.vjp(forward, *arguments)
    gradients = pull_back(cotangent.astype(jnp.float32))
    return (mixed.astype(jnp.bfloat16), gradients[0].astype(jnp.bfloat16), gradients[1], gradients[2], gradients[3], gradients[4], gradients[5], gradients[6], gradients[7], gradients[8], gradients[9], gradients[10], gradients[11], gradients[12])
```

```python
import math

import jax
import jax.numpy as jnp
from jax import lax
from jax.sharding import Mesh, PartitionSpec as P

HEADS = 8
HD = 256
ROT = 64
CORES = 2


epsilon = 1e-05
masked_value = -1e30


def layer_norm(values, gain, shift):
    average = jnp.mean(values, axis=-1, keepdims=True)
    centered = values - average
    variance = jnp.mean(centered * centered, axis=-1, keepdims=True)
    return centered * lax.rsqrt(variance + epsilon) * gain + shift


def rotary_tables(places):
    half_rot = ROT // 2
    frequencies = 10000.0 ** (
        -(jnp.arange(half_rot, dtype=jnp.int32).astype(jnp.float32) * 2.0 / ROT)
    )
    angles = places[:, None] * frequencies[None, :]
    return (jnp.cos(angles)[:, None, :], jnp.sin(angles)[:, None, :])


def rotate(values, cosines, sines):
    half_rot = ROT // 2
    first_half = values[..., :half_rot]
    second_half = values[..., half_rot:ROT]
    return jnp.concatenate(
        [
            first_half * cosines - second_half * sines,
            second_half * cosines + first_half * sines,
            values[..., ROT:],
        ],
        axis=-1,
    )


def gelu_exact(values):
    return jax.nn.gelu(values, approximate=False)


def visible(query_seg, query_pos, key_seg, key_pos):
    causal = key_pos[None, :] <= query_pos[:, None]
    same_doc = query_seg[:, :, None] == key_seg[:, None, :]
    return (causal[None] & same_doc)[:, :, None, :]


def per_device(
    tokens,
    segments,
    ln1_gain,
    ln1_bias,
    qkv_weight,
    qkv_bias,
    out_weight,
    out_bias,
    ln2_gain,
    ln2_bias,
    fc1_weight,
    fc1_bias,
    fc2_weight,
    fc2_bias,
    cotangent,
):
    group_size, block_size, model_width = tokens.shape
    row_count = group_size * block_size
    attention_full = (
        lax.all_gather(ln1_gain, ("dp", "seq"), axis=0, tiled=True),
        lax.all_gather(ln1_bias, ("dp", "seq"), axis=0, tiled=True),
        lax.all_gather(qkv_weight, ("dp", "seq"), axis=0, tiled=True),
        lax.all_gather(qkv_bias, ("dp", "seq"), axis=0, tiled=True),
        lax.all_gather(out_weight, ("dp", "seq"), axis=0, tiled=True),
        lax.all_gather(out_bias, ("dp", "seq"), axis=0, tiled=True),
    )
    gain_one, bias_one, weight_qkv, bias_qkv, weight_out, bias_out = attention_full
    flat_in = tokens.reshape(row_count, model_width).astype(jnp.float32)
    normed_one, norm_back_one = jax.vjp(
        layer_norm, flat_in, gain_one.astype(jnp.float32), bias_one.astype(jnp.float32)
    )
    act_one = normed_one.astype(jnp.bfloat16)
    mixed_qkv = jnp.dot(act_one, weight_qkv, preferred_element_type=jnp.float32) + bias_qkv.astype(
        jnp.float32
    )
    mixed_qkv = mixed_qkv.reshape(group_size, block_size, 3, HEADS, HD)
    first_pos = lax.axis_index("seq") * block_size
    local_pos = first_pos + jnp.arange(block_size, dtype=jnp.int32)
    cosines, sines = rotary_tables(local_pos.astype(jnp.float32))

    def turn_all(query_raw, key_raw):
        return (rotate(query_raw, cosines, sines) * 0.0625, rotate(key_raw, cosines, sines))

    (query_turned, key_turned), turn_back = jax.vjp(
        turn_all, mixed_qkv[:, :, 0], mixed_qkv[:, :, 1]
    )
    query_low = query_turned.astype(jnp.bfloat16)
    key_low = key_turned.astype(jnp.bfloat16)
    value_low = mixed_qkv[:, :, 2].astype(jnp.bfloat16)
    start_top = jnp.full((group_size, block_size, HEADS), masked_value, jnp.float32)
    key_piece = lax.all_gather(key_low, "seq", axis=1, tiled=True)
    value_piece = lax.all_gather(value_low, "seq", axis=1, tiled=True)
    seg_piece = lax.all_gather(segments, "seq", axis=1, tiled=True)
    key_pos = jnp.arange(seg_piece.shape[1], dtype=jnp.int32)
    allowed = visible(segments, local_pos, seg_piece, key_pos)
    scores = jnp.einsum("gqhd,gkhd->gqhk", query_low, key_piece, preferred_element_type=jnp.float32)
    scores = jnp.where(allowed, scores, masked_value)
    new_top = jnp.maximum(start_top, jnp.max(scores, axis=-1))
    weights = jnp.where(allowed, jnp.exp(scores - new_top[..., None]), 0.0)
    new_total = jnp.sum(weights, axis=-1)
    new_out = jnp.einsum(
        "gqhk,gkhd->gqhd",
        weights.astype(jnp.bfloat16),
        value_piece,
        preferred_element_type=jnp.float32,
    )
    attended = new_out / new_total[..., None]
    log_total = new_top + jnp.log(new_total)
    attended_low = attended.astype(jnp.bfloat16).reshape(row_count, model_width)
    attn_out = jnp.dot(
        attended_low, weight_out, preferred_element_type=jnp.float32
    ) + bias_out.astype(jnp.float32)
    mlp_full = (
        lax.all_gather(ln2_gain, ("dp", "seq"), axis=0, tiled=True),
        lax.all_gather(ln2_bias, ("dp", "seq"), axis=0, tiled=True),
        lax.all_gather(fc1_weight, ("dp", "seq"), axis=0, tiled=True),
        lax.all_gather(fc1_bias, ("dp", "seq"), axis=0, tiled=True),
        lax.all_gather(fc2_weight, ("dp", "seq"), axis=0, tiled=True),
        lax.all_gather(fc2_bias, ("dp", "seq"), axis=0, tiled=True),
    )
    gain_two, bias_two, weight_up, bias_up, weight_down, bias_down = mlp_full
    normed_two, norm_back_two = jax.vjp(
        layer_norm, flat_in, gain_two.astype(jnp.float32), bias_two.astype(jnp.float32)
    )
    act_two = normed_two.astype(jnp.bfloat16)
    hidden = jnp.dot(act_two, weight_up, preferred_element_type=jnp.float32) + bias_up.astype(
        jnp.float32
    )
    activated, gelu_back = jax.vjp(gelu_exact, hidden)
    act_hidden = activated.astype(jnp.bfloat16)
    mlp_out = jnp.dot(
        act_hidden, weight_down, preferred_element_type=jnp.float32
    ) + bias_down.astype(jnp.float32)
    mixed = (
        (flat_in + attn_out + mlp_out)
        .astype(jnp.bfloat16)
        .reshape(group_size, block_size, model_width)
    )
    back_up, back_down = (
        lax.all_gather(fc1_weight, ("dp", "seq"), axis=0, tiled=True),
        lax.all_gather(fc2_weight, ("dp", "seq"), axis=0, tiled=True),
    )
    back_qkv, back_out = (
        lax.all_gather(qkv_weight, ("dp", "seq"), axis=0, tiled=True),
        lax.all_gather(out_weight, ("dp", "seq"), axis=0, tiled=True),
    )
    grad_out = cotangent.reshape(row_count, model_width)
    grad_float = grad_out.astype(jnp.float32)
    grad_down_weight = jnp.dot(act_hidden.T, grad_out, preferred_element_type=jnp.float32)
    grad_down_bias = jnp.sum(grad_float, axis=0)
    grad_activated = jnp.dot(grad_out, back_down.T, preferred_element_type=jnp.float32)
    (grad_hidden,) = gelu_back(grad_activated)
    grad_hidden_low = grad_hidden.astype(jnp.bfloat16)
    grad_up_weight = jnp.dot(act_two.T, grad_hidden_low, preferred_element_type=jnp.float32)
    grad_up_bias = jnp.sum(grad_hidden_low.astype(jnp.float32), axis=0)
    grad_act_two = jnp.dot(grad_hidden_low, back_up.T, preferred_element_type=jnp.float32)
    grad_in_two, grad_gain_two, grad_bias_two = norm_back_two(grad_act_two)
    mlp_shards = (
        lax.psum_scatter(grad_gain_two, ("dp", "seq"), scatter_dimension=0, tiled=True),
        lax.psum_scatter(grad_bias_two, ("dp", "seq"), scatter_dimension=0, tiled=True),
        lax.psum_scatter(grad_up_weight, ("dp", "seq"), scatter_dimension=0, tiled=True),
        lax.psum_scatter(grad_up_bias, ("dp", "seq"), scatter_dimension=0, tiled=True),
        lax.psum_scatter(grad_down_weight, ("dp", "seq"), scatter_dimension=0, tiled=True),
        lax.psum_scatter(grad_down_bias, ("dp", "seq"), scatter_dimension=0, tiled=True),
    )
    grad_out_weight = jnp.dot(attended_low.T, grad_out, preferred_element_type=jnp.float32)
    grad_out_bias = jnp.sum(grad_float, axis=0)
    grad_attended = jnp.dot(grad_out, back_out.T, preferred_element_type=jnp.float32)
    grad_low = grad_attended.reshape(group_size, block_size, HEADS, HD).astype(jnp.bfloat16)
    delta = jnp.sum(grad_low.astype(jnp.float32) * attended, axis=-1)
    key_piece = lax.all_gather(key_low, "seq", axis=1, tiled=True)
    value_piece = lax.all_gather(value_low, "seq", axis=1, tiled=True)
    seg_piece = lax.all_gather(segments, "seq", axis=1, tiled=True)
    key_pos = jnp.arange(seg_piece.shape[1], dtype=jnp.int32)
    allowed = visible(segments, local_pos, seg_piece, key_pos)
    scores = jnp.einsum("gqhd,gkhd->gqhk", query_low, key_piece, preferred_element_type=jnp.float32)
    chances = jnp.where(allowed, jnp.exp(scores - log_total[..., None]), 0.0)
    grad_chances = jnp.einsum(
        "gqhd,gkhd->gqhk", grad_low, value_piece, preferred_element_type=jnp.float32
    )
    grad_scores = (chances * (grad_chances - delta[..., None])).astype(jnp.bfloat16)
    grad_query = jnp.einsum(
        "gqhk,gkhd->gqhd", grad_scores, key_piece, preferred_element_type=jnp.float32
    )
    query_piece = lax.all_gather(query_low, "seq", axis=1, tiled=True)
    grad_piece = lax.all_gather(grad_low, "seq", axis=1, tiled=True)
    lse_piece = lax.all_gather(log_total.astype(jnp.bfloat16), "seq", axis=1, tiled=True).astype(
        jnp.float32
    )
    delta_piece = lax.all_gather(delta.astype(jnp.bfloat16), "seq", axis=1, tiled=True).astype(
        jnp.float32
    )
    seg_piece = lax.all_gather(segments, "seq", axis=1, tiled=True)
    query_pos = jnp.arange(seg_piece.shape[1], dtype=jnp.int32)
    allowed = visible(seg_piece, query_pos, segments, local_pos)
    scores = jnp.einsum("gqhd,gkhd->gqhk", query_piece, key_low, preferred_element_type=jnp.float32)
    chances = jnp.where(allowed, jnp.exp(scores - lse_piece[..., None]), 0.0)
    new_value = jnp.einsum(
        "gqhk,gqhd->gkhd",
        chances.astype(jnp.bfloat16),
        grad_piece,
        preferred_element_type=jnp.float32,
    )
    grad_chances = jnp.einsum(
        "gqhd,gkhd->gqhk", grad_piece, value_low, preferred_element_type=jnp.float32
    )
    grad_scores = (chances * (grad_chances - delta_piece[..., None])).astype(jnp.bfloat16)
    new_key = jnp.einsum(
        "gqhk,gqhd->gkhd", grad_scores, query_piece, preferred_element_type=jnp.float32
    )
    grad_query_raw, grad_key_raw = turn_back((grad_query, new_key))
    grad_qkv_low = (
        jnp.stack([grad_query_raw, grad_key_raw, new_value], axis=2)
        .reshape(row_count, 3 * model_width)
        .astype(jnp.bfloat16)
    )
    grad_qkv_weight = jnp.dot(act_one.T, grad_qkv_low, preferred_element_type=jnp.float32)
    grad_qkv_bias = jnp.sum(grad_qkv_low.astype(jnp.float32), axis=0)
    grad_act_one = jnp.dot(grad_qkv_low, back_qkv.T, preferred_element_type=jnp.float32)
    grad_in_one, grad_gain_one, grad_bias_one = norm_back_one(grad_act_one)
    attention_shards = (
        lax.psum_scatter(grad_gain_one, ("dp", "seq"), scatter_dimension=0, tiled=True),
        lax.psum_scatter(grad_bias_one, ("dp", "seq"), scatter_dimension=0, tiled=True),
        lax.psum_scatter(grad_qkv_weight, ("dp", "seq"), scatter_dimension=0, tiled=True),
        lax.psum_scatter(grad_qkv_bias, ("dp", "seq"), scatter_dimension=0, tiled=True),
        lax.psum_scatter(grad_out_weight, ("dp", "seq"), scatter_dimension=0, tiled=True),
        lax.psum_scatter(grad_out_bias, ("dp", "seq"), scatter_dimension=0, tiled=True),
    )
    grad_tokens = (
        (grad_float + grad_in_one + grad_in_two)
        .astype(jnp.bfloat16)
        .reshape(group_size, block_size, model_width)
    )
    return (
        mixed,
        grad_tokens,
        attention_shards[0],
        attention_shards[1],
        attention_shards[2],
        attention_shards[3],
        attention_shards[4],
        attention_shards[5],
        mlp_shards[0],
        mlp_shards[1],
        mlp_shards[2],
        mlp_shards[3],
        mlp_shards[4],
        mlp_shards[5],
    )


GROUP = ("z", "y")
PEERS = ("x", "c")
EVERY = ("z", "y", "x", "c")


def ring_places(depth, width):
    return [2 * z for z in range(depth)] + [2 * z + 1 for z in reversed(range(depth))]


def ring_perm(places, shift):
    count = len(places)
    return [(places[i], places[(i + shift) % count]) for i in range(count)]


def ring_gather(block, places):
    count = len(places)
    held = [None] * count
    held[0] = block
    ahead = behind = block
    for step in range(1, count // 2 + 1):
        behind = lax.ppermute(behind, GROUP, ring_perm(places, 1))
        held[count - step] = behind
        if step < count - step:
            ahead = lax.ppermute(ahead, GROUP, ring_perm(places, -1))
            held[step] = ahead
    return held


def ring_scatter(parts, places):
    count = len(places)
    half = count // 2
    forward = backward = None
    for step in range(half):
        ahead = parts[half - step]
        if forward is not None:
            ahead = ahead.astype(jnp.float32) + forward.astype(jnp.float32)
        forward = lax.ppermute(ahead.astype(jnp.bfloat16), GROUP, ring_perm(places, 1))
        if step > 0:
            behind = parts[half + step]
            if backward is not None:
                behind = behind.astype(jnp.float32) + backward.astype(jnp.float32)
            backward = lax.ppermute(behind.astype(jnp.bfloat16), GROUP, ring_perm(places, -1))
    return parts[0] + forward.astype(jnp.float32) + backward.astype(jnp.float32)


def swap(values, axis):
    return lax.ppermute(values, axis, [(0, 1), (1, 0)])


def both(values, axis, at):
    other = swap(values, axis)
    first = lax.axis_index(axis) == 0
    low = jnp.where(first, values, other)
    high = jnp.where(first, other, values)
    return jnp.stack([low, high], axis=at)


def halves(values, axis, at):
    mine = lax.axis_index(axis)
    return (
        lax.dynamic_index_in_dim(values, mine, at, keepdims=False),
        lax.dynamic_index_in_dim(values, 1 - mine, at, keepdims=False),
    )


def fold(values, axis, at):
    mine, other = halves(values, axis, at)
    return mine + swap(other.astype(jnp.bfloat16), axis).astype(jnp.float32)


def unrotate(values, cosines, sines):
    half_rot = ROT // 2
    first_half = values[..., :half_rot]
    second_half = values[..., half_rot:ROT]
    return jnp.concatenate(
        [
            first_half * cosines + second_half * sines,
            second_half * cosines - first_half * sines,
            values[..., ROT:],
        ],
        axis=-1,
    )


def rotate(values, cosines, sines):
    return unrotate(values, cosines, -sines)


def angles(places):
    half_rot = ROT // 2
    frequencies = 10000.0 ** (
        -(jnp.arange(half_rot, dtype=jnp.int32).astype(jnp.float32) * 2.0 / ROT)
    )
    turned = places.astype(jnp.float32)[..., None] * frequencies
    return jnp.cos(turned), jnp.sin(turned)


def dot_f32(left, right, dims=((1,), (0,))):
    return lax.dot_general(left, right, (dims, ((), ())), preferred_element_type=jnp.float32)


def grouped(
    tokens,
    segments,
    ln1_gain,
    ln1_bias,
    qkv_weight,
    qkv_bias,
    out_weight,
    out_bias,
    ln2_gain,
    ln2_bias,
    fc1_weight,
    fc1_bias,
    fc2_weight,
    fc2_bias,
    cotangent,
):
    f32, bf16 = jnp.float32, jnp.bfloat16
    depth, width = lax.axis_size("z"), lax.axis_size("y")
    share = depth * width
    devices = share * 2 * CORES
    z, y, x, c = (lax.axis_index(name) for name in EVERY)
    t = z * width + y
    places = ring_places(depth, width)
    r = jnp.where(y == 0, z, 2 * depth - 1 - z)
    seqs, rows, model = tokens.shape
    block = seqs * rows
    own = block * share
    slim = ln1_gain.shape[0]
    hidden = fc2_weight.shape[0] * 2 * CORES

    pieces = (
        ln1_gain,
        ln1_bias,
        ln2_gain,
        ln2_bias,
        out_bias,
        fc2_bias,
        qkv_bias,
        fc1_bias,
        segments.reshape(-1).astype(bf16),
    )
    ends = [0]
    for piece in pieces:
        ends.append(ends[-1] + piece.shape[0])
    packed = jnp.concatenate(pieces)
    packed = jnp.pad(packed, (0, -ends[-1] % 128))
    packed = lax.all_to_all(
        jnp.broadcast_to(packed, (devices, packed.shape[0])), EVERY, 0, 0, tiled=True
    )
    small = [
        packed[:, ends[i] : ends[i + 1]].astype(f32).reshape(-1) for i in range(len(pieces) - 1)
    ]
    gain_one, shift_one, gain_two, shift_two, bias_out, bias_down, bias_qkv, bias_up = small
    bias_up = lax.dynamic_slice_in_dim(bias_up, t * hidden, hidden)
    bias_qkv = lax.dynamic_index_in_dim(
        bias_qkv.reshape(3, HEADS, HD), t, 1, keepdims=False
    ).reshape(3 * HD)
    all_seg = packed[:, ends[-2] : ends[-1]].reshape(depth, width, 2, CORES, seqs, rows)

    up_cols = fc1_weight.reshape(slim, share, hidden)
    qkv_cols = (
        qkv_weight.reshape(slim, 3, share, HD).transpose(0, 2, 1, 3).reshape(slim, share, 3 * HD)
    )
    spread = jnp.concatenate([qkv_cols, up_cols], axis=2).transpose(1, 0, 2)
    spread = lax.all_to_all(spread, GROUP, 0, 0, tiled=True)
    down_out = jnp.concatenate([out_weight, fc2_weight], axis=0)
    down_out = both(both(down_out, "x", 0), "c", 1)
    weight_out = down_out[:, :, :slim].reshape(HD, model)
    weight_down = down_out[:, :, slim:].reshape(hidden, model)
    spread = both(both(spread, "x", 1), "c", 2).reshape(model, 3 * HD + hidden)
    weight_qkv = spread[:, : 3 * HD]
    weight_up = spread[:, 3 * HD :]

    my_rows = tokens.reshape(block, model)
    my_grad = cotangent.reshape(block, model)
    all_in = jnp.concatenate(ring_gather(my_rows, places), axis=0)
    all_grad = jnp.concatenate(ring_gather(my_grad, places), axis=0)

    wide_in = all_in.astype(f32)
    average = jnp.mean(wide_in, axis=-1, keepdims=True)
    centered = wide_in - average
    scale = lax.rsqrt(jnp.mean(centered * centered, axis=-1, keepdims=True) + epsilon)
    normal = centered * scale
    act_one = (normal * gain_one + shift_one).astype(bf16)
    act_two = (normal * gain_two + shift_two).astype(bf16)

    steps = (r + jnp.arange(share, dtype=jnp.int32)) % share
    step_y = (steps >= depth).astype(jnp.int32)
    within = jnp.tile(jnp.arange(rows, dtype=jnp.int32), seqs)
    token_pos = (((step_y * 2 + x) * CORES + c) * rows)[:, None] + within[None, :]
    cosines, sines = angles(token_pos.reshape(own))
    qkv = dot_f32(act_one, weight_qkv) + bias_qkv
    query = (rotate(qkv[:, :HD], cosines, sines) * 0.0625).astype(bf16)
    key = rotate(qkv[:, HD : 2 * HD], cosines, sines).astype(bf16)
    value = qkv[:, 2 * HD :].astype(bf16)
    grad_low = dot_f32(all_grad, weight_out, ((1,), (1,))).astype(bf16)
    sent = jnp.concatenate([query, key, value, grad_low], axis=1).reshape(share, block, 4 * HD)

    def peer(dx, dc):
        return x ^ dx, c ^ dc

    turns = [(0, 0), (0, 1), (1, 0), (1, 1)]

    def xor_perm(dx, dc):
        flip = dx * CORES + dc
        return [(i, i ^ flip) for i in range(2 * CORES)]

    def taken(buffer, px, pc):
        pz = px * CORES + pc
        return jnp.stack(
            [
                lax.dynamic_index_in_dim(buffer, (pz - r) % share, 0, keepdims=False),
                lax.dynamic_index_in_dim(buffer, (2 * depth - 1 - pz - r) % share, 0, keepdims=False),
            ]
        )

    got = []
    for dx, dc in turns:
        message = taken(sent, *peer(dx, dc))
        if (dx, dc) != (0, 0):
            message = lax.ppermute(message, PEERS, xor_perm(dx, dc))
        got.append(message)
    length = rows * width * 2 * CORES
    whole = (
        jnp.stack(got)
        .reshape(4, width, seqs, rows, 4 * HD)
        .transpose(2, 0, 1, 3, 4)
        .reshape(seqs, length, 4 * HD)
    )
    my_z = x * CORES + c
    seg_z = lax.dynamic_index_in_dim(all_seg, my_z, 0, keepdims=False)
    order = [(peer(dx, dc), py) for dx, dc in turns for py in range(width)]
    seq_pos = jnp.concatenate(
        [((py * 2 + px) * CORES + pc) * rows + jnp.arange(rows, dtype=jnp.int32) for (px, pc), py in order]
    )
    seq_seg = jnp.concatenate(
        [
            lax.dynamic_index_in_dim(
                lax.dynamic_index_in_dim(seg_z[py], px, 0, keepdims=False), pc, 0, keepdims=False
            )
            for (px, pc), py in order
        ],
        axis=1,
    )

    query, key, value, grad_low = (whole[:, :, i * HD : (i + 1) * HD] for i in range(4))
    allowed = (seq_pos[None, None, :] <= seq_pos[None, :, None]) & (
        seq_seg[:, :, None] == seq_seg[:, None, :]
    )
    scores = jnp.einsum("gqd,gkd->gqk", query, key, preferred_element_type=f32)
    scores = jnp.where(allowed, scores, masked_value)
    weights = jnp.exp(scores - jnp.max(scores, axis=-1, keepdims=True))
    chances = weights / jnp.sum(weights, axis=-1, keepdims=True)
    chances_low = chances.astype(bf16)
    attended = jnp.einsum("gqk,gkd->gqd", chances_low, value, preferred_element_type=f32)
    delta = jnp.sum(grad_low.astype(f32) * attended, axis=-1, keepdims=True)
    grad_chances = jnp.einsum("gqd,gkd->gqk", grad_low, value, preferred_element_type=f32)
    grad_scores = (chances * (grad_chances - delta)).astype(bf16)
    grad_query = jnp.einsum("gqk,gkd->gqd", grad_scores, key, preferred_element_type=f32)
    grad_key = jnp.einsum("gqk,gqd->gkd", grad_scores, query, preferred_element_type=f32)
    grad_value = jnp.einsum("gqk,gqd->gkd", chances_low, grad_low, preferred_element_type=f32)
    seq_cos, seq_sin = angles(seq_pos)
    back = jnp.concatenate(
        [
            attended.astype(bf16),
            unrotate(grad_query * 0.0625, seq_cos, seq_sin).astype(bf16),
            unrotate(grad_key, seq_cos, seq_sin).astype(bf16),
            grad_value.astype(bf16),
        ],
        axis=2,
    )
    back = (
        back.reshape(seqs, 4, width, rows, 4 * HD)
        .transpose(1, 2, 0, 3, 4)
        .reshape(4, width, block, 4 * HD)
    )
    returned = []
    for i, (dx, dc) in enumerate(turns):
        message = back[i]
        if (dx, dc) != (0, 0):
            message = lax.ppermute(message, PEERS, xor_perm(dx, dc))
        returned.append(message)
    returned = jnp.stack(returned).reshape(4 * width, block, 4 * HD)
    placed = []
    for j in range(share):
        step = (r + j) % share
        far = (step >= depth).astype(jnp.int32)
        step_z = jnp.where(far == 1, 2 * depth - 1 - step, step)
        turn = step_z ^ my_z
        placed.append(lax.dynamic_index_in_dim(returned, turn * width + far, 0, keepdims=False))
    placed = jnp.concatenate(placed, axis=0)
    attended_low = placed[:, :HD]
    grad_qkv = placed[:, HD:]

    hidden_in = dot_f32(act_two, weight_up) + bias_up
    cdf = 0.5 * (1.0 + lax.erf(hidden_in * math.sqrt(0.5)))
    act_hidden = (hidden_in * cdf).astype(bf16)
    slope = cdf + hidden_in * jnp.exp(-0.5 * hidden_in * hidden_in) * (1.0 / math.sqrt(2.0 * math.pi))
    grad_hidden = (dot_f32(all_grad, weight_down, ((1,), (1,))) * slope).astype(bf16)

    out_parts = [
        dot_f32(attended_low[j * block : (j + 1) * block], weight_out)
        + dot_f32(act_hidden[j * block : (j + 1) * block], weight_down)
        for j in range(share)
    ]
    mixed = ring_scatter(out_parts, places) + my_rows.astype(f32) + bias_out + bias_down

    grad_one = dot_f32(grad_qkv, weight_qkv, ((1,), (1,)))
    grad_two = dot_f32(grad_hidden, weight_up, ((1,), (1,)))
    vectors = [
        jnp.sum(grad_one * normal, axis=0),
        jnp.sum(grad_one, axis=0),
        jnp.sum(grad_two * normal, axis=0),
        jnp.sum(grad_two, axis=0),
    ]
    pulled = grad_one * gain_one + grad_two * gain_two
    pulled = ring_scatter([pulled[j * block : (j + 1) * block] for j in range(share)], places)
    my_normal = normal[:block]
    grad_in = my_grad.astype(f32) + scale[:block] * (
        pulled
        - jnp.mean(pulled, axis=-1, keepdims=True)
        - my_normal * jnp.mean(pulled * my_normal, axis=-1, keepdims=True)
    )

    grad_down = dot_f32(
        jnp.concatenate([attended_low, act_hidden], axis=1), all_grad, ((0,), (0,))
    )
    grad_out_w = fold(fold(grad_down[:HD].reshape(2, CORES, slim, model), "c", 1), "x", 0)
    grad_down_w = fold(
        fold(grad_down[HD:].reshape(2, CORES, hidden // (2 * CORES), model), "c", 1), "x", 0
    )
    grad_up = dot_f32(act_two, grad_hidden, ((0,), (0,))).reshape(share, 2, CORES, slim, hidden)
    grad_qkv_w = dot_f32(act_one, grad_qkv, ((0,), (0,))).reshape(share, 2, CORES, slim, 3 * HD)

    def to_owners(grad):
        grad = fold(fold(grad, "c", 2), "x", 1).astype(bf16)
        return lax.all_to_all(grad, GROUP, 0, 0, tiled=True)

    grad_up = to_owners(grad_up).transpose(1, 0, 2).reshape(slim, share * hidden).astype(f32)
    grad_qkv_w = (
        to_owners(grad_qkv_w)
        .reshape(share, slim, 3, HD)
        .transpose(1, 2, 0, 3)
        .reshape(slim, 3 * share * HD)
        .astype(f32)
    )

    up_sum = jnp.sum(grad_hidden.astype(f32), axis=0).reshape(2 * CORES, -1)
    up_rows = lax.dynamic_update_slice_in_dim(
        jnp.zeros((devices, up_sum.shape[1]), f32), up_sum, t * 2 * CORES, 0
    )
    qkv_sum = jnp.sum(grad_qkv.astype(f32), axis=0).reshape(3, 1, HD)
    qkv_rows = lax.dynamic_update_slice(
        jnp.zeros((3, HEADS, HD), f32), qkv_sum, (0, t, 0)
    ).reshape(devices, -1)
    vectors.append(jnp.sum(my_grad.astype(f32), axis=0))
    table = jnp.concatenate([v.reshape(devices, slim) for v in vectors] + [up_rows, qkv_rows], axis=1)
    table = jnp.sum(lax.all_to_all(table, EVERY, 0, 0, tiled=True), axis=0)
    sums = [table[i * slim : (i + 1) * slim] for i in range(5)]
    up_end = 5 * slim + up_rows.shape[1]
    grad_up_bias = table[5 * slim : up_end]
    grad_qkv_bias = table[up_end:]
    return (
        mixed.astype(bf16).reshape(tokens.shape),
        grad_in.astype(bf16).reshape(tokens.shape),
        sums[0],
        sums[1],
        grad_qkv_w,
        grad_qkv_bias,
        grad_out_w,
        sums[4],
        sums[2],
        sums[3],
        grad_up,
        grad_up_bias,
        grad_down_w,
        sums[4],
    )


def specs(batch, block):
    every = batch + block
    one, two, three = P(every), P(every, None), P(batch, block, None)
    arguments = (three, P(batch, block), one, one, two, one, two, one, one, one, two, one, two, one, three)
    results = (three, three, one, one, two, one, two, one, one, one, two, one, two, one)
    return arguments, results


def solution(mesh):
    depth, ring = mesh.shape["dp"], mesh.shape["seq"]
    width = ring // (2 * CORES)
    if width == 2 and depth == 2 * CORES and depth * width == HEADS:
        chips = Mesh(mesh.devices.reshape(depth, width, 2, CORES), EVERY)
        arguments, results = specs(("z",), ("y", "x", "c"))
        return jax.shard_map(
            grouped, mesh=chips, in_specs=arguments, out_specs=results, check_vma=False
        )
    arguments, results = specs(("dp",), ("seq",))
    return jax.shard_map(
        per_device, mesh=mesh, in_specs=arguments, out_specs=results, check_vma=False
    )
```

```python
import functools
import math

import jax
import jax.numpy as jnp
from jax import lax
from jax.experimental import pallas as pl
from jax.experimental.pallas import tpu as pltpu
from jax.sharding import Mesh, PartitionSpec as P

HEADS = 8
HD = 256
ROT = 64
CORES = 2


epsilon = 1e-05
masked_value = -1e30


def layer_norm(values, gain, shift):
    average = jnp.mean(values, axis=-1, keepdims=True)
    centered = values - average
    variance = jnp.mean(centered * centered, axis=-1, keepdims=True)
    return centered * lax.rsqrt(variance + epsilon) * gain + shift


def base_tables(places):
    half_rot = ROT // 2
    frequencies = 10000.0 ** (
        -(jnp.arange(half_rot, dtype=jnp.int32).astype(jnp.float32) * 2.0 / ROT)
    )
    angles = places[:, None] * frequencies[None, :]
    return (jnp.cos(angles)[:, None, :], jnp.sin(angles)[:, None, :])


def base_rotate(values, cosines, sines):
    half_rot = ROT // 2
    first_half = values[..., :half_rot]
    second_half = values[..., half_rot:ROT]
    return jnp.concatenate(
        [
            first_half * cosines - second_half * sines,
            second_half * cosines + first_half * sines,
            values[..., ROT:],
        ],
        axis=-1,
    )


def gelu_exact(values):
    return jax.nn.gelu(values, approximate=False)


def visible(query_seg, query_pos, key_seg, key_pos):
    causal = key_pos[None, :] <= query_pos[:, None]
    same_doc = query_seg[:, :, None] == key_seg[:, None, :]
    return (causal[None] & same_doc)[:, :, None, :]


def per_device(
    tokens,
    segments,
    ln1_gain,
    ln1_bias,
    qkv_weight,
    qkv_bias,
    out_weight,
    out_bias,
    ln2_gain,
    ln2_bias,
    fc1_weight,
    fc1_bias,
    fc2_weight,
    fc2_bias,
    cotangent,
):
    group_size, block_size, model_width = tokens.shape
    row_count = group_size * block_size
    attention_full = (
        lax.all_gather(ln1_gain, ("dp", "seq"), axis=0, tiled=True),
        lax.all_gather(ln1_bias, ("dp", "seq"), axis=0, tiled=True),
        lax.all_gather(qkv_weight, ("dp", "seq"), axis=0, tiled=True),
        lax.all_gather(qkv_bias, ("dp", "seq"), axis=0, tiled=True),
        lax.all_gather(out_weight, ("dp", "seq"), axis=0, tiled=True),
        lax.all_gather(out_bias, ("dp", "seq"), axis=0, tiled=True),
    )
    gain_one, bias_one, weight_qkv, bias_qkv, weight_out, bias_out = attention_full
    flat_in = tokens.reshape(row_count, model_width).astype(jnp.float32)
    normed_one, norm_back_one = jax.vjp(
        layer_norm, flat_in, gain_one.astype(jnp.float32), bias_one.astype(jnp.float32)
    )
    act_one = normed_one.astype(jnp.bfloat16)
    mixed_qkv = jnp.dot(act_one, weight_qkv, preferred_element_type=jnp.float32) + bias_qkv.astype(
        jnp.float32
    )
    mixed_qkv = mixed_qkv.reshape(group_size, block_size, 3, HEADS, HD)
    first_pos = lax.axis_index("seq") * block_size
    local_pos = first_pos + jnp.arange(block_size, dtype=jnp.int32)
    cosines, sines = base_tables(local_pos.astype(jnp.float32))

    def turn_all(query_raw, key_raw):
        return (base_rotate(query_raw, cosines, sines) * 0.0625, base_rotate(key_raw, cosines, sines))

    (query_turned, key_turned), turn_back = jax.vjp(
        turn_all, mixed_qkv[:, :, 0], mixed_qkv[:, :, 1]
    )
    query_low = query_turned.astype(jnp.bfloat16)
    key_low = key_turned.astype(jnp.bfloat16)
    value_low = mixed_qkv[:, :, 2].astype(jnp.bfloat16)
    start_top = jnp.full((group_size, block_size, HEADS), masked_value, jnp.float32)
    key_piece = lax.all_gather(key_low, "seq", axis=1, tiled=True)
    value_piece = lax.all_gather(value_low, "seq", axis=1, tiled=True)
    seg_piece = lax.all_gather(segments, "seq", axis=1, tiled=True)
    key_pos = jnp.arange(seg_piece.shape[1], dtype=jnp.int32)
    allowed = visible(segments, local_pos, seg_piece, key_pos)
    scores = jnp.einsum("gqhd,gkhd->gqhk", query_low, key_piece, preferred_element_type=jnp.float32)
    scores = jnp.where(allowed, scores, masked_value)
    new_top = jnp.maximum(start_top, jnp.max(scores, axis=-1))
    weights = jnp.where(allowed, jnp.exp(scores - new_top[..., None]), 0.0)
    new_total = jnp.sum(weights, axis=-1)
    new_out = jnp.einsum(
        "gqhk,gkhd->gqhd",
        weights.astype(jnp.bfloat16),
        value_piece,
        preferred_element_type=jnp.float32,
    )
    attended = new_out / new_total[..., None]
    log_total = new_top + jnp.log(new_total)
    attended_low = attended.astype(jnp.bfloat16).reshape(row_count, model_width)
    attn_out = jnp.dot(
        attended_low, weight_out, preferred_element_type=jnp.float32
    ) + bias_out.astype(jnp.float32)
    mlp_full = (
        lax.all_gather(ln2_gain, ("dp", "seq"), axis=0, tiled=True),
        lax.all_gather(ln2_bias, ("dp", "seq"), axis=0, tiled=True),
        lax.all_gather(fc1_weight, ("dp", "seq"), axis=0, tiled=True),
        lax.all_gather(fc1_bias, ("dp", "seq"), axis=0, tiled=True),
        lax.all_gather(fc2_weight, ("dp", "seq"), axis=0, tiled=True),
        lax.all_gather(fc2_bias, ("dp", "seq"), axis=0, tiled=True),
    )
    gain_two, bias_two, weight_up, bias_up, weight_down, bias_down = mlp_full
    normed_two, norm_back_two = jax.vjp(
        layer_norm, flat_in, gain_two.astype(jnp.float32), bias_two.astype(jnp.float32)
    )
    act_two = normed_two.astype(jnp.bfloat16)
    hidden = jnp.dot(act_two, weight_up, preferred_element_type=jnp.float32) + bias_up.astype(
        jnp.float32
    )
    activated, gelu_back = jax.vjp(gelu_exact, hidden)
    act_hidden = activated.astype(jnp.bfloat16)
    mlp_out = jnp.dot(
        act_hidden, weight_down, preferred_element_type=jnp.float32
    ) + bias_down.astype(jnp.float32)
    mixed = (
        (flat_in + attn_out + mlp_out)
        .astype(jnp.bfloat16)
        .reshape(group_size, block_size, model_width)
    )
    back_up, back_down = (
        lax.all_gather(fc1_weight, ("dp", "seq"), axis=0, tiled=True),
        lax.all_gather(fc2_weight, ("dp", "seq"), axis=0, tiled=True),
    )
    back_qkv, back_out = (
        lax.all_gather(qkv_weight, ("dp", "seq"), axis=0, tiled=True),
        lax.all_gather(out_weight, ("dp", "seq"), axis=0, tiled=True),
    )
    grad_out = cotangent.reshape(row_count, model_width)
    grad_float = grad_out.astype(jnp.float32)
    grad_down_weight = jnp.dot(act_hidden.T, grad_out, preferred_element_type=jnp.float32)
    grad_down_bias = jnp.sum(grad_float, axis=0)
    grad_activated = jnp.dot(grad_out, back_down.T, preferred_element_type=jnp.float32)
    (grad_hidden,) = gelu_back(grad_activated)
    grad_hidden_low = grad_hidden.astype(jnp.bfloat16)
    grad_up_weight = jnp.dot(act_two.T, grad_hidden_low, preferred_element_type=jnp.float32)
    grad_up_bias = jnp.sum(grad_hidden_low.astype(jnp.float32), axis=0)
    grad_act_two = jnp.dot(grad_hidden_low, back_up.T, preferred_element_type=jnp.float32)
    grad_in_two, grad_gain_two, grad_bias_two = norm_back_two(grad_act_two)
    mlp_shards = (
        lax.psum_scatter(grad_gain_two, ("dp", "seq"), scatter_dimension=0, tiled=True),
        lax.psum_scatter(grad_bias_two, ("dp", "seq"), scatter_dimension=0, tiled=True),
        lax.psum_scatter(grad_up_weight, ("dp", "seq"), scatter_dimension=0, tiled=True),
        lax.psum_scatter(grad_up_bias, ("dp", "seq"), scatter_dimension=0, tiled=True),
        lax.psum_scatter(grad_down_weight, ("dp", "seq"), scatter_dimension=0, tiled=True),
        lax.psum_scatter(grad_down_bias, ("dp", "seq"), scatter_dimension=0, tiled=True),
    )
    grad_out_weight = jnp.dot(attended_low.T, grad_out, preferred_element_type=jnp.float32)
    grad_out_bias = jnp.sum(grad_float, axis=0)
    grad_attended = jnp.dot(grad_out, back_out.T, preferred_element_type=jnp.float32)
    grad_low = grad_attended.reshape(group_size, block_size, HEADS, HD).astype(jnp.bfloat16)
    delta = jnp.sum(grad_low.astype(jnp.float32) * attended, axis=-1)
    key_piece = lax.all_gather(key_low, "seq", axis=1, tiled=True)
    value_piece = lax.all_gather(value_low, "seq", axis=1, tiled=True)
    seg_piece = lax.all_gather(segments, "seq", axis=1, tiled=True)
    key_pos = jnp.arange(seg_piece.shape[1], dtype=jnp.int32)
    allowed = visible(segments, local_pos, seg_piece, key_pos)
    scores = jnp.einsum("gqhd,gkhd->gqhk", query_low, key_piece, preferred_element_type=jnp.float32)
    chances = jnp.where(allowed, jnp.exp(scores - log_total[..., None]), 0.0)
    grad_chances = jnp.einsum(
        "gqhd,gkhd->gqhk", grad_low, value_piece, preferred_element_type=jnp.float32
    )
    grad_scores = (chances * (grad_chances - delta[..., None])).astype(jnp.bfloat16)
    grad_query = jnp.einsum(
        "gqhk,gkhd->gqhd", grad_scores, key_piece, preferred_element_type=jnp.float32
    )
    query_piece = lax.all_gather(query_low, "seq", axis=1, tiled=True)
    grad_piece = lax.all_gather(grad_low, "seq", axis=1, tiled=True)
    lse_piece = lax.all_gather(log_total.astype(jnp.bfloat16), "seq", axis=1, tiled=True).astype(
        jnp.float32
    )
    delta_piece = lax.all_gather(delta.astype(jnp.bfloat16), "seq", axis=1, tiled=True).astype(
        jnp.float32
    )
    seg_piece = lax.all_gather(segments, "seq", axis=1, tiled=True)
    query_pos = jnp.arange(seg_piece.shape[1], dtype=jnp.int32)
    allowed = visible(seg_piece, query_pos, segments, local_pos)
    scores = jnp.einsum("gqhd,gkhd->gqhk", query_piece, key_low, preferred_element_type=jnp.float32)
    chances = jnp.where(allowed, jnp.exp(scores - lse_piece[..., None]), 0.0)
    new_value = jnp.einsum(
        "gqhk,gqhd->gkhd",
        chances.astype(jnp.bfloat16),
        grad_piece,
        preferred_element_type=jnp.float32,
    )
    grad_chances = jnp.einsum(
        "gqhd,gkhd->gqhk", grad_piece, value_low, preferred_element_type=jnp.float32
    )
    grad_scores = (chances * (grad_chances - delta_piece[..., None])).astype(jnp.bfloat16)
    new_key = jnp.einsum(
        "gqhk,gqhd->gkhd", grad_scores, query_piece, preferred_element_type=jnp.float32
    )
    grad_query_raw, grad_key_raw = turn_back((grad_query, new_key))
    grad_qkv_low = (
        jnp.stack([grad_query_raw, grad_key_raw, new_value], axis=2)
        .reshape(row_count, 3 * model_width)
        .astype(jnp.bfloat16)
    )
    grad_qkv_weight = jnp.dot(act_one.T, grad_qkv_low, preferred_element_type=jnp.float32)
    grad_qkv_bias = jnp.sum(grad_qkv_low.astype(jnp.float32), axis=0)
    grad_act_one = jnp.dot(grad_qkv_low, back_qkv.T, preferred_element_type=jnp.float32)
    grad_in_one, grad_gain_one, grad_bias_one = norm_back_one(grad_act_one)
    attention_shards = (
        lax.psum_scatter(grad_gain_one, ("dp", "seq"), scatter_dimension=0, tiled=True),
        lax.psum_scatter(grad_bias_one, ("dp", "seq"), scatter_dimension=0, tiled=True),
        lax.psum_scatter(grad_qkv_weight, ("dp", "seq"), scatter_dimension=0, tiled=True),
        lax.psum_scatter(grad_qkv_bias, ("dp", "seq"), scatter_dimension=0, tiled=True),
        lax.psum_scatter(grad_out_weight, ("dp", "seq"), scatter_dimension=0, tiled=True),
        lax.psum_scatter(grad_out_bias, ("dp", "seq"), scatter_dimension=0, tiled=True),
    )
    grad_tokens = (
        (grad_float + grad_in_one + grad_in_two)
        .astype(jnp.bfloat16)
        .reshape(group_size, block_size, model_width)
    )
    return (
        mixed,
        grad_tokens,
        attention_shards[0],
        attention_shards[1],
        attention_shards[2],
        attention_shards[3],
        attention_shards[4],
        attention_shards[5],
        mlp_shards[0],
        mlp_shards[1],
        mlp_shards[2],
        mlp_shards[3],
        mlp_shards[4],
        mlp_shards[5],
    )


GROUP = ("z", "y")
PEERS = ("x", "c")
EVERY = ("z", "y", "x", "c")
TURNS = 2 * CORES
ORDER = (0, 1, 7, 2, 6, 3, 5, 4)
LIMIT = 56 * 1024 * 1024
SMALL = 26 * 1024 * 1024
bf16, f32 = jnp.bfloat16, jnp.float32


def whole_ref():
    return pl.BlockSpec(memory_space=pltpu.VMEM)


def in_place():
    return pl.BlockSpec(memory_space=pl.ANY)


def call(
    kernel, results, inputs, operands, outputs, grid=(), prefetch=0, aliases=None, scratch=(), limit=LIMIT
):
    return pl.pallas_call(
        kernel,
        out_shape=[jax.ShapeDtypeStruct(*result) for result in results],
        grid_spec=pltpu.PrefetchScalarGridSpec(
            num_scalar_prefetch=prefetch, grid=grid, in_specs=inputs, out_specs=outputs, scratch_shapes=scratch
        ),
        input_output_aliases=aliases or {},
        compiler_params=pltpu.CompilerParams(vmem_limit_bytes=limit),
        cost_estimate=pl.CostEstimate(flops=1, bytes_accessed=1, transcendentals=0),
    )(*operands)


class Line:
    def __init__(self):
        self.last = ()

    def __call__(self, function, *operands, wait=()):
        operands = lax.optimization_barrier((operands, self.last, wait))[0]
        results = function(*operands)
        self.last = tuple(jax.tree.leaves(results))
        return results

    def hold(self, values):
        return lax.optimization_barrier((values, self.last))[0]


def after(value, *others):
    return lax.optimization_barrier((value, *others))[0]


def ring_perm(shift):
    depth, width = lax.axis_size("z"), lax.axis_size("y")
    places = [z * width for z in range(depth)] + [z * width + 1 for z in reversed(range(depth))]
    count = len(places)
    return [(places[i], places[(i + shift) % count]) for i in range(count)]


class Gather:
    def __init__(self, block):
        self.held = {0: [block]}
        self.ahead = self.behind = block
        self.done = 0

    def step(self, line, *others):
        half = len(ORDER) // 2
        ahead, behind = line.hold((self.ahead, self.behind, *others))[:2]
        self.done += 1
        if self.done < half:
            self.behind = lax.ppermute(behind, GROUP, ring_perm(1))
            self.ahead = lax.ppermute(ahead, GROUP, ring_perm(-1))
            self.held[len(ORDER) - self.done] = [self.behind]
            self.held[self.done] = [self.ahead]
        else:
            cut = behind.shape[0] // 2
            self.held[half] = [
                lax.ppermute(behind[:cut], GROUP, ring_perm(1)),
                lax.ppermute(ahead[cut:], GROUP, ring_perm(-1)),
            ]


def swap(values, axis):
    return lax.ppermute(values, axis, [(0, 1), (1, 0)])


def dot_f32(left, right, dims=((1,), (0,))):
    return lax.dot_general(left, right, (dims, ((), ())), preferred_element_type=f32)


def tile_spec(shape, index):
    return pl.BlockSpec(shape, lambda i, *scalars: index(i))


def same(shape):
    return tile_spec(shape, lambda i: (0,) * len(shape))


def spread_kernel(up, qkv, result):
    share, _, columns = result.shape
    tile = columns - 3 * HD
    for t in range(share):
        for i in range(3):
            at = (i * share + t) * HD
            result[t, :, i * HD : (i + 1) * HD] = qkv[:, at : at + HD]
        result[t, :, 3 * HD :] = up[:, t * tile : (t + 1) * tile]


def spread(up, qkv, share):
    rows, columns = up.shape
    return call(
        spread_kernel,
        [((share, rows, 3 * HD + columns // share), bf16)],
        [whole_ref()] * 2,
        (up, qkv),
        [whole_ref()],
    )[0]


def assemble_kernel(mine, *refs):
    sources, result = refs[:TURNS], refs[TURNS]
    for entry in range(result.shape[0]):
        for turn in range(TURNS):
            result[entry, pl.ds(mine[0] ^ turn, 1)] = sources[turn][entry : entry + 1]


def assemble(pieces, mine, step=2):
    entries, rows, columns = pieces[0].shape
    step = min(step, entries)
    return call(
        assemble_kernel,
        [((entries, TURNS, rows, columns), pieces[0].dtype)],
        [tile_spec((step, rows, columns), lambda i: (i, 0, 0))] * TURNS,
        (mine, *pieces),
        [tile_spec((step, TURNS, rows, columns), lambda i: (i, 0, 0, 0))],
        grid=(entries // step,),
        prefetch=1,
    )[0].reshape(entries * TURNS * rows, columns)


def settle_kernel(depth, peer, *refs):
    sources, result = refs[:-1], refs[-1]
    share = sources[0].shape[0]
    for shift, source in enumerate(sources):
        at = ((depth[0] + len(sources) - shift) % len(sources)) * share
        for j in range(share):
            result[pl.ds(at + (j ^ peer[0]), 1)] = source[j : j + 1]


def settle(depth, peer, *sources):
    shape = (len(sources) * sources[0].shape[0], *sources[0].shape[1:])
    return call(
        settle_kernel,
        [(shape, sources[0].dtype)],
        [same(source.shape) for source in sources],
        (depth, peer, *sources),
        [same(shape)],
        grid=(1,),
        prefetch=2,
    )[0]


def norm_kernel(count, affine, *refs):
    pieces, (one, two, mean_ref, scale_ref, one_turned, two_turned) = refs[:count], refs[-6:]
    values = stacked(pieces).astype(f32)
    mean = jnp.mean(values, axis=-1, keepdims=True)
    centered = values - mean
    scale = lax.rsqrt(jnp.mean(centered * centered, axis=-1, keepdims=True) + epsilon)
    normal = centered * scale
    for at, result, turned in ((0, one, one_turned), (2, two, two_turned)):
        act = (normal * affine[at : at + 1] + affine[at + 1 : at + 2]).astype(bf16)
        result[...] = act
        turned[...] = act.T.reshape(turned.shape)
    mean_ref[...] = mean
    scale_ref[...] = scale


def norm_block(at, pieces, affine, kept, slim):
    block, model = sum(piece.shape[0] for piece in pieces), pieces[0].shape[1]
    rows = len(ORDER) * block
    turned = (model // (TURNS * slim), 2, CORES, slim)
    results = [
        ((rows, model), bf16),
        ((rows, model), bf16),
        ((rows, 1), f32),
        ((rows, 1), f32),
        ((*turned, rows), bf16),
        ((*turned, rows), bf16),
    ]
    outputs = [pl.BlockSpec((block, shape[1]), lambda i: (at, 0)) for shape, _ in results[:4]]
    outputs += [pl.BlockSpec((*turned, block), lambda i: (0, 0, 0, 0, at))] * 2
    operands = [affine, *pieces]
    inputs = [whole_ref()] * len(operands)
    aliases = {}
    if kept is not None:
        aliases = {len(operands) + i: i for i in range(len(results))}
        operands += kept
        inputs += [in_place()] * len(results)
    return call(
        functools.partial(norm_kernel, len(pieces)), results, inputs, operands, outputs, grid=(1,), aliases=aliases
    )


def rotary_tables(places):
    half_rot = ROT // 2
    frequencies = 10000.0 ** (
        -(jnp.arange(half_rot, dtype=jnp.int32).astype(f32) * 2.0 / ROT)
    )
    turned = places.astype(f32)[:, None] * frequencies[None, :]
    cosines, sines = jnp.cos(turned), jnp.sin(turned)
    rest = jnp.zeros((places.shape[0], 128 - ROT), f32)
    none = jnp.zeros_like(sines)
    return (
        jnp.concatenate([cosines, cosines, rest + 1.0], axis=1),
        jnp.concatenate([sines, none, rest], axis=1),
        jnp.concatenate([none, sines, rest], axis=1),
    )


def rotate(values, tables, sign):
    cosines, first, second = tables
    half_rot = ROT // 2
    low = values[:, :128]
    ahead = pltpu.roll(low, 128 - half_rot, 1)
    behind = pltpu.roll(low, half_rot, 1)
    low = low * cosines + sign * (behind * second - ahead * first)
    return jnp.concatenate([low, values[:, 128:]], axis=1)


def qkv_kernel(depth_of, far_of, core, act, weight, bias, cosines, first, second, *results):
    qkv = jnp.dot(act[...], weight[...], preferred_element_type=f32) + bias[...]
    tables = (cosines[...], first[...], second[...])
    query = (rotate(qkv[:, :HD], tables, 1.0) * 0.0625).astype(bf16)
    key = rotate(qkv[:, HD : 2 * HD], tables, 1.0).astype(bf16)
    value = qkv[:, 2 * HD :].astype(bf16)
    parts = act.shape[0] // results[0].shape[2]
    start = pl.program_id(0) * parts
    spill(jnp.concatenate([query, key, value], axis=1), depth_of, far_of, core, start, results)


def spill(values, depth_of, far_of, core, start, results):
    block = results[0].shape[2]
    for part in range(values.shape[0] // block):
        at = start + part
        rows = values[None, None, part * block : (part + 1) * block]
        owner, low = depth_of[at] // 2, depth_of[at] % 2
        for result, mine in zip(results, (True, False)):

            @pl.when((owner == core[0]) == mine)
            def _():
                result[pl.ds(low, 1), pl.ds(far_of[at], 1)] = rows


def project(act, weight, bias, tables, depth_of, far_of, core, block):
    rows, model = act.shape
    columns = weight.shape[1]
    step = 4 * block
    return call(
        qkv_kernel,
        [((2, 2, block, columns), bf16)] * 2,
        [tile_spec((step, model), lambda i: (i, 0)), same((model, columns)), same((1, columns))]
        + [tile_spec((step, 128), lambda i: (i, 0))] * 3,
        (depth_of, far_of, core, act, weight, bias, *tables),
        [same((2, 2, block, columns))] * 2,
        grid=(rows // step,),
        prefetch=3,
    )


def place_kernel(depth_of, far_of, core, mine, came, result, *turned):
    block = result.shape[1]
    for at in range(result.shape[0]):
        for source, own in ((mine, True), (came, False)):

            @pl.when((depth_of[at] // 2 == core[0]) == own)
            def _():
                values = source[pl.ds(depth_of[at] % 2, 1), pl.ds(far_of[at], 1)][0, 0]
                result[at] = values
                for other in turned:
                    other[:, at * block : (at + 1) * block] = values.T


def place(mine, came, depth_of, far_of, core, turn=False):
    low, far, block, columns = mine.shape
    count = 2 * low * far
    shapes = [(count, block, columns)] + [(columns, count * block)] * turn
    placed, *turned = call(
        place_kernel,
        [(shape, bf16) for shape in shapes],
        [same(mine.shape)] * 2,
        (depth_of, far_of, core, mine, came),
        [same(shape) for shape in shapes],
        grid=(1,),
        prefetch=3,
        limit=SMALL,
    )
    return (placed.reshape(count * block, columns), *turned)


def pairs(ref, rows):
    return [(far, slice(at, at + rows)) for far in range(ref.shape[1]) for at in range(0, ref.shape[2], rows)]


def gathered(mine, came, even, seq, start, rows):
    parts = []
    for far, at in pairs(mine, rows):
        own, other = (ref[seq, far, at, start : start + HD] for ref in (mine, came))
        parts += [jnp.where(even, own, other), jnp.where(even, other, own)]
    return jnp.concatenate(parts, axis=0)


def scattered(mine, sent, even, seq, start, rows, values):
    for i, (far, at) in enumerate(pairs(mine, rows)):
        first, second = (values[(2 * i + k) * rows : (2 * i + k + 1) * rows] for k in range(2))
        mine[seq, far, at, start : start + HD] = jnp.where(even, first, second)
        sent[seq, far, at, start : start + HD] = jnp.where(even, second, first)


def chances_of(query, key, segments):
    scores = dot_f32(query, key, ((1,), (1,)))
    col_seg = jnp.broadcast_to(segments, scores.shape)
    row_seg = col_seg.T
    row_pos = lax.broadcasted_iota(jnp.int32, scores.shape, 0)
    col_pos = lax.broadcasted_iota(jnp.int32, scores.shape, 1)
    scores = jnp.where((col_pos <= row_pos) & (col_seg == row_seg), scores, masked_value)
    weights = jnp.exp(scores - jnp.max(scores, axis=-1, keepdims=True))
    return weights / jnp.sum(weights, axis=-1, keepdims=True)


def forward_kernel(rows, core, segments, mine, came, kept, sent):
    even = core[0] == 0
    for seq in range(mine.shape[0]):
        query, key, value = (gathered(mine, came, even, seq, i * HD, rows) for i in range(3))
        chances = chances_of(query, key, segments[seq])
        scattered(kept, sent, even, seq, 0, rows, dot_f32(chances.astype(bf16), value).astype(bf16))


def backward_kernel(
    rows, core, segments, cosines, first, second, mine, came, grad_mine, grad_came, kept, sent
):
    even = core[0] == 0
    tables = (cosines[...], first[...], second[...])
    for seq in range(mine.shape[0]):
        query, key, value = (gathered(mine, came, even, seq, i * HD, rows) for i in range(3))
        grad = gathered(grad_mine, grad_came, even, seq, 0, rows)
        chances = chances_of(query, key, segments[seq])
        chances_low = chances.astype(bf16)
        grad_chances = dot_f32(grad, value, ((1,), (1,)))
        delta = jnp.sum(chances_low.astype(f32) * grad_chances, axis=-1, keepdims=True)
        grad_scores = (chances * (grad_chances - delta)).astype(bf16)
        grad_query = dot_f32(grad_scores, key)
        grad_key = dot_f32(grad_scores, query, ((0,), (0,)))
        grad_value = dot_f32(chances_low, grad, ((0,), (0,)))
        for i, part in enumerate(
            (rotate(grad_query * 0.0625, tables, -1.0), rotate(grad_key, tables, -1.0), grad_value)
        ):
            scattered(kept, sent, even, seq, i * HD, rows, part.astype(bf16))


def attend(kernel, rows, columns, core, given, *arrays):
    operands = (*given, *arrays)
    shape = (*arrays[0].shape[:3], columns)
    return call(
        functools.partial(kernel, rows),
        [(shape, bf16)] * 2,
        [same(a.shape) for a in operands],
        (core, *operands),
        [same(shape)] * 2,
        grid=(1,),
        prefetch=1,
        limit=SMALL,
    )


def widen_kernel(act, weight, bias, activated, slope, turned):
    hidden = jnp.dot(act[...], weight[...], preferred_element_type=f32) + bias[...]
    cdf = 0.5 * (1.0 + lax.erf(hidden * math.sqrt(0.5)))
    result = (hidden * cdf).astype(bf16)
    activated[...] = result
    turned[...] = result.T
    slope[...] = cdf + hidden * jnp.exp(-0.5 * hidden * hidden) * (1.0 / math.sqrt(2.0 * math.pi))


def widen(act, weight, bias, tile=256):
    rows, model = act.shape
    columns = weight.shape[1]
    return call(
        widen_kernel,
        [((rows, columns), bf16), ((rows, columns), f32), ((columns, rows), bf16)],
        [
            same((rows, model)),
            tile_spec((model, tile), lambda i: (0, i)),
            tile_spec((1, tile), lambda i: (0, i)),
        ],
        (act, weight, bias),
        [tile_spec((rows, tile), lambda i: (0, i))] * 2 + [tile_spec((tile, rows), lambda i: (i, 0))],
        grid=(columns // tile,),
    )


def stacked(refs):
    return jnp.concatenate([ref[...] for ref in refs], axis=0)


def narrow_kernel(weight, slope, *refs):
    blocks, (result, sums) = refs[:-2], refs[-2:]
    grad = dot_f32(stacked(blocks), weight[...], ((1,), (1,))) * slope[...]
    grad = grad.astype(bf16)
    result[...] = grad
    sums[...] = jnp.sum(grad.astype(f32), axis=0, keepdims=True)


def narrow(blocks, weight, slope, tile=256):
    rows, columns = slope.shape
    model = weight.shape[1]
    return call(
        narrow_kernel,
        [((rows, columns), bf16), ((1, columns), f32)],
        [tile_spec((tile, model), lambda i: (i, 0)), tile_spec((rows, tile), lambda i: (0, i))]
        + [same(piece.shape) for piece in blocks],
        (weight, slope, *blocks),
        [tile_spec((rows, tile), lambda i: (0, i)), tile_spec((1, tile), lambda i: (0, i))],
        grid=(columns // tile,),
        limit=SMALL,
    )


def head_kernel(depth_of, far_of, core, weight, *refs):
    blocks, results, total = refs[:-3], refs[-3:-1], refs[-1]
    part = dot_f32(stacked(blocks), weight[...], ((1,), (1,)))
    step = pl.program_id(0)

    @pl.when(step == 0)
    def _():
        total[...] = part

    @pl.when(step > 0)
    def _():
        total[...] += part

    @pl.when(step == pl.num_programs(0) - 1)
    def _():
        spill(total[...].astype(bf16), depth_of, far_of, core, 0, results)


def head_grads(blocks, weight, depth_of, far_of, core, block, tile=512):
    rows = sum(piece.shape[0] for piece in blocks)
    return call(
        head_kernel,
        [((2, 2, block, HD), bf16)] * 2,
        [tile_spec((piece.shape[0], tile), lambda i: (0, i)) for piece in (weight, *blocks)],
        (depth_of, far_of, core, weight, *blocks),
        [same((2, 2, block, HD))] * 2,
        grid=(weight.shape[1] // tile,),
        prefetch=3,
        scratch=[pltpu.VMEM((rows, HD), f32)],
        limit=SMALL,
    )


def across(total, half, near, far):
    first, second = total[:, 0], total[:, 1]
    low = half[0] == 0
    near[...] = jnp.where(low, first, second).reshape(near.shape)
    far[...] = jnp.where(low, second, first).astype(bf16).reshape(far.shape)


def rows_kernel(near, core, half, act, grad, *refs):
    entries, _, _, rows, tokens = act.shape
    total = dot_f32(act[...].reshape(entries * 2 * rows, tokens), grad[...])
    total = total.reshape(entries, 2, rows, grad.shape[1])
    if near:
        came, kept, sent = refs
        across(total + came[...].astype(f32), half, kept, sent)
    else:
        refs[0][...] = total.astype(bf16)


def rows_grad(turned, grad, core, half, came=None, step=4):
    entries, _, _, rows, tokens = turned.shape
    columns = grad.shape[1]
    near = came is not None
    spec = tile_spec((step, 2, rows, columns), lambda i: (i, 0, 0, 0))
    inputs = [
        pl.BlockSpec(
            (step, 2, 1, rows, tokens), lambda i, c, x: (i, 0, c[0] if near else 1 - c[0], 0, 0)
        ),
        same((tokens, columns)),
    ]
    if near:
        results = [((entries, rows, columns), f32), ((entries, rows, columns), bf16)]
        outputs = [tile_spec((step, rows, columns), lambda i: (i, 0, 0))] * 2
    else:
        results, outputs = [((entries, 2, rows, columns), bf16)], [spec]
    return call(
        functools.partial(rows_kernel, near),
        results,
        inputs + [spec] * near,
        (core, half, turned, grad) + (came,) * near,
        outputs,
        grid=(entries // step,),
        prefetch=2,
        limit=SMALL,
    )


def down_kernel(near, core, half, attended, activated, *refs):
    count = 3 if near else 1
    blocks, refs = refs[:-count], refs[-count:]
    parts = [ref[x, 0] for x in range(2) for ref in (attended, activated)]
    total = dot_f32(jnp.concatenate(parts, axis=0), stacked(blocks))
    total = total.reshape(1, 2, total.shape[0] // 2, total.shape[1])
    if near:
        came, kept, sent = refs
        across(total + came[...][None].astype(f32), half, kept, sent)
    else:
        refs[0][...] = total[0].astype(bf16)


def down_grad(attended, activated, blocks, core, half, came=None, tile=512):
    tokens = attended.shape[3]
    model = blocks[0].shape[1]
    rows = attended.shape[2] + activated.shape[2]
    near = came is not None
    spec = tile_spec((2, rows, tile), lambda i: (0, 0, i))
    inputs = [
        pl.BlockSpec(
            (2, 1, turned.shape[2], tokens), lambda i, c, x: (0, c[0] if near else 1 - c[0], 0, 0)
        )
        for turned in (attended, activated)
    ]
    inputs += [tile_spec((piece.shape[0], tile), lambda i: (0, i)) for piece in blocks]
    if near:
        results = [((rows, model), f32), ((rows, model), bf16)]
        outputs = [tile_spec((rows, tile), lambda i: (0, i))] * 2
    else:
        results, outputs = [((2, rows, model), bf16)], [spec]
    return call(
        functools.partial(down_kernel, near),
        results,
        inputs + [spec] * near,
        (core, half, attended, activated, *blocks) + (came,) * near,
        outputs,
        grid=(model // tile,),
        prefetch=2,
        limit=SMALL,
    )


def join_kernel(pieces, given, result, *sums):
    share = given.shape[0]
    width = result.shape[1] // (share * pieces)
    for t in range(share):
        for i in range(pieces):
            at = (i * share + t) * width
            result[:, at : at + width] = given[t, :, i * width : (i + 1) * width].astype(f32)
    for ref in sums:
        rows, columns = ref.shape
        ref[...] = jnp.sum(given[:, :rows, pieces * width : pieces * width + columns].astype(f32), axis=0)


def join(given, pieces, extra=None):
    share, rows, columns = given.shape
    results = [((rows, share * (columns - (extra[1] if extra else 0))), f32)]
    results += [(extra, f32)] if extra else []
    return call(
        functools.partial(join_kernel, pieces), results, [whole_ref()], (given,), [whole_ref()] * len(results)
    )


def widen_rows_kernel(mine, came, extra, result):
    columns = mine.shape[2]
    result[:, :, :columns] = (mine[...] + came[...].astype(f32)).astype(bf16)
    result[:, :, columns:] = jnp.zeros((*result.shape[:2], result.shape[2] - columns), bf16)
    result[:, : extra.shape[1], columns:] = extra[...].astype(bf16)


def total_with(mine, came, extra):
    shape = (*mine.shape[:2], mine.shape[2] + extra.shape[2])
    operands = (mine, came, extra)
    return call(widen_rows_kernel, [(shape, bf16)], [whole_ref()] * 3, operands, [whole_ref()])[0]


def share_part(pull, first, count, block, lefts, rights, pieces, extras=(), tile=512):
    model = rights[0].shape[0 if pull else 1]
    depths = [right.shape[1 if pull else 0] for right in rights]
    operands, inputs = [], []
    for left, depth in zip(lefts, depths):
        for b in range(count):
            operands.append(left)
            inputs.append(tile_spec((block, depth), lambda i, b=b: (first + b, 0)))
    for right, depth in zip(rights, depths):
        operands.append(right)
        inputs.append(
            tile_spec((tile, depth), lambda i: (i, 0)) if pull else tile_spec((depth, tile), lambda i: (0, i))
        )
    given = 0
    if pull:
        gains, values, mean, scale = extras
        given = len(values)
        for row in (*gains, *values):
            operands.append(row)
            inputs.append(tile_spec((row.shape[0], tile), lambda i: (0, i)))
        for stat in (mean, scale):
            for b in range(count):
                operands.append(stat)
                inputs.append(tile_spec((block, 1), lambda i, b=b: (first + b, 0)))

    def kernel(*refs):
        refs = list(refs)

        def take(number):
            taken = refs[:number]
            del refs[:number]
            return taken

        left_a, left_b = stacked(take(count)), stacked(take(count))
        (right_a,), (right_b,) = take(1), take(1)
        dims = ((1,), (1,)) if pull else ((1,), (0,))
        part_a = dot_f32(left_a, right_a[...], dims)
        part_b = dot_f32(left_b, right_b[...], dims)
        if pull:
            gain_a, gain_b = take(2)
            tokens = stacked(take(given)).astype(f32)
            normal = (tokens - stacked(take(count))) * stacked(take(count))
            (sums,) = take(1)
            sums[...] = jnp.concatenate(
                [
                    jnp.sum(part, axis=0, keepdims=True)
                    for part in (part_a * normal, part_a, part_b * normal, part_b)
                ]
                + [jnp.zeros((4, tile), f32)],
                axis=0,
            )
            total = part_a * gain_a[...] + part_b * gain_b[...]
        else:
            total = part_a + part_b
        for (start, rows, dtype), result in zip(pieces, refs):
            result[...] = total[start : start + rows].astype(dtype)

    results = [((rows, model), dtype) for _, rows, dtype in pieces]
    outputs = [tile_spec((rows, tile), lambda i: (0, i)) for _, rows, _ in pieces]
    if pull:
        results = [((8, model), f32)] + results
        outputs = [tile_spec((8, tile), lambda i: (0, i))] + outputs
    return call(kernel, results, inputs, operands, outputs, grid=(model // tile,))


def out_kernel(order, left_a, left_b, right_a, right_b, result):
    total = dot_f32(left_a[...], right_a[...]) + dot_f32(left_b[...], right_b[...])
    block = result.shape[1]
    for at in range(result.shape[0]):
        result[pl.ds(order[at], 1)] = total[None, at * block : (at + 1) * block].astype(bf16)


def out_parts(left_a, left_b, right_a, right_b, order, block, tile=512):
    rows = left_a.shape[0]
    model = right_a.shape[1]
    return call(
        out_kernel,
        [((rows // block, block, model), bf16)],
        [same(left_a.shape), same(left_b.shape)]
        + [tile_spec((right.shape[0], tile), lambda i: (0, i)) for right in (right_a, right_b)],
        (order, left_a, left_b, right_a, right_b),
        [tile_spec((rows // block, block, tile), lambda i: (0, 0, i))],
        grid=(model // tile,),
        prefetch=1,
    )[0]


def early_pieces(block):
    cut = block // 2
    return [(2 * block, cut, bf16), (2 * block + cut, cut, bf16), (0, block, bf16), (block, block, bf16)]


def late_pieces(block):
    return [(0, block, f32)] + [(i * block, block, bf16) for i in range(1, 5)]


def all_pieces(block):
    return late_pieces(block) + [(5 * block + start, rows, dtype) for start, rows, dtype in early_pieces(block)]


def add_kernel(one, two, ahead, behind, *results):
    cut = ahead.shape[0]
    rows = one.shape[0]
    for mine, came, result, start in ((one, ahead, results[0], 0), (two, behind, results[1], rows - cut)):
        if cut < rows:
            result[...] = mine[...]
        at = slice(start, start + cut)
        result[at] = (mine[at].astype(f32) + came[...].astype(f32)).astype(bf16)


def add_incoming(one, two, ahead, behind, tile=1024):
    rows, model = one.shape
    return call(
        add_kernel,
        [(one.shape, bf16)] * 2,
        [tile_spec((a.shape[0], tile), lambda i: (0, i)) for a in (one, two, ahead, behind)],
        (one, two, ahead, behind),
        [tile_spec((rows, tile), lambda i: (0, i))] * 2,
        grid=(model // tile,),
    )


class Scatter:
    def send(self, one, two):
        self.ahead = lax.ppermute(one, GROUP, ring_perm(1))
        self.behind = lax.ppermute(two, GROUP, ring_perm(-1))

    def step(self, line, one, two):
        self.send(*line(add_incoming, one, two, self.ahead, self.behind))


def total_kernel(mine, came, *results):
    total = mine[...] + came[...].astype(f32)
    at = 0
    for result in results:
        rows = result.shape[0]
        result[...] = total[at : at + rows].astype(result.dtype)
        at += rows


def total_rows(mine, came, pieces):
    tail = mine.shape[1:]
    steps = 2
    tile = tail[:-1] + (tail[-1] // steps,)

    def spec(rows):
        return tile_spec((rows, *tile), lambda i: (0,) * len(tile) + (i,))

    return call(
        total_kernel,
        [((rows, *tail), dtype) for rows, dtype in pieces],
        [spec(mine.shape[0])] * 2,
        (mine, came),
        [spec(rows) for rows, _ in pieces],
        grid=(steps,),
    )


def apart(values, half, kept, sent):
    cut = values.shape[0] // 2
    low = half[0] == 0
    first, second = values[:cut], values[cut:]
    kept[...] = jnp.where(low, first, second).astype(kept.dtype)
    sent[...] = jnp.where(low, second, first).astype(sent.dtype)


def mixed_kernel(half, total, tokens, bias_one, bias_two, kept, sent):
    total = total[...].astype(f32) + tokens[...].astype(f32)
    apart(total + bias_one[...] + bias_two[...], half, kept, sent)


def by_rows(kernel, half, operands, tokens):
    rows, model = tokens.shape
    return call(
        kernel,
        [((rows // 2, model), bf16)] * 2,
        [tile_spec((rows, 1), lambda i: (0, 0)) if a.shape[1] == 1 else same(a.shape) for a in operands],
        (half, *operands),
        [same((rows // 2, model))] * 2,
        grid=(1,),
        prefetch=1,
    )


def mixed_rows(half, *operands):
    return by_rows(mixed_kernel, half, operands, operands[1])


def vectors_kernel(share, norms, grad, grad_qkv, up_sum, result):
    result[...] = jnp.zeros_like(result)
    result[:4] = norms[:4]
    result[4:5] = jnp.sum(grad[...].astype(f32), axis=0, keepdims=True)
    qkv_sum = jnp.sum(grad_qkv[...].astype(f32), axis=0, keepdims=True)
    for i in range(3):
        at = pl.multiple_of(share[0] * HD, HD)
        result[5 + i : 6 + i, pl.ds(at, HD)] = qkv_sum[:, i * HD : (i + 1) * HD]
    columns = up_sum.shape[1]
    each = result.shape[1] // columns
    at = pl.multiple_of((share[0] % each) * columns, columns)
    result[pl.ds(8 + share[0] // each, 1), pl.ds(at, columns)] = up_sum[...]


def vectors(share, norms, grad, grad_qkv, up_sum):
    operands = (norms, grad, grad_qkv, up_sum)
    return call(
        vectors_kernel,
        [((16, norms.shape[1]), f32)],
        [same(a.shape) for a in operands],
        (share, *operands),
        [same((16, norms.shape[1]))],
        grid=(1,),
        prefetch=1,
    )[0]


def sum_kernel(*refs):
    total = refs[0][...]
    for ref in refs[1:-1]:
        total = total + ref[...]
    refs[-1][...] = total


def sum_arrays(*arrays):
    return call(
        sum_kernel, [(arrays[0].shape, f32)], [whole_ref()] * len(arrays), arrays, [whole_ref()]
    )[0]


def finish_kernel(half, own, ahead, behind, tokens, grad, mean, scale, kept, sent):
    pulled = own[...] + ahead[...].astype(f32) + behind[...].astype(f32)
    normal = (tokens[...].astype(f32) - mean[...]) * scale[...]
    inner = (
        pulled
        - jnp.mean(pulled, axis=-1, keepdims=True)
        - normal * jnp.mean(pulled * normal, axis=-1, keepdims=True)
    )
    apart(grad[...].astype(f32) + scale[...] * inner, half, kept, sent)


def finish(half, *operands):
    return by_rows(finish_kernel, half, operands, operands[3])


def trade_kernel(half, *refs):
    count = len(refs) // 3
    low = half[0] == 0
    for values, came, result in zip(refs[:count], refs[count : 2 * count], refs[2 * count :]):
        rows = came.shape[0]
        own = values[pl.ds(half[0], 1)][0]
        result[:rows] = jnp.where(low, own, came[...])
        result[rows:] = jnp.where(low, came[...], own)


def trade(half, arrays, came):
    shapes = [(2 * piece.shape[0], piece.shape[1]) for piece in came]
    return call(
        trade_kernel,
        [(shape, bf16) for shape in shapes],
        [same(a.shape) for a in (*arrays, *came)],
        (half, *arrays, *came),
        [same(shape) for shape in shapes],
        grid=(1,),
        prefetch=1,
    )


def in_order_kernel(half, *refs):
    count = len(refs) // 3
    for own, came, result in zip(refs[:count], refs[count : 2 * count], refs[2 * count :]):
        low = half[0] == 0
        result[0] = jnp.where(low, own[...], came[...])
        result[1] = jnp.where(low, came[...], own[...])


def in_order(half, own, came):
    operands = (*own, *came)
    return call(
        in_order_kernel,
        [((2, *a.shape), a.dtype) for a in own],
        [same(a.shape) for a in operands],
        (half, *operands),
        [same((2, *a.shape)) for a in own],
        grid=(1,),
        prefetch=1,
    )


def scalar(value):
    return jnp.reshape(value, (1,)).astype(jnp.int32)


def grouped(
    tokens,
    segments,
    ln1_gain,
    ln1_bias,
    qkv_weight,
    qkv_bias,
    out_weight,
    out_bias,
    ln2_gain,
    ln2_bias,
    fc1_weight,
    fc1_bias,
    fc2_weight,
    fc2_bias,
    cotangent,
):
    depth, width = lax.axis_size("z"), lax.axis_size("y")
    share = depth * width
    devices = share * TURNS
    z, y, x, c = (lax.axis_index(name) for name in EVERY)
    t = z * width + y
    mine = x * CORES + c
    r = jnp.where(y == 0, z, 2 * depth - 1 - z)
    seqs, rows, model = tokens.shape
    block = seqs * rows
    slim = ln1_gain.shape[0]
    hidden = fc2_weight.shape[0] * TURNS
    line = Line()

    sent = line(lambda up, qkv: spread(up, qkv, share), fc1_weight, qkv_weight)
    columns = lax.all_to_all(sent, GROUP, 0, 0, tiled=True)

    down_out = (out_weight[None], fc2_weight[None])
    down_out_near = [swap(piece, "c") for piece in line.hold(down_out)]
    came = [
        swap(lax.dynamic_index_in_dim(rows_of, 1 - x, 0, keepdims=False), "x")
        for rows_of in line.hold((tokens, cotangent))
    ]

    pieces = (
        ln1_gain,
        ln1_bias,
        ln2_gain,
        ln2_bias,
        out_bias,
        fc2_bias,
        qkv_bias,
        fc1_bias,
        segments.reshape(-1).astype(bf16),
    )
    ends = [0]
    for piece in pieces:
        ends.append(ends[-1] + piece.shape[0])
    packed = jnp.concatenate(line.hold(pieces))
    packed = jnp.pad(packed, (0, -ends[-1] % 1024)).reshape(1, -1, 128)
    for axis in ("c", "x", "y"):
        packed = jnp.concatenate([packed, swap(packed, axis)], axis=0)
    packed = [packed] + [
        lax.ppermute(packed, "z", [(i, (i + shift) % depth) for i in range(depth)]) for shift in range(1, depth)
    ]
    steps = (r + jnp.array(ORDER, jnp.int32)) % share
    far_of = (steps >= depth).astype(jnp.int32)
    depth_of = jnp.where(far_of == 1, 2 * depth - 1 - steps, steps)
    within = (jnp.arange(2, dtype=jnp.int32) * CORES + c)[:, None] * rows + jnp.arange(rows, dtype=jnp.int32)
    token_pos = far_of[:, None] * (TURNS * rows) + within.reshape(1, -1)
    token_tables = line(rotary_tables, token_pos.reshape(-1))
    seq_tables = line(rotary_tables, jnp.arange(rows * width * TURNS, dtype=jnp.int32))

    my_rows, my_grad = line(trade, scalar(x), (tokens, cotangent), came, wait=packed[0])
    down_out_far = [swap(piece, "x") for piece in line.hold(down_out)]
    packed = line(settle, scalar(z), scalar(y * TURNS + mine), *packed, wait=down_out_near).reshape(devices, -1)
    down_out_last = [swap(piece, "c") for piece in line.hold(down_out_far)]
    in_ring = Gather(my_rows)
    in_ring.step(line, columns, *down_out_last)
    small = [
        packed[:, ends[i] : ends[i + 1]].astype(f32).reshape(1, -1) for i in range(4, len(pieces) - 1)
    ]
    bias_out, bias_down, bias_qkv, bias_up = small
    affine = packed[:, : ends[4]].astype(f32).reshape(devices, 4, slim).transpose(1, 0, 2).reshape(4, model)
    bias_up = lax.dynamic_slice_in_dim(bias_up, t * hidden, hidden, 1)
    bias_qkv = lax.dynamic_index_in_dim(
        bias_qkv.reshape(3, HEADS, HD), t, 1, keepdims=False
    ).reshape(1, 3 * HD)

    all_seg = packed[:, ends[-2] : ends[-1]].reshape(depth, width * TURNS, seqs, rows)
    seq_seg = lax.dynamic_slice_in_dim(all_seg, c * 2, 2, 0)
    seq_seg = lax.dynamic_index_in_dim(seq_seg, x, 2, keepdims=False).reshape(2, -1).astype(f32)
    masks = (seq_seg[:, None, :],)

    def norm(at, kept):
        pieces = in_ring.held[ORDER[at]]
        return line(lambda *given: norm_block(at, *given, slim), pieces, affine, kept)

    kept = norm(0, None)
    qkv_cols, up_cols = after((columns[:, :, : 3 * HD], columns[:, :, 3 * HD :]), columns)
    qkv_far, up_far = swap(qkv_cols, "x"), swap(up_cols, "x")
    qkv_near, up_near = swap(qkv_cols, "c"), swap(up_cols, "c")
    weight_out, weight_down = (
        line(assemble, pieces, scalar(mine))
        for pieces in zip(down_out, down_out_near, down_out_far, down_out_last)
    )
    in_ring.step(line)
    kept = norm(1, kept)
    kept = norm(2, kept)
    in_ring.step(line)
    qkv_last = swap(line.hold(qkv_far), "c")
    kept = norm(3, kept)
    kept = norm(4, kept)
    weight_qkv = line(assemble, (qkv_cols, qkv_near, qkv_far, qkv_last), scalar(mine))
    in_ring.step(line)
    kept = norm(5, kept)
    kept = norm(6, kept)
    grad_ring = Gather(my_grad)
    grad_ring.step(line, *in_ring.held[4])
    up_last = swap(line.hold(up_far), "c")
    act_one, act_two, means, scales, turned_one, turned_two = norm(7, kept)

    lie = (depth_of, far_of, scalar(c))
    qkv_mine, sent = line(
        lambda *given: project(*given, block), act_one, weight_qkv, bias_qkv, token_tables, *lie
    )
    grad_ring.step(line)
    qkv_came = swap(sent, "c")
    weight_up = line(assemble, (up_cols, up_near, up_far, up_last), scalar(mine))
    out_mine, sent = line(
        lambda *given: attend(forward_kernel, rows, HD, *given), scalar(c), masks, qkv_mine, qkv_came
    )
    out_came = swap(sent, "c")
    grad_ring.step(line)
    act_hidden, slope, hidden_turned = line(widen, act_two, weight_up, bias_up)
    attended, attended_turned = line(lambda *given: place(*given, turn=True), out_mine, out_came, *lie)
    grad_ring.step(line)

    parts = line(
        lambda *given: out_parts(*given, block),
        attended,
        act_hidden,
        weight_out,
        weight_down,
        depth_of * width + far_of,
    )

    grads = [piece for j in ORDER for piece in grad_ring.held[j]]
    grad_mine, sent = line(lambda *given: head_grads(*given, block), grads, weight_out, *lie)
    grad_came = swap(sent, "c")
    mixed = lax.psum_scatter(line.hold(parts), GROUP, scatter_dimension=0, tiled=False)
    grad_hidden, up_sum = line(narrow, grads, weight_down, slope)
    which = (scalar(c), scalar(x))
    (up_far,) = line(rows_grad, turned_two, grad_hidden, *which)
    back_mine, sent = line(
        lambda *given: attend(backward_kernel, rows, 3 * HD, *given),
        scalar(c),
        (*masks, *seq_tables),
        qkv_mine,
        qkv_came,
        grad_mine,
        grad_came,
    )
    back_came, up_came = swap(sent, "c"), swap(line.hold(up_far), "c")
    down_lefts = (
        attended_turned.reshape(2, CORES, slim, -1),
        hidden_turned.reshape(2, CORES, hidden // TURNS, -1),
    )
    (down_far,) = line(down_grad, *down_lefts, grads, *which)
    (grad_qkv,) = line(place, back_mine, back_came, *lie)
    (qkv_far,) = line(rows_grad, turned_one, grad_qkv, *which)
    qkv_came = swap(qkv_far, "c")
    grad_up, up_far = line(rows_grad, turned_two, grad_hidden, *which, up_came)
    up_came = swap(up_far, "x")

    lefts, rights = (grad_qkv, grad_hidden), (weight_qkv, weight_up)

    def pull(left, right, more):
        return share_part(True, 0, len(ORDER), block, left, right, all_pieces(block), more)

    values = [piece for j in ORDER for piece in in_ring.held[j]]
    norm_sums, pull_own, *late = line(
        pull, lefts, rights, ((affine[0:1], affine[2:3]), values, means, scales)
    )
    late, (one, two, *early) = late[:4], late[4:]
    pull_ring = Scatter()
    pull_ring.send(one, two)
    sums = line(vectors, scalar(t), norm_sums, my_grad, grad_qkv, up_sum)
    grad_qkv_w, qkv_far = line(rows_grad, turned_one, grad_qkv, *which, qkv_came)
    (grad_up,) = line(lambda a, b: total_rows(a, b, [(share, bf16)]), grad_up, up_came)
    pull_ring.step(line, *early)
    grad_up = lax.all_to_all(line.hold(grad_up), GROUP, 0, 0, tiled=True)
    qkv_came, down_came = swap(line.hold(qkv_far), "x"), swap(line.hold(down_far), "c")
    sums_came = swap(line.hold(sums), "c")
    sums = line(sum_arrays, sums, sums_came)
    grad_down, down_far = line(down_grad, *down_lefts, grads, *which, down_came)
    kept_out, sent_out = line(mixed_rows, scalar(x), mixed, my_rows, bias_out, bias_down)
    pull_ring.step(line, late[2], late[3])
    sums_came = swap(line.hold(sums), "x")
    sums = line(sum_arrays, sums, sums_came)

    def slices(values, rows):
        cut = values.reshape(rows, share, TURNS, -1)
        return lax.dynamic_index_in_dim(cut, mine, 2, keepdims=False).transpose(1, 0, 2).reshape(share, -1)

    sums = jnp.concatenate([slices(sums[:5], 5), slices(sums[5:8], 1), slices(sums[8:12], 1)], axis=1)
    sums = jnp.pad(sums.reshape(share, -1, 128), ((0, 0), (0, 2), (0, 0)))
    grad_qkv_w = line(total_with, grad_qkv_w, qkv_came, sums)
    pull_ring.step(line, late[0], late[1])
    grad_qkv_w = lax.all_to_all(line.hold(grad_qkv_w), GROUP, 0, 0, tiled=True)
    down_came = swap(line.hold(down_far), "x")
    (grad_up,) = line(lambda given: join(given, 1), grad_up)
    kept_in, sent_in = line(
        finish, scalar(x), pull_own, pull_ring.ahead, pull_ring.behind, my_rows, my_grad, means, scales
    )
    grad_out, grad_down = line(
        lambda a, b: total_rows(a, b, [(slim, f32), (hidden // TURNS, f32)]), grad_down, down_came
    )
    grad_qkv_w, sums = line(lambda given: join(given, 3, (8, 128)), grad_qkv_w)
    came_in, came_out = (swap(sent, "x") for sent in line.hold((sent_in, sent_out)))
    mixed, grad_in = line(in_order, scalar(x), (kept_out, kept_in), (came_out, came_in))

    sums = sums.reshape(-1)
    norm_sums = [sums[i * slim : (i + 1) * slim] for i in range(5)]
    qkv_end = 5 * slim + qkv_bias.shape[0]
    return (
        mixed,
        grad_in,
        norm_sums[0],
        norm_sums[1],
        grad_qkv_w,
        sums[5 * slim : qkv_end],
        grad_out,
        norm_sums[4],
        norm_sums[2],
        norm_sums[3],
        grad_up,
        sums[qkv_end : qkv_end + fc1_bias.shape[0]],
        grad_down,
        norm_sums[4],
    )


def specs(batch, block):
    every = batch + block
    one, two, three = P(every), P(every, None), P(batch, block, None)
    arguments = (three, P(batch, block), one, one, two, one, two, one, one, one, two, one, two, one, three)
    results = (three, three, one, one, two, one, two, one, one, one, two, one, two, one)
    return arguments, results


def solution(mesh):
    depth, ring = mesh.shape["dp"], mesh.shape["seq"]
    width = ring // TURNS
    if width == 2 and depth == TURNS and depth * width == HEADS:
        chips = Mesh(mesh.devices.reshape(depth, width, 2, CORES), EVERY)
        arguments, results = specs(("z",), ("y", "x", "c"))
        return jax.shard_map(
            grouped, mesh=chips, in_specs=arguments, out_specs=results, check_vma=False
        )
    arguments, results = specs(("dp",), ("seq",))
    return jax.shard_map(
        per_device, mesh=mesh, in_specs=arguments, out_specs=results, check_vma=False
    )
```

```python
import functools
import math

import jax
import jax.numpy as jnp
from jax import lax
from jax.experimental import pallas as pl
from jax.experimental.pallas import tpu as pltpu
from jax.sharding import Mesh, PartitionSpec as P

HEADS = 8
HD = 256
ROT = 64
CORES = 2


epsilon = 1e-05
masked_value = -1e30


def layer_norm(values, gain, shift):
    average = jnp.mean(values, axis=-1, keepdims=True)
    centered = values - average
    variance = jnp.mean(centered * centered, axis=-1, keepdims=True)
    return centered * lax.rsqrt(variance + epsilon) * gain + shift


def base_tables(places):
    half_rot = ROT // 2
    frequencies = 10000.0 ** (
        -(jnp.arange(half_rot, dtype=jnp.int32).astype(jnp.float32) * 2.0 / ROT)
    )
    angles = places[:, None] * frequencies[None, :]
    return (jnp.cos(angles)[:, None, :], jnp.sin(angles)[:, None, :])


def base_rotate(values, cosines, sines):
    half_rot = ROT // 2
    first_half = values[..., :half_rot]
    second_half = values[..., half_rot:ROT]
    return jnp.concatenate(
        [
            first_half * cosines - second_half * sines,
            second_half * cosines + first_half * sines,
            values[..., ROT:],
        ],
        axis=-1,
    )


def gelu_exact(values):
    return jax.nn.gelu(values, approximate=False)


def visible(query_seg, query_pos, key_seg, key_pos):
    causal = key_pos[None, :] <= query_pos[:, None]
    same_doc = query_seg[:, :, None] == key_seg[:, None, :]
    return (causal[None] & same_doc)[:, :, None, :]


def per_device(
    tokens,
    segments,
    ln1_gain,
    ln1_bias,
    qkv_weight,
    qkv_bias,
    out_weight,
    out_bias,
    ln2_gain,
    ln2_bias,
    fc1_weight,
    fc1_bias,
    fc2_weight,
    fc2_bias,
    cotangent,
):
    group_size, block_size, model_width = tokens.shape
    row_count = group_size * block_size
    attention_full = (
        lax.all_gather(ln1_gain, ("dp", "seq"), axis=0, tiled=True),
        lax.all_gather(ln1_bias, ("dp", "seq"), axis=0, tiled=True),
        lax.all_gather(qkv_weight, ("dp", "seq"), axis=0, tiled=True),
        lax.all_gather(qkv_bias, ("dp", "seq"), axis=0, tiled=True),
        lax.all_gather(out_weight, ("dp", "seq"), axis=0, tiled=True),
        lax.all_gather(out_bias, ("dp", "seq"), axis=0, tiled=True),
    )
    gain_one, bias_one, weight_qkv, bias_qkv, weight_out, bias_out = attention_full
    flat_in = tokens.reshape(row_count, model_width).astype(jnp.float32)
    normed_one, norm_back_one = jax.vjp(
        layer_norm, flat_in, gain_one.astype(jnp.float32), bias_one.astype(jnp.float32)
    )
    act_one = normed_one.astype(jnp.bfloat16)
    mixed_qkv = jnp.dot(act_one, weight_qkv, preferred_element_type=jnp.float32) + bias_qkv.astype(
        jnp.float32
    )
    mixed_qkv = mixed_qkv.reshape(group_size, block_size, 3, HEADS, HD)
    first_pos = lax.axis_index("seq") * block_size
    local_pos = first_pos + jnp.arange(block_size, dtype=jnp.int32)
    cosines, sines = base_tables(local_pos.astype(jnp.float32))

    def turn_all(query_raw, key_raw):
        return (base_rotate(query_raw, cosines, sines) * 0.0625, base_rotate(key_raw, cosines, sines))

    (query_turned, key_turned), turn_back = jax.vjp(
        turn_all, mixed_qkv[:, :, 0], mixed_qkv[:, :, 1]
    )
    query_low = query_turned.astype(jnp.bfloat16)
    key_low = key_turned.astype(jnp.bfloat16)
    value_low = mixed_qkv[:, :, 2].astype(jnp.bfloat16)
    start_top = jnp.full((group_size, block_size, HEADS), masked_value, jnp.float32)
    key_piece = lax.all_gather(key_low, "seq", axis=1, tiled=True)
    value_piece = lax.all_gather(value_low, "seq", axis=1, tiled=True)
    seg_piece = lax.all_gather(segments, "seq", axis=1, tiled=True)
    key_pos = jnp.arange(seg_piece.shape[1], dtype=jnp.int32)
    allowed = visible(segments, local_pos, seg_piece, key_pos)
    scores = jnp.einsum("gqhd,gkhd->gqhk", query_low, key_piece, preferred_element_type=jnp.float32)
    scores = jnp.where(allowed, scores, masked_value)
    new_top = jnp.maximum(start_top, jnp.max(scores, axis=-1))
    weights = jnp.where(allowed, jnp.exp(scores - new_top[..., None]), 0.0)
    new_total = jnp.sum(weights, axis=-1)
    new_out = jnp.einsum(
        "gqhk,gkhd->gqhd",
        weights.astype(jnp.bfloat16),
        value_piece,
        preferred_element_type=jnp.float32,
    )
    attended = new_out / new_total[..., None]
    log_total = new_top + jnp.log(new_total)
    attended_low = attended.astype(jnp.bfloat16).reshape(row_count, model_width)
    attn_out = jnp.dot(
        attended_low, weight_out, preferred_element_type=jnp.float32
    ) + bias_out.astype(jnp.float32)
    mlp_full = (
        lax.all_gather(ln2_gain, ("dp", "seq"), axis=0, tiled=True),
        lax.all_gather(ln2_bias, ("dp", "seq"), axis=0, tiled=True),
        lax.all_gather(fc1_weight, ("dp", "seq"), axis=0, tiled=True),
        lax.all_gather(fc1_bias, ("dp", "seq"), axis=0, tiled=True),
        lax.all_gather(fc2_weight, ("dp", "seq"), axis=0, tiled=True),
        lax.all_gather(fc2_bias, ("dp", "seq"), axis=0, tiled=True),
    )
    gain_two, bias_two, weight_up, bias_up, weight_down, bias_down = mlp_full
    normed_two, norm_back_two = jax.vjp(
        layer_norm, flat_in, gain_two.astype(jnp.float32), bias_two.astype(jnp.float32)
    )
    act_two = normed_two.astype(jnp.bfloat16)
    hidden = jnp.dot(act_two, weight_up, preferred_element_type=jnp.float32) + bias_up.astype(
        jnp.float32
    )
    activated, gelu_back = jax.vjp(gelu_exact, hidden)
    act_hidden = activated.astype(jnp.bfloat16)
    mlp_out = jnp.dot(
        act_hidden, weight_down, preferred_element_type=jnp.float32
    ) + bias_down.astype(jnp.float32)
    mixed = (
        (flat_in + attn_out + mlp_out)
        .astype(jnp.bfloat16)
        .reshape(group_size, block_size, model_width)
    )
    back_up, back_down = (
        lax.all_gather(fc1_weight, ("dp", "seq"), axis=0, tiled=True),
        lax.all_gather(fc2_weight, ("dp", "seq"), axis=0, tiled=True),
    )
    back_qkv, back_out = (
        lax.all_gather(qkv_weight, ("dp", "seq"), axis=0, tiled=True),
        lax.all_gather(out_weight, ("dp", "seq"), axis=0, tiled=True),
    )
    grad_out = cotangent.reshape(row_count, model_width)
    grad_float = grad_out.astype(jnp.float32)
    grad_down_weight = jnp.dot(act_hidden.T, grad_out, preferred_element_type=jnp.float32)
    grad_down_bias = jnp.sum(grad_float, axis=0)
    grad_activated = jnp.dot(grad_out, back_down.T, preferred_element_type=jnp.float32)
    (grad_hidden,) = gelu_back(grad_activated)
    grad_hidden_low = grad_hidden.astype(jnp.bfloat16)
    grad_up_weight = jnp.dot(act_two.T, grad_hidden_low, preferred_element_type=jnp.float32)
    grad_up_bias = jnp.sum(grad_hidden_low.astype(jnp.float32), axis=0)
    grad_act_two = jnp.dot(grad_hidden_low, back_up.T, preferred_element_type=jnp.float32)
    grad_in_two, grad_gain_two, grad_bias_two = norm_back_two(grad_act_two)
    mlp_shards = (
        lax.psum_scatter(grad_gain_two, ("dp", "seq"), scatter_dimension=0, tiled=True),
        lax.psum_scatter(grad_bias_two, ("dp", "seq"), scatter_dimension=0, tiled=True),
        lax.psum_scatter(grad_up_weight, ("dp", "seq"), scatter_dimension=0, tiled=True),
        lax.psum_scatter(grad_up_bias, ("dp", "seq"), scatter_dimension=0, tiled=True),
        lax.psum_scatter(grad_down_weight, ("dp", "seq"), scatter_dimension=0, tiled=True),
        lax.psum_scatter(grad_down_bias, ("dp", "seq"), scatter_dimension=0, tiled=True),
    )
    grad_out_weight = jnp.dot(attended_low.T, grad_out, preferred_element_type=jnp.float32)
    grad_out_bias = jnp.sum(grad_float, axis=0)
    grad_attended = jnp.dot(grad_out, back_out.T, preferred_element_type=jnp.float32)
    grad_low = grad_attended.reshape(group_size, block_size, HEADS, HD).astype(jnp.bfloat16)
    delta = jnp.sum(grad_low.astype(jnp.float32) * attended, axis=-1)
    key_piece = lax.all_gather(key_low, "seq", axis=1, tiled=True)
    value_piece = lax.all_gather(value_low, "seq", axis=1, tiled=True)
    seg_piece = lax.all_gather(segments, "seq", axis=1, tiled=True)
    key_pos = jnp.arange(seg_piece.shape[1], dtype=jnp.int32)
    allowed = visible(segments, local_pos, seg_piece, key_pos)
    scores = jnp.einsum("gqhd,gkhd->gqhk", query_low, key_piece, preferred_element_type=jnp.float32)
    chances = jnp.where(allowed, jnp.exp(scores - log_total[..., None]), 0.0)
    grad_chances = jnp.einsum(
        "gqhd,gkhd->gqhk", grad_low, value_piece, preferred_element_type=jnp.float32
    )
    grad_scores = (chances * (grad_chances - delta[..., None])).astype(jnp.bfloat16)
    grad_query = jnp.einsum(
        "gqhk,gkhd->gqhd", grad_scores, key_piece, preferred_element_type=jnp.float32
    )
    query_piece = lax.all_gather(query_low, "seq", axis=1, tiled=True)
    grad_piece = lax.all_gather(grad_low, "seq", axis=1, tiled=True)
    lse_piece = lax.all_gather(log_total.astype(jnp.bfloat16), "seq", axis=1, tiled=True).astype(
        jnp.float32
    )
    delta_piece = lax.all_gather(delta.astype(jnp.bfloat16), "seq", axis=1, tiled=True).astype(
        jnp.float32
    )
    seg_piece = lax.all_gather(segments, "seq", axis=1, tiled=True)
    query_pos = jnp.arange(seg_piece.shape[1], dtype=jnp.int32)
    allowed = visible(seg_piece, query_pos, segments, local_pos)
    scores = jnp.einsum("gqhd,gkhd->gqhk", query_piece, key_low, preferred_element_type=jnp.float32)
    chances = jnp.where(allowed, jnp.exp(scores - lse_piece[..., None]), 0.0)
    new_value = jnp.einsum(
        "gqhk,gqhd->gkhd",
        chances.astype(jnp.bfloat16),
        grad_piece,
        preferred_element_type=jnp.float32,
    )
    grad_chances = jnp.einsum(
        "gqhd,gkhd->gqhk", grad_piece, value_low, preferred_element_type=jnp.float32
    )
    grad_scores = (chances * (grad_chances - delta_piece[..., None])).astype(jnp.bfloat16)
    new_key = jnp.einsum(
        "gqhk,gqhd->gkhd", grad_scores, query_piece, preferred_element_type=jnp.float32
    )
    grad_query_raw, grad_key_raw = turn_back((grad_query, new_key))
    grad_qkv_low = (
        jnp.stack([grad_query_raw, grad_key_raw, new_value], axis=2)
        .reshape(row_count, 3 * model_width)
        .astype(jnp.bfloat16)
    )
    grad_qkv_weight = jnp.dot(act_one.T, grad_qkv_low, preferred_element_type=jnp.float32)
    grad_qkv_bias = jnp.sum(grad_qkv_low.astype(jnp.float32), axis=0)
    grad_act_one = jnp.dot(grad_qkv_low, back_qkv.T, preferred_element_type=jnp.float32)
    grad_in_one, grad_gain_one, grad_bias_one = norm_back_one(grad_act_one)
    attention_shards = (
        lax.psum_scatter(grad_gain_one, ("dp", "seq"), scatter_dimension=0, tiled=True),
        lax.psum_scatter(grad_bias_one, ("dp", "seq"), scatter_dimension=0, tiled=True),
        lax.psum_scatter(grad_qkv_weight, ("dp", "seq"), scatter_dimension=0, tiled=True),
        lax.psum_scatter(grad_qkv_bias, ("dp", "seq"), scatter_dimension=0, tiled=True),
        lax.psum_scatter(grad_out_weight, ("dp", "seq"), scatter_dimension=0, tiled=True),
        lax.psum_scatter(grad_out_bias, ("dp", "seq"), scatter_dimension=0, tiled=True),
    )
    grad_tokens = (
        (grad_float + grad_in_one + grad_in_two)
        .astype(jnp.bfloat16)
        .reshape(group_size, block_size, model_width)
    )
    return (
        mixed,
        grad_tokens,
        attention_shards[0],
        attention_shards[1],
        attention_shards[2],
        attention_shards[3],
        attention_shards[4],
        attention_shards[5],
        mlp_shards[0],
        mlp_shards[1],
        mlp_shards[2],
        mlp_shards[3],
        mlp_shards[4],
        mlp_shards[5],
    )


GROUP = ("z", "y")
PEERS = ("x", "c")
EVERY = ("z", "y", "x", "c")
TURNS = 2 * CORES
ORDER = (0, 1, 7, 2, 6, 3, 5, 4)
LIMIT = 56 * 1024 * 1024
SMALL = 26 * 1024 * 1024
bf16, f32 = jnp.bfloat16, jnp.float32


def whole_ref():
    return pl.BlockSpec(memory_space=pltpu.VMEM)


def in_place():
    return pl.BlockSpec(memory_space=pl.ANY)


def call(
    kernel, results, inputs, operands, outputs, grid=(), prefetch=0, aliases=None, scratch=(), limit=LIMIT
):
    return pl.pallas_call(
        kernel,
        out_shape=[jax.ShapeDtypeStruct(*result) for result in results],
        grid_spec=pltpu.PrefetchScalarGridSpec(
            num_scalar_prefetch=prefetch, grid=grid, in_specs=inputs, out_specs=outputs, scratch_shapes=scratch
        ),
        input_output_aliases=aliases or {},
        compiler_params=pltpu.CompilerParams(vmem_limit_bytes=limit),
        cost_estimate=pl.CostEstimate(flops=1, bytes_accessed=1, transcendentals=0),
    )(*operands)


class Line:
    def __init__(self):
        self.last = ()

    def __call__(self, function, *operands, wait=()):
        operands = lax.optimization_barrier((operands, self.last, wait))[0]
        results = function(*operands)
        self.last = tuple(jax.tree.leaves(results))
        return results

    def hold(self, values):
        return lax.optimization_barrier((values, self.last))[0]


def after(value, *others):
    return lax.optimization_barrier((value, *others))[0]


def ring_perm(shift):
    depth, width = lax.axis_size("z"), lax.axis_size("y")
    places = [z * width for z in range(depth)] + [z * width + 1 for z in reversed(range(depth))]
    count = len(places)
    return [(places[i], places[(i + shift) % count]) for i in range(count)]


class Gather:
    def __init__(self, block):
        self.held = {0: [block]}
        self.ahead = self.behind = block
        self.done = 0

    def step(self, line, *others):
        half = len(ORDER) // 2
        ahead, behind = line.hold((self.ahead, self.behind, *others))[:2]
        self.done += 1
        if self.done < half:
            self.behind = lax.ppermute(behind, GROUP, ring_perm(1))
            self.ahead = lax.ppermute(ahead, GROUP, ring_perm(-1))
            self.held[len(ORDER) - self.done] = [self.behind]
            self.held[self.done] = [self.ahead]
        else:
            cut = behind.shape[0] // 2
            self.held[half] = [
                lax.ppermute(behind[:cut], GROUP, ring_perm(1)),
                lax.ppermute(ahead[cut:], GROUP, ring_perm(-1)),
            ]


def swap(values, axis):
    return lax.ppermute(values, axis, [(0, 1), (1, 0)])


def dot_f32(left, right, dims=((1,), (0,))):
    return lax.dot_general(left, right, (dims, ((), ())), preferred_element_type=f32)


def tile_spec(shape, index):
    return pl.BlockSpec(shape, lambda i, *scalars: index(i))


def same(shape):
    return tile_spec(shape, lambda i: (0,) * len(shape))


def spread_kernel(up, qkv, result):
    share, _, columns = result.shape
    tile = columns - 3 * HD
    for t in range(share):
        for i in range(3):
            at = (i * share + t) * HD
            result[t, :, i * HD : (i + 1) * HD] = qkv[:, at : at + HD]
        result[t, :, 3 * HD :] = up[:, t * tile : (t + 1) * tile]


def spread(up, qkv, share):
    rows, columns = up.shape
    return call(
        spread_kernel,
        [((share, rows, 3 * HD + columns // share), bf16)],
        [whole_ref()] * 2,
        (up, qkv),
        [whole_ref()],
    )[0]


def assemble_kernel(mine, *refs):
    sources, result = refs[:TURNS], refs[TURNS]
    for entry in range(result.shape[0]):
        for turn in range(TURNS):
            result[entry, pl.ds(mine[0] ^ turn, 1)] = sources[turn][entry : entry + 1]


def assemble(pieces, mine, step=2):
    entries, rows, columns = pieces[0].shape
    step = min(step, entries)
    return call(
        assemble_kernel,
        [((entries, TURNS, rows, columns), pieces[0].dtype)],
        [tile_spec((step, rows, columns), lambda i: (i, 0, 0))] * TURNS,
        (mine, *pieces),
        [tile_spec((step, TURNS, rows, columns), lambda i: (i, 0, 0, 0))],
        grid=(entries // step,),
        prefetch=1,
    )[0].reshape(entries * TURNS * rows, columns)


def settle_kernel(depth, peer, *refs):
    sources, result = refs[:-1], refs[-1]
    share = sources[0].shape[0]
    for shift, source in enumerate(sources):
        at = ((depth[0] + len(sources) - shift) % len(sources)) * share
        for j in range(share):
            result[pl.ds(at + (j ^ peer[0]), 1)] = source[j : j + 1]


def settle(depth, peer, *sources):
    shape = (len(sources) * sources[0].shape[0], *sources[0].shape[1:])
    return call(
        settle_kernel,
        [(shape, sources[0].dtype)],
        [same(source.shape) for source in sources],
        (depth, peer, *sources),
        [same(shape)],
        grid=(1,),
        prefetch=2,
    )[0]


def norm_kernel(count, affine, *refs):
    pieces, (one, two, mean_ref, scale_ref, one_turned, two_turned) = refs[:count], refs[-6:]
    values = stacked(pieces).astype(f32)
    mean = jnp.mean(values, axis=-1, keepdims=True)
    centered = values - mean
    scale = lax.rsqrt(jnp.mean(centered * centered, axis=-1, keepdims=True) + epsilon)
    normal = centered * scale
    for at, result, turned in ((0, one, one_turned), (2, two, two_turned)):
        act = (normal * affine[at : at + 1] + affine[at + 1 : at + 2]).astype(bf16)
        result[...] = act
        turned[...] = act.T.reshape(turned.shape)
    mean_ref[...] = mean
    scale_ref[...] = scale


def norm_block(at, pieces, affine, kept, slim):
    block, model = sum(piece.shape[0] for piece in pieces), pieces[0].shape[1]
    rows = len(ORDER) * block
    turned = (model // (TURNS * slim), 2, CORES, slim)
    results = [
        ((rows, model), bf16),
        ((rows, model), bf16),
        ((rows, 1), f32),
        ((rows, 1), f32),
        ((*turned, rows), bf16),
        ((*turned, rows), bf16),
    ]
    outputs = [pl.BlockSpec((block, shape[1]), lambda i: (at, 0)) for shape, _ in results[:4]]
    outputs += [pl.BlockSpec((*turned, block), lambda i: (0, 0, 0, 0, at))] * 2
    operands = [affine, *pieces]
    inputs = [whole_ref()] * len(operands)
    aliases = {}
    if kept is not None:
        aliases = {len(operands) + i: i for i in range(len(results))}
        operands += kept
        inputs += [in_place()] * len(results)
    return call(
        functools.partial(norm_kernel, len(pieces)), results, inputs, operands, outputs, grid=(1,), aliases=aliases
    )


def rotary_tables(places):
    half_rot = ROT // 2
    frequencies = 10000.0 ** (
        -(jnp.arange(half_rot, dtype=jnp.int32).astype(f32) * 2.0 / ROT)
    )
    turned = places.astype(f32)[:, None] * frequencies[None, :]
    cosines, sines = jnp.cos(turned), jnp.sin(turned)
    rest = jnp.zeros((places.shape[0], 128 - ROT), f32)
    none = jnp.zeros_like(sines)
    return (
        jnp.concatenate([cosines, cosines, rest + 1.0], axis=1),
        jnp.concatenate([sines, none, rest], axis=1),
        jnp.concatenate([none, sines, rest], axis=1),
    )


def rotate(values, tables, sign):
    cosines, first, second = tables
    half_rot = ROT // 2
    low = values[:, :128]
    ahead = pltpu.roll(low, 128 - half_rot, 1)
    behind = pltpu.roll(low, half_rot, 1)
    low = low * cosines + sign * (behind * second - ahead * first)
    return jnp.concatenate([low, values[:, 128:]], axis=1)


def qkv_kernel(depth_of, far_of, core, act, weight, bias, cosines, first, second, *results):
    qkv = jnp.dot(act[...], weight[...], preferred_element_type=f32) + bias[...]
    tables = (cosines[...], first[...], second[...])
    query = (rotate(qkv[:, :HD], tables, 1.0) * 0.0625).astype(bf16)
    key = rotate(qkv[:, HD : 2 * HD], tables, 1.0).astype(bf16)
    value = qkv[:, 2 * HD :].astype(bf16)
    parts = act.shape[0] // results[0].shape[2]
    start = pl.program_id(0) * parts
    spill(jnp.concatenate([query, key, value], axis=1), depth_of, far_of, core, start, results)


def spill(values, depth_of, far_of, core, start, results):
    block = results[0].shape[2]
    for part in range(values.shape[0] // block):
        at = start + part
        rows = values[None, None, part * block : (part + 1) * block]
        owner, low = depth_of[at] // 2, depth_of[at] % 2
        for result, mine in zip(results, (True, False)):

            @pl.when((owner == core[0]) == mine)
            def _():
                result[pl.ds(low, 1), pl.ds(far_of[at], 1)] = rows


def project(act, weight, bias, tables, depth_of, far_of, core, block):
    rows, model = act.shape
    columns = weight.shape[1]
    step = 4 * block
    return call(
        qkv_kernel,
        [((2, 2, block, columns), bf16)] * 2,
        [tile_spec((step, model), lambda i: (i, 0)), same((model, columns)), same((1, columns))]
        + [tile_spec((step, 128), lambda i: (i, 0))] * 3,
        (depth_of, far_of, core, act, weight, bias, *tables),
        [same((2, 2, block, columns))] * 2,
        grid=(rows // step,),
        prefetch=3,
    )


def place_kernel(depth_of, far_of, core, mine, came, result, *turned):
    block = result.shape[1]
    for at in range(result.shape[0]):
        for source, own in ((mine, True), (came, False)):

            @pl.when((depth_of[at] // 2 == core[0]) == own)
            def _():
                values = source[pl.ds(depth_of[at] % 2, 1), pl.ds(far_of[at], 1)][0, 0]
                result[at] = values
                for other in turned:
                    other[:, at * block : (at + 1) * block] = values.T


def place(mine, came, depth_of, far_of, core, turn=False):
    low, far, block, columns = mine.shape
    count = 2 * low * far
    shapes = [(count, block, columns)] + [(columns, count * block)] * turn
    placed, *turned = call(
        place_kernel,
        [(shape, bf16) for shape in shapes],
        [same(mine.shape)] * 2,
        (depth_of, far_of, core, mine, came),
        [same(shape) for shape in shapes],
        grid=(1,),
        prefetch=3,
        limit=SMALL,
    )
    return (placed.reshape(count * block, columns), *turned)


def pairs(ref, rows):
    return [(far, slice(at, at + rows)) for far in range(ref.shape[1]) for at in range(0, ref.shape[2], rows)]


def gathered(mine, came, even, seq, start, rows):
    parts = []
    for far, at in pairs(mine, rows):
        own, other = (ref[seq, far, at, start : start + HD] for ref in (mine, came))
        parts += [jnp.where(even, own, other), jnp.where(even, other, own)]
    return jnp.concatenate(parts, axis=0)


def scattered(mine, sent, even, seq, start, rows, values):
    for i, (far, at) in enumerate(pairs(mine, rows)):
        first, second = (values[(2 * i + k) * rows : (2 * i + k + 1) * rows] for k in range(2))
        mine[seq, far, at, start : start + HD] = jnp.where(even, first, second)
        sent[seq, far, at, start : start + HD] = jnp.where(even, second, first)


def chances_of(query, key, segments):
    scores = dot_f32(query, key, ((1,), (1,)))
    col_seg = jnp.broadcast_to(segments, scores.shape)
    row_seg = col_seg.T
    row_pos = lax.broadcasted_iota(jnp.int32, scores.shape, 0)
    col_pos = lax.broadcasted_iota(jnp.int32, scores.shape, 1)
    scores = jnp.where((col_pos <= row_pos) & (col_seg == row_seg), scores, masked_value)
    weights = jnp.exp(scores - jnp.max(scores, axis=-1, keepdims=True))
    return weights / jnp.sum(weights, axis=-1, keepdims=True)


def forward_kernel(rows, core, segments, mine, came, kept, sent):
    even = core[0] == 0
    for seq in range(mine.shape[0]):
        query, key, value = (gathered(mine, came, even, seq, i * HD, rows) for i in range(3))
        chances = chances_of(query, key, segments[seq])
        scattered(kept, sent, even, seq, 0, rows, dot_f32(chances.astype(bf16), value).astype(bf16))


def backward_kernel(
    rows, core, segments, cosines, first, second, mine, came, grad_mine, grad_came, kept, sent
):
    even = core[0] == 0
    tables = (cosines[...], first[...], second[...])
    for seq in range(mine.shape[0]):
        query, key, value = (gathered(mine, came, even, seq, i * HD, rows) for i in range(3))
        grad = gathered(grad_mine, grad_came, even, seq, 0, rows)
        chances = chances_of(query, key, segments[seq])
        chances_low = chances.astype(bf16)
        grad_chances = dot_f32(grad, value, ((1,), (1,)))
        delta = jnp.sum(chances_low.astype(f32) * grad_chances, axis=-1, keepdims=True)
        grad_scores = (chances * (grad_chances - delta)).astype(bf16)
        grad_query = dot_f32(grad_scores, key)
        grad_key = dot_f32(grad_scores, query, ((0,), (0,)))
        grad_value = dot_f32(chances_low, grad, ((0,), (0,)))
        for i, part in enumerate(
            (rotate(grad_query * 0.0625, tables, -1.0), rotate(grad_key, tables, -1.0), grad_value)
        ):
            scattered(kept, sent, even, seq, i * HD, rows, part.astype(bf16))


def attend(kernel, rows, columns, core, given, *arrays):
    operands = (*given, *arrays)
    shape = (*arrays[0].shape[:3], columns)
    return call(
        functools.partial(kernel, rows),
        [(shape, bf16)] * 2,
        [same(a.shape) for a in operands],
        (core, *operands),
        [same(shape)] * 2,
        grid=(1,),
        prefetch=1,
        limit=SMALL,
    )


def widen_kernel(act, weight, bias, activated, slope, turned):
    hidden = jnp.dot(act[...], weight[...], preferred_element_type=f32) + bias[...]
    cdf = 0.5 * (1.0 + lax.erf(hidden * math.sqrt(0.5)))
    result = (hidden * cdf).astype(bf16)
    activated[...] = result
    turned[...] = result.T
    slope[...] = cdf + hidden * jnp.exp(-0.5 * hidden * hidden) * (1.0 / math.sqrt(2.0 * math.pi))


def widen(act, weight, bias, tile=256):
    rows, model = act.shape
    columns = weight.shape[1]
    return call(
        widen_kernel,
        [((rows, columns), bf16), ((rows, columns), f32), ((columns, rows), bf16)],
        [
            same((rows, model)),
            tile_spec((model, tile), lambda i: (0, i)),
            tile_spec((1, tile), lambda i: (0, i)),
        ],
        (act, weight, bias),
        [tile_spec((rows, tile), lambda i: (0, i))] * 2 + [tile_spec((tile, rows), lambda i: (i, 0))],
        grid=(columns // tile,),
    )


def stacked(refs):
    return jnp.concatenate([ref[...] for ref in refs], axis=0)


def narrow_kernel(weight, slope, *refs):
    blocks, (result, sums) = refs[:-2], refs[-2:]
    grad = dot_f32(stacked(blocks), weight[...], ((1,), (1,))) * slope[...]
    grad = grad.astype(bf16)
    result[...] = grad
    sums[...] = jnp.sum(grad.astype(f32), axis=0, keepdims=True)


def narrow(blocks, weight, slope, tile=256):
    rows, columns = slope.shape
    model = weight.shape[1]
    return call(
        narrow_kernel,
        [((rows, columns), bf16), ((1, columns), f32)],
        [tile_spec((tile, model), lambda i: (i, 0)), tile_spec((rows, tile), lambda i: (0, i))]
        + [same(piece.shape) for piece in blocks],
        (weight, slope, *blocks),
        [tile_spec((rows, tile), lambda i: (0, i)), tile_spec((1, tile), lambda i: (0, i))],
        grid=(columns // tile,),
        limit=SMALL,
    )


def head_kernel(depth_of, far_of, core, weight, *refs):
    blocks, results, total = refs[:-3], refs[-3:-1], refs[-1]
    part = dot_f32(stacked(blocks), weight[...], ((1,), (1,)))
    step = pl.program_id(0)

    @pl.when(step == 0)
    def _():
        total[...] = part

    @pl.when(step > 0)
    def _():
        total[...] += part

    @pl.when(step == pl.num_programs(0) - 1)
    def _():
        spill(total[...].astype(bf16), depth_of, far_of, core, 0, results)


def head_grads(blocks, weight, depth_of, far_of, core, block, tile=512):
    rows = sum(piece.shape[0] for piece in blocks)
    return call(
        head_kernel,
        [((2, 2, block, HD), bf16)] * 2,
        [tile_spec((piece.shape[0], tile), lambda i: (0, i)) for piece in (weight, *blocks)],
        (depth_of, far_of, core, weight, *blocks),
        [same((2, 2, block, HD))] * 2,
        grid=(weight.shape[1] // tile,),
        prefetch=3,
        scratch=[pltpu.VMEM((rows, HD), f32)],
        limit=SMALL,
    )


def across(total, half, near, far, slots=False):
    first, second = total[:, 0], total[:, 1]
    low = half[0] == 0
    near[...] = jnp.where(low, first, second).reshape(near.shape)
    other = jnp.where(low, second, first).astype(bf16)
    if slots:
        far[pl.ds(1 - half[0], 1)] = other[None]
    else:
        far[...] = other.reshape(far.shape)


def rows_kernel(near, slots, core, half, act, grad, *refs):
    entries, _, _, rows, tokens = act.shape
    total = dot_f32(act[...].reshape(entries * 2 * rows, tokens), grad[...])
    total = total.reshape(entries, 2, rows, grad.shape[1])
    if near:
        came, kept, sent = refs
        across(total + came[...].astype(f32), half, kept, sent, slots)
    else:
        refs[0][...] = total.astype(bf16)


def rows_grad(turned, grad, core, half, came=None, step=4, slots=False):
    entries, _, _, rows, tokens = turned.shape
    columns = grad.shape[1]
    near = came is not None
    spec = tile_spec((step, 2, rows, columns), lambda i: (i, 0, 0, 0))
    inputs = [
        pl.BlockSpec(
            (step, 2, 1, rows, tokens), lambda i, c, x: (i, 0, c[0] if near else 1 - c[0], 0, 0)
        ),
        same((tokens, columns)),
    ]
    if near:
        results = [((entries, rows, columns), f32), ((entries, rows, columns), bf16)]
        outputs = [tile_spec((step, rows, columns), lambda i: (i, 0, 0))] * 2
        if slots:
            results[1] = ((2, entries, rows, columns), bf16)
            outputs[1] = tile_spec((2, step, rows, columns), lambda i: (0, i, 0, 0))
    else:
        results, outputs = [((entries, 2, rows, columns), bf16)], [spec]
    return call(
        functools.partial(rows_kernel, near, slots),
        results,
        inputs + [spec] * near,
        (core, half, turned, grad) + (came,) * near,
        outputs,
        grid=(entries // step,),
        prefetch=2,
        limit=SMALL,
    )


def down_kernel(near, core, half, attended, activated, *refs):
    count = 3 if near else 1
    blocks, refs = refs[:-count], refs[-count:]
    parts = [ref[x, 0] for x in range(2) for ref in (attended, activated)]
    total = dot_f32(jnp.concatenate(parts, axis=0), stacked(blocks))
    total = total.reshape(1, 2, total.shape[0] // 2, total.shape[1])
    if near:
        came, kept, sent = refs
        across(total + came[...][None].astype(f32), half, kept, sent)
    else:
        refs[0][...] = total[0].astype(bf16)


def down_grad(attended, activated, blocks, core, half, came=None, tile=512):
    tokens = attended.shape[3]
    model = blocks[0].shape[1]
    rows = attended.shape[2] + activated.shape[2]
    near = came is not None
    spec = tile_spec((2, rows, tile), lambda i: (0, 0, i))
    inputs = [
        pl.BlockSpec(
            (2, 1, turned.shape[2], tokens), lambda i, c, x: (0, c[0] if near else 1 - c[0], 0, 0)
        )
        for turned in (attended, activated)
    ]
    inputs += [tile_spec((piece.shape[0], tile), lambda i: (0, i)) for piece in blocks]
    if near:
        results = [((rows, model), f32), ((rows, model), bf16)]
        outputs = [tile_spec((rows, tile), lambda i: (0, i))] * 2
    else:
        results, outputs = [((2, rows, model), bf16)], [spec]
    return call(
        functools.partial(down_kernel, near),
        results,
        inputs + [spec] * near,
        (core, half, attended, activated, *blocks) + (came,) * near,
        outputs,
        grid=(model // tile,),
        prefetch=2,
        limit=SMALL,
    )


def join_kernel(pieces, given, result, *sums):
    share = given.shape[0]
    width = result.shape[1] // (share * pieces)
    for t in range(share):
        for i in range(pieces):
            at = (i * share + t) * width
            result[:, at : at + width] = given[t, :, i * width : (i + 1) * width].astype(f32)
    for ref in sums:
        rows, columns = ref.shape
        ref[...] = jnp.sum(given[:, :rows, pieces * width : pieces * width + columns].astype(f32), axis=0)


def join(given, pieces, extra=None):
    share, rows, columns = given.shape
    results = [((rows, share * (columns - (extra[1] if extra else 0))), f32)]
    results += [(extra, f32)] if extra else []
    return call(
        functools.partial(join_kernel, pieces), results, [whole_ref()], (given,), [whole_ref()] * len(results), limit=SMALL)


def widen_rows_kernel(mine, came, extra, result):
    columns = mine.shape[2]
    result[:, :, :columns] = (mine[...] + came[...].astype(f32)).astype(bf16)
    result[:, :, columns:] = jnp.zeros((*result.shape[:2], result.shape[2] - columns), bf16)
    result[:, : extra.shape[1], columns:] = extra[...].astype(bf16)


def total_with(mine, came, extra):
    shape = (*mine.shape[:2], mine.shape[2] + extra.shape[2])
    operands = (mine, came, extra)
    return call(widen_rows_kernel, [(shape, bf16)], [whole_ref()] * 3, operands, [whole_ref()], limit=SMALL)[0]


def share_part(pull, first, count, block, lefts, rights, pieces, extras=(), tile=512):
    model = rights[0].shape[0 if pull else 1]
    depths = [right.shape[1 if pull else 0] for right in rights]
    operands, inputs = [], []
    for left, depth in zip(lefts, depths):
        for b in range(count):
            operands.append(left)
            inputs.append(tile_spec((block, depth), lambda i, b=b: (first + b, 0)))
    for right, depth in zip(rights, depths):
        operands.append(right)
        inputs.append(
            tile_spec((tile, depth), lambda i: (i, 0)) if pull else tile_spec((depth, tile), lambda i: (0, i))
        )
    given = 0
    if pull:
        gains, values, mean, scale = extras
        given = len(values)
        for row in (*gains, *values):
            operands.append(row)
            inputs.append(tile_spec((row.shape[0], tile), lambda i: (0, i)))
        for stat in (mean, scale):
            for b in range(count):
                operands.append(stat)
                inputs.append(tile_spec((block, 1), lambda i, b=b: (first + b, 0)))

    def kernel(*refs):
        refs = list(refs)

        def take(number):
            taken = refs[:number]
            del refs[:number]
            return taken

        left_a, left_b = stacked(take(count)), stacked(take(count))
        (right_a,), (right_b,) = take(1), take(1)
        dims = ((1,), (1,)) if pull else ((1,), (0,))
        part_a = dot_f32(left_a, right_a[...], dims)
        part_b = dot_f32(left_b, right_b[...], dims)
        if pull:
            (gains_ref,) = take(1)
            tokens = stacked(take(given)).astype(f32)
            normal = (tokens - stacked(take(count))) * stacked(take(count))
            (sums,) = take(1)
            sums[...] = jnp.concatenate(
                [
                    jnp.sum(part, axis=0, keepdims=True)
                    for part in (part_a * normal, part_a, part_b * normal, part_b)
                ]
                + [jnp.zeros((4, tile), f32)],
                axis=0,
            )
            total = part_a * gains_ref[0:1] + part_b * gains_ref[2:3]
        else:
            total = part_a + part_b
        for (start, rows, dtype), result in zip(pieces, refs):
            result[...] = total[start : start + rows].astype(dtype)

    results = [((rows, model), dtype) for _, rows, dtype in pieces]
    outputs = [tile_spec((rows, tile), lambda i: (0, i)) for _, rows, _ in pieces]
    if pull:
        results = [((8, model), f32)] + results
        outputs = [tile_spec((8, tile), lambda i: (0, i))] + outputs
    return call(
        kernel, results, inputs, operands, outputs, grid=(model // tile,), limit=LIMIT if pull else SMALL
    )


def early_pieces(block):
    cut = block // 2
    return [(2 * block, cut, bf16), (2 * block + cut, cut, bf16), (0, block, bf16), (block, block, bf16)]


def late_pieces(block):
    return [(0, block, f32)] + [(i * block, block, bf16) for i in range(1, 5)]


def all_pieces(block):
    return late_pieces(block) + [(5 * block + start, rows, dtype) for start, rows, dtype in early_pieces(block)]


def add_kernel(one, two, ahead, behind, *results):
    cut = ahead.shape[0]
    rows = one.shape[0]
    for mine, came, result, start in ((one, ahead, results[0], 0), (two, behind, results[1], rows - cut)):
        if cut < rows:
            result[...] = mine[...]
        at = slice(start, start + cut)
        result[at] = (mine[at].astype(f32) + came[...].astype(f32)).astype(bf16)


def add_incoming(one, two, ahead, behind, tile=1024):
    rows, model = one.shape
    return call(
        add_kernel,
        [(one.shape, bf16)] * 2,
        [tile_spec((a.shape[0], tile), lambda i: (0, i)) for a in (one, two, ahead, behind)],
        (one, two, ahead, behind),
        [tile_spec((rows, tile), lambda i: (0, i))] * 2,
        grid=(model // tile,), limit=SMALL)


class Scatter:
    def send(self, one, two):
        self.ahead = lax.ppermute(one, GROUP, ring_perm(1))
        self.behind = lax.ppermute(two, GROUP, ring_perm(-1))

    def step(self, line, one, two, wait=()):
        self.send(*line(add_incoming, one, two, self.ahead, self.behind, wait=wait))


def total_slot_kernel(half, mine, came, result):
    result[...] = (mine[...] + came[...].reshape(mine.shape).astype(f32)).astype(bf16)


def total_slot(half, mine, came, step=2):
    entries, rows, columns = mine.shape
    block = (entries // step, rows, columns)
    return call(
        total_slot_kernel,
        [(mine.shape, bf16)],
        [
            tile_spec(block, lambda i: (i, 0, 0)),
            pl.BlockSpec((1, *block), lambda i, x: (1 - x[0], i, 0, 0)),
        ],
        (half, mine, came),
        [tile_spec(block, lambda i: (i, 0, 0))],
        grid=(step,),
        prefetch=1, limit=SMALL)[0]


def total_kernel(mine, came, *results):
    total = mine[...] + came[...].astype(f32)
    at = 0
    for result in results:
        rows = result.shape[0]
        result[...] = total[at : at + rows].astype(result.dtype)
        at += rows


def total_rows(mine, came, pieces):
    tail = mine.shape[1:]
    steps = 2
    tile = tail[:-1] + (tail[-1] // steps,)

    def spec(rows):
        return tile_spec((rows, *tile), lambda i: (0,) * len(tile) + (i,))

    return call(
        total_kernel,
        [((rows, *tail), dtype) for rows, dtype in pieces],
        [spec(mine.shape[0])] * 2,
        (mine, came),
        [spec(rows) for rows, _ in pieces],
        grid=(steps,), limit=SMALL)


def apart(values, half, kept, sent):
    cut = values.shape[0] // 2
    low = half[0] == 0
    first, second = values[:cut], values[cut:]
    kept[...] = jnp.where(low, first, second).astype(kept.dtype)
    sent[...] = jnp.where(low, second, first).astype(sent.dtype)


def mixed_kernel(half, own, ahead, behind, tokens, bias_one, bias_two, kept, sent):
    total = own[...] + ahead[...].astype(f32) + behind[...].astype(f32) + tokens[...].astype(f32)
    apart(total + bias_one[...] + bias_two[...], half, kept, sent)


def by_rows(kernel, half, operands, tokens):
    rows, model = tokens.shape
    return call(
        kernel,
        [((rows // 2, model), bf16)] * 2,
        [tile_spec((rows, 1), lambda i: (0, 0)) if a.shape[1] == 1 else same(a.shape) for a in operands],
        (half, *operands),
        [same((rows // 2, model))] * 2,
        grid=(1,),
        prefetch=1, limit=SMALL)


def mixed_rows(half, *operands):
    return by_rows(mixed_kernel, half, operands, operands[3])


def vectors_kernel(share, norms, grad, grad_qkv, up_sum, result):
    result[...] = jnp.zeros_like(result)
    result[:4] = norms[:4]
    result[4:5] = jnp.sum(grad[...].astype(f32), axis=0, keepdims=True)
    qkv_sum = jnp.sum(grad_qkv[...].astype(f32), axis=0, keepdims=True)
    for i in range(3):
        at = pl.multiple_of(share[0] * HD, HD)
        result[5 + i : 6 + i, pl.ds(at, HD)] = qkv_sum[:, i * HD : (i + 1) * HD]
    columns = up_sum.shape[1]
    each = result.shape[1] // columns
    at = pl.multiple_of((share[0] % each) * columns, columns)
    result[pl.ds(8 + share[0] // each, 1), pl.ds(at, columns)] = up_sum[...]


def vectors(share, norms, grad, grad_qkv, up_sum):
    operands = (norms, grad, grad_qkv, up_sum)
    return call(
        vectors_kernel,
        [((16, norms.shape[1]), f32)],
        [same(a.shape) for a in operands],
        (share, *operands),
        [same((16, norms.shape[1]))],
        grid=(1,),
        prefetch=1, limit=SMALL)[0]


def sum_kernel(*refs):
    total = refs[0][...]
    for ref in refs[1:-1]:
        total = total + ref[...]
    refs[-1][...] = total


def sum_arrays(*arrays):
    return call(
        sum_kernel, [(arrays[0].shape, f32)], [whole_ref()] * len(arrays), arrays, [whole_ref()], limit=SMALL)[0]


def finish_kernel(half, own, ahead, behind, tokens, grad, mean, scale, kept, sent):
    pulled = own[...] + ahead[...].astype(f32) + behind[...].astype(f32)
    normal = (tokens[...].astype(f32) - mean[...]) * scale[...]
    inner = (
        pulled
        - jnp.mean(pulled, axis=-1, keepdims=True)
        - normal * jnp.mean(pulled * normal, axis=-1, keepdims=True)
    )
    apart(grad[...].astype(f32) + scale[...] * inner, half, kept, sent)


def finish(half, *operands):
    return by_rows(finish_kernel, half, operands, operands[3])


def trade_kernel(half, *refs):
    count = len(refs) // 3
    low = half[0] == 0
    for values, came, result in zip(refs[:count], refs[count : 2 * count], refs[2 * count :]):
        rows = came.shape[0]
        own = values[pl.ds(half[0], 1)][0]
        result[:rows] = jnp.where(low, own, came[...])
        result[rows:] = jnp.where(low, came[...], own)


def trade(half, arrays, came):
    shapes = [(2 * piece.shape[0], piece.shape[1]) for piece in came]
    return call(
        trade_kernel,
        [(shape, bf16) for shape in shapes],
        [same(a.shape) for a in (*arrays, *came)],
        (half, *arrays, *came),
        [same(shape) for shape in shapes],
        grid=(1,),
        prefetch=1,
    )


def in_order_kernel(half, *refs):
    count = len(refs) // 3
    for own, came, result in zip(refs[:count], refs[count : 2 * count], refs[2 * count :]):
        low = half[0] == 0
        result[0] = jnp.where(low, own[...], came[...])
        result[1] = jnp.where(low, came[...], own[...])


def in_order(half, own, came):
    operands = (*own, *came)
    return call(
        in_order_kernel,
        [((2, *a.shape), a.dtype) for a in own],
        [same(a.shape) for a in operands],
        (half, *operands),
        [same((2, *a.shape)) for a in own],
        grid=(1,),
        prefetch=1, limit=SMALL)


def scalar(value):
    return jnp.reshape(value, (1,)).astype(jnp.int32)


def grouped(
    tokens,
    segments,
    ln1_gain,
    ln1_bias,
    qkv_weight,
    qkv_bias,
    out_weight,
    out_bias,
    ln2_gain,
    ln2_bias,
    fc1_weight,
    fc1_bias,
    fc2_weight,
    fc2_bias,
    cotangent,
):
    depth, width = lax.axis_size("z"), lax.axis_size("y")
    share = depth * width
    devices = share * TURNS
    z, y, x, c = (lax.axis_index(name) for name in EVERY)
    t = z * width + y
    mine = x * CORES + c
    r = jnp.where(y == 0, z, 2 * depth - 1 - z)
    seqs, rows, model = tokens.shape
    block = seqs * rows
    slim = ln1_gain.shape[0]
    hidden = fc2_weight.shape[0] * TURNS
    line = Line()

    sent = line(lambda up, qkv: spread(up, qkv, share), fc1_weight, qkv_weight)
    columns = lax.all_to_all(sent, GROUP, 0, 0, tiled=True)

    down_out = (out_weight[None], fc2_weight[None])
    down_out_near = [swap(piece, "c") for piece in line.hold(down_out)]
    came = [
        swap(lax.dynamic_index_in_dim(rows_of, 1 - x, 0, keepdims=False), "x")
        for rows_of in line.hold((tokens, cotangent))
    ]

    pieces = (
        ln1_gain,
        ln1_bias,
        ln2_gain,
        ln2_bias,
        out_bias,
        fc2_bias,
        qkv_bias,
        fc1_bias,
        segments.reshape(-1).astype(bf16),
    )
    ends = [0]
    for piece in pieces:
        ends.append(ends[-1] + piece.shape[0])
    packed = jnp.concatenate(line.hold(pieces))
    packed = jnp.pad(packed, (0, -ends[-1] % 1024)).reshape(1, -1, 128)
    for axis in ("c", "x", "y"):
        packed = jnp.concatenate([packed, swap(packed, axis)], axis=0)
    packed = [packed] + [
        lax.ppermute(packed, "z", [(i, (i + shift) % depth) for i in range(depth)]) for shift in range(1, depth)
    ]
    steps = (r + jnp.array(ORDER, jnp.int32)) % share
    far_of = (steps >= depth).astype(jnp.int32)
    depth_of = jnp.where(far_of == 1, 2 * depth - 1 - steps, steps)
    within = (jnp.arange(2, dtype=jnp.int32) * CORES + c)[:, None] * rows + jnp.arange(rows, dtype=jnp.int32)
    token_pos = far_of[:, None] * (TURNS * rows) + within.reshape(1, -1)
    token_tables = line(rotary_tables, token_pos.reshape(-1))
    seq_tables = line(rotary_tables, jnp.arange(rows * width * TURNS, dtype=jnp.int32))

    my_rows, my_grad = line(trade, scalar(x), (tokens, cotangent), came, wait=packed[0])
    down_out_far = [swap(piece, "x") for piece in line.hold(down_out)]
    packed = line(settle, scalar(z), scalar(y * TURNS + mine), *packed, wait=down_out_near).reshape(devices, -1)
    down_out_last = [swap(piece, "c") for piece in line.hold(down_out_far)]
    in_ring = Gather(my_rows)
    in_ring.step(line, columns, *down_out_last)
    small = [
        packed[:, ends[i] : ends[i + 1]].astype(f32).reshape(1, -1) for i in range(4, len(pieces) - 1)
    ]
    bias_out, bias_down, bias_qkv, bias_up = small
    affine = packed[:, : ends[4]].astype(f32).reshape(devices, 4, slim).transpose(1, 0, 2).reshape(4, model)
    bias_up = lax.dynamic_slice_in_dim(bias_up, t * hidden, hidden, 1)
    bias_qkv = lax.dynamic_index_in_dim(
        bias_qkv.reshape(3, HEADS, HD), t, 1, keepdims=False
    ).reshape(1, 3 * HD)

    all_seg = packed[:, ends[-2] : ends[-1]].reshape(depth, width * TURNS, seqs, rows)
    seq_seg = lax.dynamic_slice_in_dim(all_seg, c * 2, 2, 0)
    seq_seg = lax.dynamic_index_in_dim(seq_seg, x, 2, keepdims=False).reshape(2, -1).astype(f32)
    masks = (seq_seg[:, None, :],)

    def norm(at, kept):
        pieces = in_ring.held[ORDER[at]]
        return line(lambda *given: norm_block(at, *given, slim), pieces, affine, kept)

    kept = norm(0, None)
    qkv_cols, up_cols = after((columns[:, :, : 3 * HD], columns[:, :, 3 * HD :]), columns)
    qkv_far, up_far = swap(qkv_cols, "x"), swap(up_cols, "x")
    qkv_near, up_near = swap(qkv_cols, "c"), swap(up_cols, "c")
    weight_out, weight_down = (
        line(assemble, pieces, scalar(mine))
        for pieces in zip(down_out, down_out_near, down_out_far, down_out_last)
    )
    in_ring.step(line)
    kept = norm(1, kept)
    kept = norm(2, kept)
    in_ring.step(line)
    qkv_last = swap(line.hold(qkv_far), "c")
    kept = norm(3, kept)
    kept = norm(4, kept)
    weight_qkv = line(assemble, (qkv_cols, qkv_near, qkv_far, qkv_last), scalar(mine))
    in_ring.step(line)
    kept = norm(5, kept)
    kept = norm(6, kept)
    grad_ring = Gather(my_grad)
    grad_ring.step(line, *in_ring.held[4])
    up_last = swap(line.hold(up_far), "c")
    act_one, act_two, means, scales, turned_one, turned_two = norm(7, kept)

    lie = (depth_of, far_of, scalar(c))
    qkv_mine, sent = line(
        lambda *given: project(*given, block), act_one, weight_qkv, bias_qkv, token_tables, *lie
    )
    grad_ring.step(line)
    qkv_came = swap(sent, "c")
    weight_up = line(assemble, (up_cols, up_near, up_far, up_last), scalar(mine))
    out_mine, sent = line(
        lambda *given: attend(forward_kernel, rows, HD, *given), scalar(c), masks, qkv_mine, qkv_came
    )
    out_came = swap(sent, "c")
    grad_ring.step(line)
    act_hidden, slope, hidden_turned = line(widen, act_two, weight_up, bias_up)
    grad_ring.step(line)
    attended, attended_turned = line(lambda *given: place(*given, turn=True), out_mine, out_came, *lie)

    out_own, *out_late = line(
        lambda a, b: share_part(False, 0, len(ORDER), block, a, b, all_pieces(block)),
        (attended, act_hidden),
        (weight_out, weight_down),
    )
    out_late, (one, two, *out_early) = out_late[:4], out_late[4:]
    out_ring = Scatter()

    grads = [piece for j in ORDER for piece in grad_ring.held[j]]
    grad_mine, sent = line(lambda *given: head_grads(*given, block), grads, weight_out, *lie)
    grad_came = swap(sent, "c")
    out_ring.send(*line.hold((one, two)))
    grad_hidden, up_sum = line(narrow, grads, weight_down, slope)
    which = (scalar(c), scalar(x))
    (up_far,) = line(rows_grad, turned_two, grad_hidden, *which)
    back_mine, sent = line(
        lambda *given: attend(backward_kernel, rows, 3 * HD, *given),
        scalar(c),
        (*masks, *seq_tables),
        qkv_mine,
        qkv_came,
        grad_mine,
        grad_came,
        wait=(out_ring.ahead, out_ring.behind),
    )
    back_came = swap(sent, "c")
    out_ring.step(line, *out_early)
    up_came = swap(line.hold(up_far), "c")
    down_lefts = (
        attended_turned.reshape(2, CORES, slim, -1),
        hidden_turned.reshape(2, CORES, hidden // TURNS, -1),
    )
    (down_far,) = line(down_grad, *down_lefts, grads, *which)
    (grad_qkv,) = line(place, back_mine, back_came, *lie)
    (qkv_far,) = line(rows_grad, turned_one, grad_qkv, *which)
    grad_up, up_far = line(
        lambda *given: rows_grad(*given, slots=True), turned_two, grad_hidden, *which, up_came
    )
    out_ring.step(line, out_late[2], out_late[3])
    qkv_came = swap(line.hold(qkv_far), "c")
    up_came = lax.all_to_all(line.hold(up_far), "x", 0, 0, tiled=True)

    lefts, rights = (grad_qkv, grad_hidden), (weight_qkv, weight_up)

    def pull(left, right, more):
        return share_part(True, 0, len(ORDER), block, left, right, all_pieces(block), more)

    values = [piece for j in ORDER for piece in in_ring.held[j]]
    norm_sums, pull_own, *late = line(
        pull, lefts, rights, ((affine,), values, means, scales)
    )
    late, (one, two, *early) = late[:4], late[4:]
    pull_ring = Scatter()
    pull_ring.send(one, two)
    out_ring.step(line, out_late[0], out_late[1])
    sums = line(vectors, scalar(t), norm_sums, my_grad, grad_qkv, up_sum)
    grad_qkv_w, qkv_far = line(rows_grad, turned_one, grad_qkv, *which, qkv_came)
    grad_up = line(total_slot, scalar(x), grad_up, up_came)
    pull_ring.step(line, *early, wait=(out_ring.ahead, out_ring.behind))
    grad_up = lax.all_to_all(line.hold(grad_up), GROUP, 0, 0, tiled=True)
    qkv_came, down_came = swap(line.hold(qkv_far), "x"), swap(line.hold(down_far), "c")
    sums_came = swap(line.hold(sums), "c")
    sums = line(sum_arrays, sums, sums_came)
    grad_down, down_far = line(down_grad, *down_lefts, grads, *which, down_came)
    pull_ring.step(line, late[2], late[3])
    sums_came = swap(line.hold(sums), "x")
    sums = line(sum_arrays, sums, sums_came)

    def slices(values, rows):
        cut = values.reshape(rows, share, TURNS, -1)
        return lax.dynamic_index_in_dim(cut, mine, 2, keepdims=False).transpose(1, 0, 2).reshape(share, -1)

    sums = jnp.concatenate([slices(sums[:5], 5), slices(sums[5:8], 1), slices(sums[8:12], 1)], axis=1)
    sums = jnp.pad(sums.reshape(share, -1, 128), ((0, 0), (0, 2), (0, 0)))
    grad_qkv_w = line(total_with, grad_qkv_w, qkv_came, sums)
    pull_ring.step(line, late[0], late[1])
    grad_qkv_w = lax.all_to_all(line.hold(grad_qkv_w), GROUP, 0, 0, tiled=True)
    down_came = swap(line.hold(down_far), "x")
    (grad_up,) = line(lambda given: join(given, 1), grad_up)
    kept_out, sent_out = line(
        mixed_rows, scalar(x), out_own, out_ring.ahead, out_ring.behind, my_rows, bias_out, bias_down
    )
    kept_in, sent_in = line(
        finish, scalar(x), pull_own, pull_ring.ahead, pull_ring.behind, my_rows, my_grad, means, scales
    )
    grad_out, grad_down = line(
        lambda a, b: total_rows(a, b, [(slim, f32), (hidden // TURNS, f32)]), grad_down, down_came
    )
    grad_qkv_w, sums = line(lambda given: join(given, 3, (8, 128)), grad_qkv_w)
    came_in, came_out = (swap(sent, "x") for sent in line.hold((sent_in, sent_out)))
    mixed, grad_in = line(in_order, scalar(x), (kept_out, kept_in), (came_out, came_in))

    sums = sums.reshape(-1)
    norm_sums = [sums[i * slim : (i + 1) * slim] for i in range(5)]
    qkv_end = 5 * slim + qkv_bias.shape[0]
    return (
        mixed,
        grad_in,
        norm_sums[0],
        norm_sums[1],
        grad_qkv_w,
        sums[5 * slim : qkv_end],
        grad_out,
        norm_sums[4],
        norm_sums[2],
        norm_sums[3],
        grad_up,
        sums[qkv_end : qkv_end + fc1_bias.shape[0]],
        grad_down,
        norm_sums[4],
    )


def specs(batch, block):
    every = batch + block
    one, two, three = P(every), P(every, None), P(batch, block, None)
    arguments = (three, P(batch, block), one, one, two, one, two, one, one, one, two, one, two, one, three)
    results = (three, three, one, one, two, one, two, one, one, one, two, one, two, one)
    return arguments, results


def solution(mesh):
    depth, ring = mesh.shape["dp"], mesh.shape["seq"]
    width = ring // TURNS
    if width == 2 and depth == TURNS and depth * width == HEADS:
        chips = Mesh(mesh.devices.reshape(depth, width, 2, CORES), EVERY)
        arguments, results = specs(("z",), ("y", "x", "c"))
        return jax.shard_map(
            grouped, mesh=chips, in_specs=arguments, out_specs=results, check_vma=False
        )
    arguments, results = specs(("dp",), ("seq",))
    return jax.shard_map(
        per_device, mesh=mesh, in_specs=arguments, out_specs=results, check_vma=False
    )
```

```python
import functools
import math

import jax
import jax.numpy as jnp
from jax import lax
from jax.experimental import pallas as pl
from jax.experimental.pallas import tpu as pltpu
from jax.sharding import Mesh, PartitionSpec as P

HEADS = 8
HD = 256
ROT = 64
CORES = 2


epsilon = 1e-05
masked_value = -1e30


def layer_norm(values, gain, shift):
    average = jnp.mean(values, axis=-1, keepdims=True)
    centered = values - average
    variance = jnp.mean(centered * centered, axis=-1, keepdims=True)
    return centered * lax.rsqrt(variance + epsilon) * gain + shift


def base_tables(places):
    half_rot = ROT // 2
    frequencies = 10000.0 ** (
        -(jnp.arange(half_rot, dtype=jnp.int32).astype(jnp.float32) * 2.0 / ROT)
    )
    angles = places[:, None] * frequencies[None, :]
    return (jnp.cos(angles)[:, None, :], jnp.sin(angles)[:, None, :])


def base_rotate(values, cosines, sines):
    half_rot = ROT // 2
    first_half = values[..., :half_rot]
    second_half = values[..., half_rot:ROT]
    return jnp.concatenate(
        [
            first_half * cosines - second_half * sines,
            second_half * cosines + first_half * sines,
            values[..., ROT:],
        ],
        axis=-1,
    )


def gelu_exact(values):
    return jax.nn.gelu(values, approximate=False)


def visible(query_seg, query_pos, key_seg, key_pos):
    causal = key_pos[None, :] <= query_pos[:, None]
    same_doc = query_seg[:, :, None] == key_seg[:, None, :]
    return (causal[None] & same_doc)[:, :, None, :]


def per_device(
    tokens,
    segments,
    ln1_gain,
    ln1_bias,
    qkv_weight,
    qkv_bias,
    out_weight,
    out_bias,
    ln2_gain,
    ln2_bias,
    fc1_weight,
    fc1_bias,
    fc2_weight,
    fc2_bias,
    cotangent,
):
    group_size, block_size, model_width = tokens.shape
    row_count = group_size * block_size
    attention_full = (
        lax.all_gather(ln1_gain, ("dp", "seq"), axis=0, tiled=True),
        lax.all_gather(ln1_bias, ("dp", "seq"), axis=0, tiled=True),
        lax.all_gather(qkv_weight, ("dp", "seq"), axis=0, tiled=True),
        lax.all_gather(qkv_bias, ("dp", "seq"), axis=0, tiled=True),
        lax.all_gather(out_weight, ("dp", "seq"), axis=0, tiled=True),
        lax.all_gather(out_bias, ("dp", "seq"), axis=0, tiled=True),
    )
    gain_one, bias_one, weight_qkv, bias_qkv, weight_out, bias_out = attention_full
    flat_in = tokens.reshape(row_count, model_width).astype(jnp.float32)
    normed_one, norm_back_one = jax.vjp(
        layer_norm, flat_in, gain_one.astype(jnp.float32), bias_one.astype(jnp.float32)
    )
    act_one = normed_one.astype(jnp.bfloat16)
    mixed_qkv = jnp.dot(act_one, weight_qkv, preferred_element_type=jnp.float32) + bias_qkv.astype(
        jnp.float32
    )
    mixed_qkv = mixed_qkv.reshape(group_size, block_size, 3, HEADS, HD)
    first_pos = lax.axis_index("seq") * block_size
    local_pos = first_pos + jnp.arange(block_size, dtype=jnp.int32)
    cosines, sines = base_tables(local_pos.astype(jnp.float32))

    def turn_all(query_raw, key_raw):
        return (base_rotate(query_raw, cosines, sines) * 0.0625, base_rotate(key_raw, cosines, sines))

    (query_turned, key_turned), turn_back = jax.vjp(
        turn_all, mixed_qkv[:, :, 0], mixed_qkv[:, :, 1]
    )
    query_low = query_turned.astype(jnp.bfloat16)
    key_low = key_turned.astype(jnp.bfloat16)
    value_low = mixed_qkv[:, :, 2].astype(jnp.bfloat16)
    start_top = jnp.full((group_size, block_size, HEADS), masked_value, jnp.float32)
    key_piece = lax.all_gather(key_low, "seq", axis=1, tiled=True)
    value_piece = lax.all_gather(value_low, "seq", axis=1, tiled=True)
    seg_piece = lax.all_gather(segments, "seq", axis=1, tiled=True)
    key_pos = jnp.arange(seg_piece.shape[1], dtype=jnp.int32)
    allowed = visible(segments, local_pos, seg_piece, key_pos)
    scores = jnp.einsum("gqhd,gkhd->gqhk", query_low, key_piece, preferred_element_type=jnp.float32)
    scores = jnp.where(allowed, scores, masked_value)
    new_top = jnp.maximum(start_top, jnp.max(scores, axis=-1))
    weights = jnp.where(allowed, jnp.exp(scores - new_top[..., None]), 0.0)
    new_total = jnp.sum(weights, axis=-1)
    new_out = jnp.einsum(
        "gqhk,gkhd->gqhd",
        weights.astype(jnp.bfloat16),
        value_piece,
        preferred_element_type=jnp.float32,
    )
    attended = new_out / new_total[..., None]
    log_total = new_top + jnp.log(new_total)
    attended_low = attended.astype(jnp.bfloat16).reshape(row_count, model_width)
    attn_out = jnp.dot(
        attended_low, weight_out, preferred_element_type=jnp.float32
    ) + bias_out.astype(jnp.float32)
    mlp_full = (
        lax.all_gather(ln2_gain, ("dp", "seq"), axis=0, tiled=True),
        lax.all_gather(ln2_bias, ("dp", "seq"), axis=0, tiled=True),
        lax.all_gather(fc1_weight, ("dp", "seq"), axis=0, tiled=True),
        lax.all_gather(fc1_bias, ("dp", "seq"), axis=0, tiled=True),
        lax.all_gather(fc2_weight, ("dp", "seq"), axis=0, tiled=True),
        lax.all_gather(fc2_bias, ("dp", "seq"), axis=0, tiled=True),
    )
    gain_two, bias_two, weight_up, bias_up, weight_down, bias_down = mlp_full
    normed_two, norm_back_two = jax.vjp(
        layer_norm, flat_in, gain_two.astype(jnp.float32), bias_two.astype(jnp.float32)
    )
    act_two = normed_two.astype(jnp.bfloat16)
    hidden = jnp.dot(act_two, weight_up, preferred_element_type=jnp.float32) + bias_up.astype(
        jnp.float32
    )
    activated, gelu_back = jax.vjp(gelu_exact, hidden)
    act_hidden = activated.astype(jnp.bfloat16)
    mlp_out = jnp.dot(
        act_hidden, weight_down, preferred_element_type=jnp.float32
    ) + bias_down.astype(jnp.float32)
    mixed = (
        (flat_in + attn_out + mlp_out)
        .astype(jnp.bfloat16)
        .reshape(group_size, block_size, model_width)
    )
    back_up, back_down = (
        lax.all_gather(fc1_weight, ("dp", "seq"), axis=0, tiled=True),
        lax.all_gather(fc2_weight, ("dp", "seq"), axis=0, tiled=True),
    )
    back_qkv, back_out = (
        lax.all_gather(qkv_weight, ("dp", "seq"), axis=0, tiled=True),
        lax.all_gather(out_weight, ("dp", "seq"), axis=0, tiled=True),
    )
    grad_out = cotangent.reshape(row_count, model_width)
    grad_float = grad_out.astype(jnp.float32)
    grad_down_weight = jnp.dot(act_hidden.T, grad_out, preferred_element_type=jnp.float32)
    grad_down_bias = jnp.sum(grad_float, axis=0)
    grad_activated = jnp.dot(grad_out, back_down.T, preferred_element_type=jnp.float32)
    (grad_hidden,) = gelu_back(grad_activated)
    grad_hidden_low = grad_hidden.astype(jnp.bfloat16)
    grad_up_weight = jnp.dot(act_two.T, grad_hidden_low, preferred_element_type=jnp.float32)
    grad_up_bias = jnp.sum(grad_hidden_low.astype(jnp.float32), axis=0)
    grad_act_two = jnp.dot(grad_hidden_low, back_up.T, preferred_element_type=jnp.float32)
    grad_in_two, grad_gain_two, grad_bias_two = norm_back_two(grad_act_two)
    mlp_shards = (
        lax.psum_scatter(grad_gain_two, ("dp", "seq"), scatter_dimension=0, tiled=True),
        lax.psum_scatter(grad_bias_two, ("dp", "seq"), scatter_dimension=0, tiled=True),
        lax.psum_scatter(grad_up_weight, ("dp", "seq"), scatter_dimension=0, tiled=True),
        lax.psum_scatter(grad_up_bias, ("dp", "seq"), scatter_dimension=0, tiled=True),
        lax.psum_scatter(grad_down_weight, ("dp", "seq"), scatter_dimension=0, tiled=True),
        lax.psum_scatter(grad_down_bias, ("dp", "seq"), scatter_dimension=0, tiled=True),
    )
    grad_out_weight = jnp.dot(attended_low.T, grad_out, preferred_element_type=jnp.float32)
    grad_out_bias = jnp.sum(grad_float, axis=0)
    grad_attended = jnp.dot(grad_out, back_out.T, preferred_element_type=jnp.float32)
    grad_low = grad_attended.reshape(group_size, block_size, HEADS, HD).astype(jnp.bfloat16)
    delta = jnp.sum(grad_low.astype(jnp.float32) * attended, axis=-1)
    key_piece = lax.all_gather(key_low, "seq", axis=1, tiled=True)
    value_piece = lax.all_gather(value_low, "seq", axis=1, tiled=True)
    seg_piece = lax.all_gather(segments, "seq", axis=1, tiled=True)
    key_pos = jnp.arange(seg_piece.shape[1], dtype=jnp.int32)
    allowed = visible(segments, local_pos, seg_piece, key_pos)
    scores = jnp.einsum("gqhd,gkhd->gqhk", query_low, key_piece, preferred_element_type=jnp.float32)
    chances = jnp.where(allowed, jnp.exp(scores - log_total[..., None]), 0.0)
    grad_chances = jnp.einsum(
        "gqhd,gkhd->gqhk", grad_low, value_piece, preferred_element_type=jnp.float32
    )
    grad_scores = (chances * (grad_chances - delta[..., None])).astype(jnp.bfloat16)
    grad_query = jnp.einsum(
        "gqhk,gkhd->gqhd", grad_scores, key_piece, preferred_element_type=jnp.float32
    )
    query_piece = lax.all_gather(query_low, "seq", axis=1, tiled=True)
    grad_piece = lax.all_gather(grad_low, "seq", axis=1, tiled=True)
    lse_piece = lax.all_gather(log_total.astype(jnp.bfloat16), "seq", axis=1, tiled=True).astype(
        jnp.float32
    )
    delta_piece = lax.all_gather(delta.astype(jnp.bfloat16), "seq", axis=1, tiled=True).astype(
        jnp.float32
    )
    seg_piece = lax.all_gather(segments, "seq", axis=1, tiled=True)
    query_pos = jnp.arange(seg_piece.shape[1], dtype=jnp.int32)
    allowed = visible(seg_piece, query_pos, segments, local_pos)
    scores = jnp.einsum("gqhd,gkhd->gqhk", query_piece, key_low, preferred_element_type=jnp.float32)
    chances = jnp.where(allowed, jnp.exp(scores - lse_piece[..., None]), 0.0)
    new_value = jnp.einsum(
        "gqhk,gqhd->gkhd",
        chances.astype(jnp.bfloat16),
        grad_piece,
        preferred_element_type=jnp.float32,
    )
    grad_chances = jnp.einsum(
        "gqhd,gkhd->gqhk", grad_piece, value_low, preferred_element_type=jnp.float32
    )
    grad_scores = (chances * (grad_chances - delta_piece[..., None])).astype(jnp.bfloat16)
    new_key = jnp.einsum(
        "gqhk,gqhd->gkhd", grad_scores, query_piece, preferred_element_type=jnp.float32
    )
    grad_query_raw, grad_key_raw = turn_back((grad_query, new_key))
    grad_qkv_low = (
        jnp.stack([grad_query_raw, grad_key_raw, new_value], axis=2)
        .reshape(row_count, 3 * model_width)
        .astype(jnp.bfloat16)
    )
    grad_qkv_weight = jnp.dot(act_one.T, grad_qkv_low, preferred_element_type=jnp.float32)
    grad_qkv_bias = jnp.sum(grad_qkv_low.astype(jnp.float32), axis=0)
    grad_act_one = jnp.dot(grad_qkv_low, back_qkv.T, preferred_element_type=jnp.float32)
    grad_in_one, grad_gain_one, grad_bias_one = norm_back_one(grad_act_one)
    attention_shards = (
        lax.psum_scatter(grad_gain_one, ("dp", "seq"), scatter_dimension=0, tiled=True),
        lax.psum_scatter(grad_bias_one, ("dp", "seq"), scatter_dimension=0, tiled=True),
        lax.psum_scatter(grad_qkv_weight, ("dp", "seq"), scatter_dimension=0, tiled=True),
        lax.psum_scatter(grad_qkv_bias, ("dp", "seq"), scatter_dimension=0, tiled=True),
        lax.psum_scatter(grad_out_weight, ("dp", "seq"), scatter_dimension=0, tiled=True),
        lax.psum_scatter(grad_out_bias, ("dp", "seq"), scatter_dimension=0, tiled=True),
    )
    grad_tokens = (
        (grad_float + grad_in_one + grad_in_two)
        .astype(jnp.bfloat16)
        .reshape(group_size, block_size, model_width)
    )
    return (
        mixed,
        grad_tokens,
        attention_shards[0],
        attention_shards[1],
        attention_shards[2],
        attention_shards[3],
        attention_shards[4],
        attention_shards[5],
        mlp_shards[0],
        mlp_shards[1],
        mlp_shards[2],
        mlp_shards[3],
        mlp_shards[4],
        mlp_shards[5],
    )


GROUP = ("z", "y")
PEERS = ("x", "c")
EVERY = ("z", "y", "x", "c")
TURNS = 2 * CORES
ORDER = (0, 1, 7, 2, 6, 3, 5, 4)
LIMIT = 56 * 1024 * 1024
SMALL = 26 * 1024 * 1024
bf16, f32 = jnp.bfloat16, jnp.float32


def whole_ref():
    return pl.BlockSpec(memory_space=pltpu.VMEM)


def in_place():
    return pl.BlockSpec(memory_space=pl.ANY)


def call(
    kernel, results, inputs, operands, outputs, grid=(), prefetch=0, aliases=None, scratch=(), limit=LIMIT
):
    return pl.pallas_call(
        kernel,
        out_shape=[jax.ShapeDtypeStruct(*result) for result in results],
        grid_spec=pltpu.PrefetchScalarGridSpec(
            num_scalar_prefetch=prefetch, grid=grid, in_specs=inputs, out_specs=outputs, scratch_shapes=scratch
        ),
        input_output_aliases=aliases or {},
        compiler_params=pltpu.CompilerParams(vmem_limit_bytes=limit),
        cost_estimate=pl.CostEstimate(flops=1, bytes_accessed=1, transcendentals=0),
    )(*operands)


class Line:
    def __init__(self):
        self.last = ()

    def __call__(self, function, *operands, wait=()):
        operands = lax.optimization_barrier((operands, self.last, wait))[0]
        results = function(*operands)
        self.last = tuple(jax.tree.leaves(results))
        return results

    def hold(self, values):
        return lax.optimization_barrier((values, self.last))[0]


def after(value, *others):
    return lax.optimization_barrier((value, *others))[0]


def ring_perm(shift):
    depth, width = lax.axis_size("z"), lax.axis_size("y")
    places = [z * width for z in range(depth)] + [z * width + 1 for z in reversed(range(depth))]
    count = len(places)
    return [(places[i], places[(i + shift) % count]) for i in range(count)]


class Gather:
    def __init__(self, block):
        self.held = {0: [block]}
        self.ahead = self.behind = block
        self.done = 0

    def step(self, line, *others):
        half = len(ORDER) // 2
        ahead, behind = line.hold((self.ahead, self.behind, *others))[:2]
        self.done += 1
        if self.done < half:
            self.behind = lax.ppermute(behind, GROUP, ring_perm(1))
            self.ahead = lax.ppermute(ahead, GROUP, ring_perm(-1))
            self.held[len(ORDER) - self.done] = [self.behind]
            self.held[self.done] = [self.ahead]
        else:
            cut = behind.shape[0] // 2
            self.held[half] = [
                lax.ppermute(behind[:cut], GROUP, ring_perm(1)),
                lax.ppermute(ahead[cut:], GROUP, ring_perm(-1)),
            ]


def swap(values, axis):
    return lax.ppermute(values, axis, [(0, 1), (1, 0)])


def dot_f32(left, right, dims=((1,), (0,))):
    return lax.dot_general(left, right, (dims, ((), ())), preferred_element_type=f32)


def tile_spec(shape, index):
    return pl.BlockSpec(shape, lambda i, *scalars: index(i))


def same(shape):
    return tile_spec(shape, lambda i: (0,) * len(shape))


def spread_kernel(up, qkv, result):
    share, _, columns = result.shape
    tile = columns - 3 * HD
    for t in range(share):
        for i in range(3):
            at = (i * share + t) * HD
            result[t, :, i * HD : (i + 1) * HD] = qkv[:, at : at + HD]
        result[t, :, 3 * HD :] = up[:, t * tile : (t + 1) * tile]


def spread(up, qkv, share):
    rows, columns = up.shape
    return call(
        spread_kernel,
        [((share, rows, 3 * HD + columns // share), bf16)],
        [whole_ref()] * 2,
        (up, qkv),
        [whole_ref()],
    )[0]


def assemble_kernel(mine, *refs):
    sources, result = refs[:TURNS], refs[TURNS]
    for entry in range(result.shape[0]):
        for turn in range(TURNS):
            result[entry, pl.ds(mine[0] ^ turn, 1)] = sources[turn][entry : entry + 1]


def assemble(pieces, mine, step=2):
    entries, rows, columns = pieces[0].shape
    step = min(step, entries)
    return call(
        assemble_kernel,
        [((entries, TURNS, rows, columns), pieces[0].dtype)],
        [tile_spec((step, rows, columns), lambda i: (i, 0, 0))] * TURNS,
        (mine, *pieces),
        [tile_spec((step, TURNS, rows, columns), lambda i: (i, 0, 0, 0))],
        grid=(entries // step,),
        prefetch=1,
    )[0].reshape(entries * TURNS * rows, columns)


def settle_kernel(depth, peer, *refs):
    sources, result = refs[:-1], refs[-1]
    share = sources[0].shape[0]
    for shift, source in enumerate(sources):
        at = ((depth[0] + len(sources) - shift) % len(sources)) * share
        for j in range(share):
            result[pl.ds(at + (j ^ peer[0]), 1)] = source[j : j + 1]


def settle(depth, peer, *sources):
    shape = (len(sources) * sources[0].shape[0], *sources[0].shape[1:])
    return call(
        settle_kernel,
        [(shape, sources[0].dtype)],
        [same(source.shape) for source in sources],
        (depth, peer, *sources),
        [same(shape)],
        grid=(1,),
        prefetch=2,
    )[0]


def norm_kernel(count, affine, *refs):
    pieces, (one, two, mean_ref, scale_ref, one_turned, two_turned) = refs[:count], refs[-6:]
    values = stacked(pieces).astype(f32)
    mean = jnp.mean(values, axis=-1, keepdims=True)
    centered = values - mean
    scale = lax.rsqrt(jnp.mean(centered * centered, axis=-1, keepdims=True) + epsilon)
    normal = centered * scale
    for at, result, turned in ((0, one, one_turned), (2, two, two_turned)):
        act = (normal * affine[at : at + 1] + affine[at + 1 : at + 2]).astype(bf16)
        result[...] = act
        turned[...] = act.T.reshape(turned.shape)
    mean_ref[...] = mean
    scale_ref[...] = scale


def norm_block(at, pieces, affine, kept, slim):
    block, model = sum(piece.shape[0] for piece in pieces), pieces[0].shape[1]
    rows = len(ORDER) * block
    turned = (model // (TURNS * slim), 2, CORES, slim)
    results = [
        ((rows, model), bf16),
        ((rows, model), bf16),
        ((rows, 1), f32),
        ((rows, 1), f32),
        ((*turned, rows), bf16),
        ((*turned, rows), bf16),
    ]
    outputs = [pl.BlockSpec((block, shape[1]), lambda i: (at, 0)) for shape, _ in results[:4]]
    outputs += [pl.BlockSpec((*turned, block), lambda i: (0, 0, 0, 0, at))] * 2
    operands = [affine, *pieces]
    inputs = [whole_ref()] * len(operands)
    aliases = {}
    if kept is not None:
        aliases = {len(operands) + i: i for i in range(len(results))}
        operands += kept
        inputs += [in_place()] * len(results)
    return call(
        functools.partial(norm_kernel, len(pieces)), results, inputs, operands, outputs, grid=(1,), aliases=aliases
    )


def rotary_tables(places):
    half_rot = ROT // 2
    frequencies = 10000.0 ** (
        -(jnp.arange(half_rot, dtype=jnp.int32).astype(f32) * 2.0 / ROT)
    )
    turned = places.astype(f32)[:, None] * frequencies[None, :]
    cosines, sines = jnp.cos(turned), jnp.sin(turned)
    rest = jnp.zeros((places.shape[0], 128 - ROT), f32)
    none = jnp.zeros_like(sines)
    return (
        jnp.concatenate([cosines, cosines, rest + 1.0], axis=1),
        jnp.concatenate([sines, none, rest], axis=1),
        jnp.concatenate([none, sines, rest], axis=1),
    )


def rotate(values, tables, sign):
    cosines, first, second = tables
    half_rot = ROT // 2
    low = values[:, :128]
    ahead = pltpu.roll(low, 128 - half_rot, 1)
    behind = pltpu.roll(low, half_rot, 1)
    low = low * cosines + sign * (behind * second - ahead * first)
    return jnp.concatenate([low, values[:, 128:]], axis=1)


def qkv_kernel(depth_of, far_of, core, act, weight, bias, cosines, first, second, *results):
    qkv = jnp.dot(act[...], weight[...], preferred_element_type=f32) + bias[...]
    tables = (cosines[...], first[...], second[...])
    query = (rotate(qkv[:, :HD], tables, 1.0) * 0.0625).astype(bf16)
    key = rotate(qkv[:, HD : 2 * HD], tables, 1.0).astype(bf16)
    value = qkv[:, 2 * HD :].astype(bf16)
    parts = act.shape[0] // results[0].shape[2]
    start = pl.program_id(0) * parts
    spill(jnp.concatenate([query, key, value], axis=1), depth_of, far_of, core, start, results)


def spill(values, depth_of, far_of, core, start, results):
    block = results[0].shape[2]
    for part in range(values.shape[0] // block):
        at = start + part
        rows = values[None, None, part * block : (part + 1) * block]
        owner, low = depth_of[at] // 2, depth_of[at] % 2
        for result, mine in zip(results, (True, False)):

            @pl.when((owner == core[0]) == mine)
            def _():
                result[pl.ds(low, 1), pl.ds(far_of[at], 1)] = rows


def project(act, weight, bias, tables, depth_of, far_of, core, block):
    rows, model = act.shape
    columns = weight.shape[1]
    step = 4 * block
    return call(
        qkv_kernel,
        [((2, 2, block, columns), bf16)] * 2,
        [tile_spec((step, model), lambda i: (i, 0)), same((model, columns)), same((1, columns))]
        + [tile_spec((step, 128), lambda i: (i, 0))] * 3,
        (depth_of, far_of, core, act, weight, bias, *tables),
        [same((2, 2, block, columns))] * 2,
        grid=(rows // step,),
        prefetch=3,
    )


def place_kernel(depth_of, far_of, core, mine, came, result, *turned):
    block = result.shape[1]
    for at in range(result.shape[0]):
        for source, own in ((mine, True), (came, False)):

            @pl.when((depth_of[at] // 2 == core[0]) == own)
            def _():
                values = source[pl.ds(depth_of[at] % 2, 1), pl.ds(far_of[at], 1)][0, 0]
                result[at] = values
                for other in turned:
                    other[:, at * block : (at + 1) * block] = values.T


def place(mine, came, depth_of, far_of, core, turn=False):
    low, far, block, columns = mine.shape
    count = 2 * low * far
    shapes = [(count, block, columns)] + [(columns, count * block)] * turn
    placed, *turned = call(
        place_kernel,
        [(shape, bf16) for shape in shapes],
        [same(mine.shape)] * 2,
        (depth_of, far_of, core, mine, came),
        [same(shape) for shape in shapes],
        grid=(1,),
        prefetch=3,
        limit=SMALL,
    )
    return (placed.reshape(count * block, columns), *turned)


def pairs(ref, rows):
    return [(far, slice(at, at + rows)) for far in range(ref.shape[1]) for at in range(0, ref.shape[2], rows)]


def gathered(mine, came, even, seq, start, rows):
    parts = []
    for far, at in pairs(mine, rows):
        own, other = (ref[seq, far, at, start : start + HD] for ref in (mine, came))
        parts += [jnp.where(even, own, other), jnp.where(even, other, own)]
    return jnp.concatenate(parts, axis=0)


def scattered(mine, sent, even, seq, start, rows, values):
    for i, (far, at) in enumerate(pairs(mine, rows)):
        first, second = (values[(2 * i + k) * rows : (2 * i + k + 1) * rows] for k in range(2))
        mine[seq, far, at, start : start + HD] = jnp.where(even, first, second)
        sent[seq, far, at, start : start + HD] = jnp.where(even, second, first)


def chances_of(query, key, segments):
    scores = dot_f32(query, key, ((1,), (1,)))
    col_seg = jnp.broadcast_to(segments, scores.shape)
    row_seg = col_seg.T
    row_pos = lax.broadcasted_iota(jnp.int32, scores.shape, 0)
    col_pos = lax.broadcasted_iota(jnp.int32, scores.shape, 1)
    scores = jnp.where((col_pos <= row_pos) & (col_seg == row_seg), scores, masked_value)
    weights = jnp.exp(scores - jnp.max(scores, axis=-1, keepdims=True))
    return weights / jnp.sum(weights, axis=-1, keepdims=True)


def forward_kernel(rows, core, segments, mine, came, kept, sent):
    even = core[0] == 0
    for seq in range(mine.shape[0]):
        query, key, value = (gathered(mine, came, even, seq, i * HD, rows) for i in range(3))
        chances = chances_of(query, key, segments[seq])
        scattered(kept, sent, even, seq, 0, rows, dot_f32(chances.astype(bf16), value).astype(bf16))


def backward_kernel(
    rows, core, segments, cosines, first, second, mine, came, grad_mine, grad_came, kept, sent
):
    even = core[0] == 0
    tables = (cosines[...], first[...], second[...])
    for seq in range(mine.shape[0]):
        query, key, value = (gathered(mine, came, even, seq, i * HD, rows) for i in range(3))
        grad = gathered(grad_mine, grad_came, even, seq, 0, rows)
        chances = chances_of(query, key, segments[seq])
        chances_low = chances.astype(bf16)
        grad_chances = dot_f32(grad, value, ((1,), (1,)))
        delta = jnp.sum(chances_low.astype(f32) * grad_chances, axis=-1, keepdims=True)
        grad_scores = (chances * (grad_chances - delta)).astype(bf16)
        grad_query = dot_f32(grad_scores, key)
        grad_key = dot_f32(grad_scores, query, ((0,), (0,)))
        grad_value = dot_f32(chances_low, grad, ((0,), (0,)))
        for i, part in enumerate(
            (rotate(grad_query * 0.0625, tables, -1.0), rotate(grad_key, tables, -1.0), grad_value)
        ):
            scattered(kept, sent, even, seq, i * HD, rows, part.astype(bf16))


def attend(kernel, rows, columns, core, given, *arrays):
    operands = (*given, *arrays)
    shape = (*arrays[0].shape[:3], columns)
    return call(
        functools.partial(kernel, rows),
        [(shape, bf16)] * 2,
        [same(a.shape) for a in operands],
        (core, *operands),
        [same(shape)] * 2,
        grid=(1,),
        prefetch=1,
        limit=SMALL,
    )


def widen_kernel(act, weight, bias, activated, slope, turned):
    hidden = jnp.dot(act[...], weight[...], preferred_element_type=f32) + bias[...]
    cdf = 0.5 * (1.0 + lax.erf(hidden * math.sqrt(0.5)))
    result = (hidden * cdf).astype(bf16)
    activated[...] = result
    turned[...] = result.T
    slope[...] = (cdf + hidden * jnp.exp(-0.5 * hidden * hidden) * (1.0 / math.sqrt(2.0 * math.pi))).astype(bf16)


def widen(act, weight, bias, tile=256):
    rows, model = act.shape
    columns = weight.shape[1]
    return call(
        widen_kernel,
        [((rows, columns), bf16), ((rows, columns), bf16), ((columns, rows), bf16)],
        [
            same((rows, model)),
            tile_spec((model, tile), lambda i: (0, i)),
            tile_spec((1, tile), lambda i: (0, i)),
        ],
        (act, weight, bias),
        [tile_spec((rows, tile), lambda i: (0, i))] * 2 + [tile_spec((tile, rows), lambda i: (i, 0))],
        grid=(columns // tile,),
    )


def stacked(refs):
    return jnp.concatenate([ref[...] for ref in refs], axis=0)


def narrow_kernel(weight, slope, *refs):
    blocks, (result, sums) = refs[:-2], refs[-2:]
    grad = dot_f32(stacked(blocks), weight[...], ((1,), (1,))) * slope[...].astype(f32)
    grad = grad.astype(bf16)
    result[...] = grad
    sums[...] = jnp.sum(grad.astype(f32), axis=0, keepdims=True)


def narrow(blocks, weight, slope, tile=256):
    rows, columns = slope.shape
    model = weight.shape[1]
    return call(
        narrow_kernel,
        [((rows, columns), bf16), ((1, columns), f32)],
        [tile_spec((tile, model), lambda i: (i, 0)), tile_spec((rows, tile), lambda i: (0, i))]
        + [same(piece.shape) for piece in blocks],
        (weight, slope, *blocks),
        [tile_spec((rows, tile), lambda i: (0, i)), tile_spec((1, tile), lambda i: (0, i))],
        grid=(columns // tile,),
        limit=SMALL,
    )


def head_kernel(depth_of, far_of, core, weight, *refs):
    blocks, results, total = refs[:-3], refs[-3:-1], refs[-1]
    part = dot_f32(stacked(blocks), weight[...], ((1,), (1,)))
    step = pl.program_id(0)

    @pl.when(step == 0)
    def _():
        total[...] = part

    @pl.when(step > 0)
    def _():
        total[...] += part

    @pl.when(step == pl.num_programs(0) - 1)
    def _():
        spill(total[...].astype(bf16), depth_of, far_of, core, 0, results)


def head_grads(blocks, weight, depth_of, far_of, core, block, tile=512):
    rows = sum(piece.shape[0] for piece in blocks)
    return call(
        head_kernel,
        [((2, 2, block, HD), bf16)] * 2,
        [tile_spec((piece.shape[0], tile), lambda i: (0, i)) for piece in (weight, *blocks)],
        (depth_of, far_of, core, weight, *blocks),
        [same((2, 2, block, HD))] * 2,
        grid=(weight.shape[1] // tile,),
        prefetch=3,
        scratch=[pltpu.VMEM((rows, HD), f32)],
        limit=SMALL,
    )


def across(total, half, near, far, slots=False):
    first, second = total[:, 0], total[:, 1]
    low = half[0] == 0
    near[...] = jnp.where(low, first, second).reshape(near.shape)
    other = jnp.where(low, second, first).astype(bf16)
    if slots:
        far[pl.ds(1 - half[0], 1)] = other[None]
    else:
        far[...] = other.reshape(far.shape)


def rows_kernel(near, slots, core, half, act, grad, *refs):
    entries, _, _, rows, tokens = act.shape
    total = dot_f32(act[...].reshape(entries * 2 * rows, tokens), grad[...])
    total = total.reshape(entries, 2, rows, grad.shape[1])
    if near:
        came, kept, sent = refs
        across(total + came[...].astype(f32), half, kept, sent, slots)
    else:
        refs[0][...] = total.astype(bf16)


def rows_grad(turned, grad, core, half, came=None, step=4, slots=False):
    entries, _, _, rows, tokens = turned.shape
    columns = grad.shape[1]
    near = came is not None
    spec = tile_spec((step, 2, rows, columns), lambda i: (i, 0, 0, 0))
    inputs = [
        pl.BlockSpec(
            (step, 2, 1, rows, tokens), lambda i, c, x: (i, 0, c[0] if near else 1 - c[0], 0, 0)
        ),
        same((tokens, columns)),
    ]
    if near:
        results = [((entries, rows, columns), f32), ((entries, rows, columns), bf16)]
        outputs = [tile_spec((step, rows, columns), lambda i: (i, 0, 0))] * 2
        if slots:
            results[1] = ((2, entries, rows, columns), bf16)
            outputs[1] = tile_spec((2, step, rows, columns), lambda i: (0, i, 0, 0))
    else:
        results, outputs = [((entries, 2, rows, columns), bf16)], [spec]
    return call(
        functools.partial(rows_kernel, near, slots),
        results,
        inputs + [spec] * near,
        (core, half, turned, grad) + (came,) * near,
        outputs,
        grid=(entries // step,),
        prefetch=2,
        limit=SMALL,
    )


def down_kernel(near, core, half, attended, activated, *refs):
    count = 3 if near else 1
    blocks, refs = refs[:-count], refs[-count:]
    parts = [ref[x, 0] for x in range(2) for ref in (attended, activated)]
    total = dot_f32(jnp.concatenate(parts, axis=0), stacked(blocks))
    total = total.reshape(1, 2, total.shape[0] // 2, total.shape[1])
    if near:
        came, kept, sent = refs
        across(total + came[...][None].astype(f32), half, kept, sent)
    else:
        refs[0][...] = total[0].astype(bf16)


def down_grad(attended, activated, blocks, core, half, came=None, tile=512):
    tokens = attended.shape[3]
    model = blocks[0].shape[1]
    rows = attended.shape[2] + activated.shape[2]
    near = came is not None
    spec = tile_spec((2, rows, tile), lambda i: (0, 0, i))
    inputs = [
        pl.BlockSpec(
            (2, 1, turned.shape[2], tokens), lambda i, c, x: (0, c[0] if near else 1 - c[0], 0, 0)
        )
        for turned in (attended, activated)
    ]
    inputs += [tile_spec((piece.shape[0], tile), lambda i: (0, i)) for piece in blocks]
    if near:
        results = [((rows, model), f32), ((rows, model), bf16)]
        outputs = [tile_spec((rows, tile), lambda i: (0, i))] * 2
    else:
        results, outputs = [((2, rows, model), bf16)], [spec]
    return call(
        functools.partial(down_kernel, near),
        results,
        inputs + [spec] * near,
        (core, half, attended, activated, *blocks) + (came,) * near,
        outputs,
        grid=(model // tile,),
        prefetch=2,
        limit=SMALL,
    )


def join_kernel(pieces, given, result, *sums):
    share = given.shape[0]
    width = result.shape[1] // (share * pieces)
    for t in range(share):
        for i in range(pieces):
            at = (i * share + t) * width
            result[:, at : at + width] = given[t, :, i * width : (i + 1) * width].astype(f32)
    for ref in sums:
        rows, columns = ref.shape
        ref[...] = jnp.sum(given[:, :rows, pieces * width : pieces * width + columns].astype(f32), axis=0)


def join(given, pieces, extra=None):
    share, rows, columns = given.shape
    results = [((rows, share * (columns - (extra[1] if extra else 0))), f32)]
    results += [(extra, f32)] if extra else []
    return call(
        functools.partial(join_kernel, pieces), results, [whole_ref()], (given,), [whole_ref()] * len(results), limit=SMALL)


def widen_rows_kernel(mine, came, extra, result):
    columns = mine.shape[2]
    result[:, :, :columns] = (mine[...] + came[...].astype(f32)).astype(bf16)
    result[:, :, columns:] = jnp.zeros((*result.shape[:2], result.shape[2] - columns), bf16)
    result[:, : extra.shape[1], columns:] = extra[...].astype(bf16)


def total_with(mine, came, extra):
    shape = (*mine.shape[:2], mine.shape[2] + extra.shape[2])
    operands = (mine, came, extra)
    return call(widen_rows_kernel, [(shape, bf16)], [whole_ref()] * 3, operands, [whole_ref()], limit=SMALL)[0]


def share_part(pull, first, count, block, lefts, rights, pieces, extras=(), tile=512):
    model = rights[0].shape[0 if pull else 1]
    depths = [right.shape[1 if pull else 0] for right in rights]
    operands, inputs = [], []
    for left, depth in zip(lefts, depths):
        for b in range(count):
            operands.append(left)
            inputs.append(tile_spec((block, depth), lambda i, b=b: (first + b, 0)))
    for right, depth in zip(rights, depths):
        operands.append(right)
        inputs.append(
            tile_spec((tile, depth), lambda i: (i, 0)) if pull else tile_spec((depth, tile), lambda i: (0, i))
        )
    given = 0
    if pull:
        gains, values, mean, scale = extras
        given = len(values)
        for row in (*gains, *values):
            operands.append(row)
            inputs.append(tile_spec((row.shape[0], tile), lambda i: (0, i)))
        for stat in (mean, scale):
            for b in range(count):
                operands.append(stat)
                inputs.append(tile_spec((block, 1), lambda i, b=b: (first + b, 0)))

    def kernel(*refs):
        refs = list(refs)

        def take(number):
            taken = refs[:number]
            del refs[:number]
            return taken

        left_a, left_b = stacked(take(count)), stacked(take(count))
        (right_a,), (right_b,) = take(1), take(1)
        dims = ((1,), (1,)) if pull else ((1,), (0,))
        part_a = dot_f32(left_a, right_a[...], dims)
        part_b = dot_f32(left_b, right_b[...], dims)
        if pull:
            (gains_ref,) = take(1)
            tokens = stacked(take(given)).astype(f32)
            normal = (tokens - stacked(take(count))) * stacked(take(count))
            (sums,) = take(1)
            sums[...] = jnp.concatenate(
                [
                    jnp.sum(part, axis=0, keepdims=True)
                    for part in (part_a * normal, part_a, part_b * normal, part_b)
                ]
                + [jnp.zeros((4, tile), f32)],
                axis=0,
            )
            total = part_a * gains_ref[0:1] + part_b * gains_ref[2:3]
        else:
            total = part_a + part_b
        for (start, rows, dtype), result in zip(pieces, refs):
            result[...] = total[start : start + rows].astype(dtype)

    results = [((rows, model), dtype) for _, rows, dtype in pieces]
    outputs = [tile_spec((rows, tile), lambda i: (0, i)) for _, rows, _ in pieces]
    if pull:
        results = [((8, model), f32)] + results
        outputs = [tile_spec((8, tile), lambda i: (0, i))] + outputs
    return call(
        kernel, results, inputs, operands, outputs, grid=(model // tile,), limit=LIMIT if pull else SMALL
    )


def early_pieces(block):
    cut = block // 2
    return [(2 * block, cut, bf16), (2 * block + cut, cut, bf16), (0, block, bf16), (block, block, bf16)]


def late_pieces(block):
    return [(0, block, f32)] + [(i * block, block, bf16) for i in range(1, 5)]


def all_pieces(block):
    return late_pieces(block) + [(5 * block + start, rows, dtype) for start, rows, dtype in early_pieces(block)]


def add_kernel(one, two, ahead, behind, *results):
    cut = ahead.shape[0]
    rows = one.shape[0]
    for mine, came, result, start in ((one, ahead, results[0], 0), (two, behind, results[1], rows - cut)):
        if cut < rows:
            result[...] = mine[...]
        at = slice(start, start + cut)
        result[at] = (mine[at].astype(f32) + came[...].astype(f32)).astype(bf16)


def add_incoming(one, two, ahead, behind, tile=1024):
    rows, model = one.shape
    return call(
        add_kernel,
        [(one.shape, bf16)] * 2,
        [tile_spec((a.shape[0], tile), lambda i: (0, i)) for a in (one, two, ahead, behind)],
        (one, two, ahead, behind),
        [tile_spec((rows, tile), lambda i: (0, i))] * 2,
        grid=(model // tile,), limit=SMALL)


class Scatter:
    def send(self, one, two):
        self.ahead = lax.ppermute(one, GROUP, ring_perm(1))
        self.behind = lax.ppermute(two, GROUP, ring_perm(-1))

    def step(self, line, one, two, wait=()):
        self.send(*line(add_incoming, one, two, self.ahead, self.behind, wait=wait))


def total_slot_kernel(half, mine, came, result):
    result[...] = (mine[...] + came[...].reshape(mine.shape).astype(f32)).astype(bf16)


def total_slot(half, mine, came, step=2):
    entries, rows, columns = mine.shape
    block = (entries // step, rows, columns)
    return call(
        total_slot_kernel,
        [(mine.shape, bf16)],
        [
            tile_spec(block, lambda i: (i, 0, 0)),
            pl.BlockSpec((1, *block), lambda i, x: (1 - x[0], i, 0, 0)),
        ],
        (half, mine, came),
        [tile_spec(block, lambda i: (i, 0, 0))],
        grid=(step,),
        prefetch=1, limit=SMALL)[0]


def total_kernel(mine, came, *results):
    total = mine[...] + came[...].astype(f32)
    at = 0
    for result in results:
        rows = result.shape[0]
        result[...] = total[at : at + rows].astype(result.dtype)
        at += rows


def total_rows(mine, came, pieces):
    tail = mine.shape[1:]
    steps = 2
    tile = tail[:-1] + (tail[-1] // steps,)

    def spec(rows):
        return tile_spec((rows, *tile), lambda i: (0,) * len(tile) + (i,))

    return call(
        total_kernel,
        [((rows, *tail), dtype) for rows, dtype in pieces],
        [spec(mine.shape[0])] * 2,
        (mine, came),
        [spec(rows) for rows, _ in pieces],
        grid=(steps,), limit=SMALL)


def apart(values, half, kept, sent):
    cut = values.shape[0] // 2
    low = half[0] == 0
    first, second = values[:cut], values[cut:]
    kept[...] = jnp.where(low, first, second).astype(kept.dtype)
    sent[...] = jnp.where(low, second, first).astype(sent.dtype)


def mixed_kernel(half, own, ahead, behind, tokens, bias_one, bias_two, kept, sent):
    total = own[...] + ahead[...].astype(f32) + behind[...].astype(f32) + tokens[...].astype(f32)
    apart(total + bias_one[...] + bias_two[...], half, kept, sent)


def by_rows(kernel, half, operands, tokens):
    rows, model = tokens.shape
    return call(
        kernel,
        [((rows // 2, model), bf16)] * 2,
        [tile_spec((rows, 1), lambda i: (0, 0)) if a.shape[1] == 1 else same(a.shape) for a in operands],
        (half, *operands),
        [same((rows // 2, model))] * 2,
        grid=(1,),
        prefetch=1, limit=SMALL)


def mixed_rows(half, *operands):
    return by_rows(mixed_kernel, half, operands, operands[3])


def vectors_kernel(share, early, late, grad, grad_qkv, up_sum, result):
    result[...] = jnp.zeros_like(result)
    result[:4] = early[:4] + late[:4]
    result[4:5] = jnp.sum(grad[...].astype(f32), axis=0, keepdims=True)
    qkv_sum = jnp.sum(grad_qkv[...].astype(f32), axis=0, keepdims=True)
    for i in range(3):
        at = pl.multiple_of(share[0] * HD, HD)
        result[5 + i : 6 + i, pl.ds(at, HD)] = qkv_sum[:, i * HD : (i + 1) * HD]
    columns = up_sum.shape[1]
    each = result.shape[1] // columns
    at = pl.multiple_of((share[0] % each) * columns, columns)
    result[pl.ds(8 + share[0] // each, 1), pl.ds(at, columns)] = up_sum[...]


def vectors(share, early, late, grad, grad_qkv, up_sum):
    operands = (early, late, grad, grad_qkv, up_sum)
    return call(
        vectors_kernel,
        [((16, early.shape[1]), f32)],
        [same(a.shape) for a in operands],
        (share, *operands),
        [same((16, early.shape[1]))],
        grid=(1,),
        prefetch=1, limit=SMALL)[0]


def sum_kernel(*refs):
    total = refs[0][...]
    for ref in refs[1:-1]:
        total = total + ref[...]
    refs[-1][...] = total


def sum_arrays(*arrays):
    return call(
        sum_kernel, [(arrays[0].shape, f32)], [whole_ref()] * len(arrays), arrays, [whole_ref()], limit=SMALL)[0]


def finish_kernel(half, own, ahead, behind, tokens, grad, mean, scale, kept, sent):
    pulled = own[...] + ahead[...].astype(f32) + behind[...].astype(f32)
    normal = (tokens[...].astype(f32) - mean[...]) * scale[...]
    inner = (
        pulled
        - jnp.mean(pulled, axis=-1, keepdims=True)
        - normal * jnp.mean(pulled * normal, axis=-1, keepdims=True)
    )
    apart(grad[...].astype(f32) + scale[...] * inner, half, kept, sent)


def finish(half, *operands):
    return by_rows(finish_kernel, half, operands, operands[3])


def trade_kernel(half, *refs):
    count = len(refs) // 3
    low = half[0] == 0
    for values, came, result in zip(refs[:count], refs[count : 2 * count], refs[2 * count :]):
        rows = came.shape[0]
        own = values[pl.ds(half[0], 1)][0]
        result[:rows] = jnp.where(low, own, came[...])
        result[rows:] = jnp.where(low, came[...], own)


def trade(half, arrays, came):
    shapes = [(2 * piece.shape[0], piece.shape[1]) for piece in came]
    return call(
        trade_kernel,
        [(shape, bf16) for shape in shapes],
        [same(a.shape) for a in (*arrays, *came)],
        (half, *arrays, *came),
        [same(shape) for shape in shapes],
        grid=(1,),
        prefetch=1,
    )


def in_order_kernel(half, *refs):
    count = len(refs) // 3
    for own, came, result in zip(refs[:count], refs[count : 2 * count], refs[2 * count :]):
        low = half[0] == 0
        result[0] = jnp.where(low, own[...], came[...])
        result[1] = jnp.where(low, came[...], own[...])


def in_order(half, own, came):
    operands = (*own, *came)
    return call(
        in_order_kernel,
        [((2, *a.shape), a.dtype) for a in own],
        [same(a.shape) for a in operands],
        (half, *operands),
        [same((2, *a.shape)) for a in own],
        grid=(1,),
        prefetch=1, limit=SMALL)


def scalar(value):
    return jnp.reshape(value, (1,)).astype(jnp.int32)


def grouped(
    tokens,
    segments,
    ln1_gain,
    ln1_bias,
    qkv_weight,
    qkv_bias,
    out_weight,
    out_bias,
    ln2_gain,
    ln2_bias,
    fc1_weight,
    fc1_bias,
    fc2_weight,
    fc2_bias,
    cotangent,
):
    depth, width = lax.axis_size("z"), lax.axis_size("y")
    share = depth * width
    devices = share * TURNS
    z, y, x, c = (lax.axis_index(name) for name in EVERY)
    t = z * width + y
    mine = x * CORES + c
    r = jnp.where(y == 0, z, 2 * depth - 1 - z)
    seqs, rows, model = tokens.shape
    block = seqs * rows
    slim = ln1_gain.shape[0]
    hidden = fc2_weight.shape[0] * TURNS
    line = Line()

    sent = line(lambda up, qkv: spread(up, qkv, share), fc1_weight, qkv_weight)
    columns = lax.all_to_all(sent, GROUP, 0, 0, tiled=True)

    down_out = (out_weight[None], fc2_weight[None])
    down_out_near = [swap(piece, "c") for piece in line.hold(down_out)]
    came = [
        swap(lax.dynamic_index_in_dim(rows_of, 1 - x, 0, keepdims=False), "x")
        for rows_of in line.hold((tokens, cotangent))
    ]

    pieces = (
        ln1_gain,
        ln1_bias,
        ln2_gain,
        ln2_bias,
        out_bias,
        fc2_bias,
        qkv_bias,
        fc1_bias,
        segments.reshape(-1).astype(bf16),
    )
    ends = [0]
    for piece in pieces:
        ends.append(ends[-1] + piece.shape[0])
    packed = jnp.concatenate(line.hold(pieces))
    packed = jnp.pad(packed, (0, -ends[-1] % 1024)).reshape(1, -1, 128)
    for axis in ("c", "x", "y"):
        packed = jnp.concatenate([packed, swap(packed, axis)], axis=0)
    packed = [packed] + [
        lax.ppermute(packed, "z", [(i, (i + shift) % depth) for i in range(depth)]) for shift in range(1, depth)
    ]
    steps = (r + jnp.array(ORDER, jnp.int32)) % share
    far_of = (steps >= depth).astype(jnp.int32)
    depth_of = jnp.where(far_of == 1, 2 * depth - 1 - steps, steps)
    within = (jnp.arange(2, dtype=jnp.int32) * CORES + c)[:, None] * rows + jnp.arange(rows, dtype=jnp.int32)
    token_pos = far_of[:, None] * (TURNS * rows) + within.reshape(1, -1)
    token_tables = line(rotary_tables, token_pos.reshape(-1))
    seq_tables = line(rotary_tables, jnp.arange(rows * width * TURNS, dtype=jnp.int32))

    my_rows, my_grad = line(trade, scalar(x), (tokens, cotangent), came, wait=packed[0])
    down_out_far = [swap(piece, "x") for piece in line.hold(down_out)]
    packed = line(settle, scalar(z), scalar(y * TURNS + mine), *packed, wait=down_out_near).reshape(devices, -1)
    down_out_last = [swap(piece, "c") for piece in line.hold(down_out_far)]
    in_ring = Gather(my_rows)
    in_ring.step(line, columns, *down_out_last)
    small = [
        packed[:, ends[i] : ends[i + 1]].astype(f32).reshape(1, -1) for i in range(4, len(pieces) - 1)
    ]
    bias_out, bias_down, bias_qkv, bias_up = small
    affine = packed[:, : ends[4]].astype(f32).reshape(devices, 4, slim).transpose(1, 0, 2).reshape(4, model)
    bias_up = lax.dynamic_slice_in_dim(bias_up, t * hidden, hidden, 1)
    bias_qkv = lax.dynamic_index_in_dim(
        bias_qkv.reshape(3, HEADS, HD), t, 1, keepdims=False
    ).reshape(1, 3 * HD)

    all_seg = packed[:, ends[-2] : ends[-1]].reshape(depth, width * TURNS, seqs, rows)
    seq_seg = lax.dynamic_slice_in_dim(all_seg, c * 2, 2, 0)
    seq_seg = lax.dynamic_index_in_dim(seq_seg, x, 2, keepdims=False).reshape(2, -1).astype(f32)
    masks = (seq_seg[:, None, :],)

    def norm(at, kept):
        pieces = in_ring.held[ORDER[at]]
        return line(lambda *given: norm_block(at, *given, slim), pieces, affine, kept)

    kept = norm(0, None)
    qkv_cols, up_cols = after((columns[:, :, : 3 * HD], columns[:, :, 3 * HD :]), columns)
    qkv_far, up_far = swap(qkv_cols, "x"), swap(up_cols, "x")
    qkv_near, up_near = swap(qkv_cols, "c"), swap(up_cols, "c")
    weight_out, weight_down = (
        line(assemble, pieces, scalar(mine))
        for pieces in zip(down_out, down_out_near, down_out_far, down_out_last)
    )
    in_ring.step(line)
    kept = norm(1, kept)
    kept = norm(2, kept)
    in_ring.step(line)
    qkv_last = swap(line.hold(qkv_far), "c")
    kept = norm(3, kept)
    kept = norm(4, kept)
    weight_qkv = line(assemble, (qkv_cols, qkv_near, qkv_far, qkv_last), scalar(mine))
    in_ring.step(line)
    kept = norm(5, kept)
    kept = norm(6, kept)
    grad_ring = Gather(my_grad)
    grad_ring.step(line, *in_ring.held[4])
    up_last = swap(line.hold(up_far), "c")
    act_one, act_two, means, scales, turned_one, turned_two = norm(7, kept)

    lie = (depth_of, far_of, scalar(c))
    qkv_mine, sent = line(
        lambda *given: project(*given, block), act_one, weight_qkv, bias_qkv, token_tables, *lie
    )
    grad_ring.step(line)
    qkv_came = swap(sent, "c")
    weight_up = line(assemble, (up_cols, up_near, up_far, up_last), scalar(mine))
    out_mine, sent = line(
        lambda *given: attend(forward_kernel, rows, HD, *given), scalar(c), masks, qkv_mine, qkv_came
    )
    out_came = swap(sent, "c")
    grad_ring.step(line)
    act_hidden, slope, hidden_turned = line(widen, act_two, weight_up, bias_up)
    grad_ring.step(line)
    attended, attended_turned = line(lambda *given: place(*given, turn=True), out_mine, out_came, *lie)

    out_own, *out_late = line(
        lambda a, b: share_part(False, 0, len(ORDER), block, a, b, all_pieces(block)),
        (attended, act_hidden),
        (weight_out, weight_down),
    )
    out_late, (one, two, *out_early) = out_late[:4], out_late[4:]
    out_ring = Scatter()

    grads = [piece for j in ORDER for piece in grad_ring.held[j]]
    grad_mine, sent = line(lambda *given: head_grads(*given, block), grads, weight_out, *lie)
    grad_came = swap(sent, "c")
    out_ring.send(*line.hold((one, two)))
    grad_hidden, up_sum = line(narrow, grads, weight_down, slope)
    which = (scalar(c), scalar(x))
    (up_far,) = line(rows_grad, turned_two, grad_hidden, *which)
    back_mine, sent = line(
        lambda *given: attend(backward_kernel, rows, 3 * HD, *given),
        scalar(c),
        (*masks, *seq_tables),
        qkv_mine,
        qkv_came,
        grad_mine,
        grad_came,
        wait=(out_ring.ahead, out_ring.behind),
    )
    back_came = swap(sent, "c")
    out_ring.step(line, *out_early)
    up_came = swap(line.hold(up_far), "c")
    down_lefts = (
        attended_turned.reshape(2, CORES, slim, -1),
        hidden_turned.reshape(2, CORES, hidden // TURNS, -1),
    )
    (down_far,) = line(down_grad, *down_lefts, grads, *which)
    (grad_qkv,) = line(place, back_mine, back_came, *lie)
    (qkv_far,) = line(rows_grad, turned_one, grad_qkv, *which)
    grad_up, up_far = line(
        lambda *given: rows_grad(*given, slots=True), turned_two, grad_hidden, *which, up_came
    )
    out_ring.step(line, out_late[2], out_late[3])
    qkv_came = swap(line.hold(qkv_far), "c")
    up_came = lax.all_to_all(line.hold(up_far), "x", 0, 0, tiled=True)

    lefts, rights = (grad_qkv, grad_hidden), (weight_qkv, weight_up)

    def pull(first, count, pieces):
        values = [piece for j in ORDER[first : first + count] for piece in in_ring.held[j]]
        return line(
            lambda left, right, more: share_part(True, first, count, block, left, right, pieces, more),
            lefts,
            rights,
            ((affine,), values, means, scales),
        )

    early_sums, one, two, *early = pull(5, 3, early_pieces(block))
    pull_ring = Scatter()
    pull_ring.send(one, two)
    out_ring.step(line, out_late[0], out_late[1])
    late_sums, pull_own, *late = pull(0, 5, late_pieces(block))
    sums = line(vectors, scalar(t), early_sums, late_sums, my_grad, grad_qkv, up_sum)
    grad_qkv_w, qkv_far = line(rows_grad, turned_one, grad_qkv, *which, qkv_came)
    grad_up = line(total_slot, scalar(x), grad_up, up_came)
    pull_ring.step(line, *early, wait=(out_ring.ahead, out_ring.behind))
    grad_up = lax.all_to_all(line.hold(grad_up), GROUP, 0, 0, tiled=True)
    qkv_came, down_came = swap(line.hold(qkv_far), "x"), swap(line.hold(down_far), "c")
    sums_came = swap(line.hold(sums), "c")
    sums = line(sum_arrays, sums, sums_came)
    grad_down, down_far = line(down_grad, *down_lefts, grads, *which, down_came)
    pull_ring.step(line, late[2], late[3])
    sums_came = swap(line.hold(sums), "x")
    sums = line(sum_arrays, sums, sums_came)

    def slices(values, rows):
        cut = values.reshape(rows, share, TURNS, -1)
        return lax.dynamic_index_in_dim(cut, mine, 2, keepdims=False).transpose(1, 0, 2).reshape(share, -1)

    sums = jnp.concatenate([slices(sums[:5], 5), slices(sums[5:8], 1), slices(sums[8:12], 1)], axis=1)
    sums = jnp.pad(sums.reshape(share, -1, 128), ((0, 0), (0, 2), (0, 0)))
    grad_qkv_w = line(total_with, grad_qkv_w, qkv_came, sums)
    pull_ring.step(line, late[0], late[1])
    grad_qkv_w = lax.all_to_all(line.hold(grad_qkv_w), GROUP, 0, 0, tiled=True)
    down_came = swap(line.hold(down_far), "x")
    (grad_up,) = line(lambda given: join(given, 1), grad_up)
    kept_out, sent_out = line(
        mixed_rows, scalar(x), out_own, out_ring.ahead, out_ring.behind, my_rows, bias_out, bias_down
    )
    grad_out, grad_down = line(
        lambda a, b: total_rows(a, b, [(slim, f32), (hidden // TURNS, f32)]), grad_down, down_came
    )
    grad_qkv_w, sums = line(lambda given: join(given, 3, (8, 128)), grad_qkv_w)
    kept_in, sent_in = line(
        finish, scalar(x), pull_own, pull_ring.ahead, pull_ring.behind, my_rows, my_grad, means, scales
    )
    came_in, came_out = (swap(sent, "x") for sent in line.hold((sent_in, sent_out)))
    mixed, grad_in = line(in_order, scalar(x), (kept_out, kept_in), (came_out, came_in))

    sums = sums.reshape(-1)
    norm_sums = [sums[i * slim : (i + 1) * slim] for i in range(5)]
    qkv_end = 5 * slim + qkv_bias.shape[0]
    return (
        mixed,
        grad_in,
        norm_sums[0],
        norm_sums[1],
        grad_qkv_w,
        sums[5 * slim : qkv_end],
        grad_out,
        norm_sums[4],
        norm_sums[2],
        norm_sums[3],
        grad_up,
        sums[qkv_end : qkv_end + fc1_bias.shape[0]],
        grad_down,
        norm_sums[4],
    )


def specs(batch, block):
    every = batch + block
    one, two, three = P(every), P(every, None), P(batch, block, None)
    arguments = (three, P(batch, block), one, one, two, one, two, one, one, one, two, one, two, one, three)
    results = (three, three, one, one, two, one, two, one, one, one, two, one, two, one)
    return arguments, results


def solution(mesh):
    depth, ring = mesh.shape["dp"], mesh.shape["seq"]
    width = ring // TURNS
    if width == 2 and depth == TURNS and depth * width == HEADS:
        chips = Mesh(mesh.devices.reshape(depth, width, 2, CORES), EVERY)
        arguments, results = specs(("z",), ("y", "x", "c"))
        return jax.shard_map(
            grouped, mesh=chips, in_specs=arguments, out_specs=results, check_vma=False
        )
    arguments, results = specs(("dp",), ("seq",))
    return jax.shard_map(
        per_device, mesh=mesh, in_specs=arguments, out_specs=results, check_vma=False
    )
```

```python
import functools
import math

import jax
import jax.numpy as jnp
from jax import lax
from jax.experimental import pallas as pl
from jax.experimental.pallas import tpu as pltpu
from jax.sharding import Mesh, PartitionSpec as P

HEADS = 8
HD = 256
ROT = 64
CORES = 2


epsilon = 1e-05
masked_value = -1e30


def layer_norm(values, gain, shift):
    average = jnp.mean(values, axis=-1, keepdims=True)
    centered = values - average
    variance = jnp.mean(centered * centered, axis=-1, keepdims=True)
    return centered * lax.rsqrt(variance + epsilon) * gain + shift


def base_tables(places):
    half_rot = ROT // 2
    frequencies = 10000.0 ** (
        -(jnp.arange(half_rot, dtype=jnp.int32).astype(jnp.float32) * 2.0 / ROT)
    )
    angles = places[:, None] * frequencies[None, :]
    return (jnp.cos(angles)[:, None, :], jnp.sin(angles)[:, None, :])


def base_rotate(values, cosines, sines):
    half_rot = ROT // 2
    first_half = values[..., :half_rot]
    second_half = values[..., half_rot:ROT]
    return jnp.concatenate(
        [
            first_half * cosines - second_half * sines,
            second_half * cosines + first_half * sines,
            values[..., ROT:],
        ],
        axis=-1,
    )


def gelu_exact(values):
    return jax.nn.gelu(values, approximate=False)


def visible(query_seg, query_pos, key_seg, key_pos):
    causal = key_pos[None, :] <= query_pos[:, None]
    same_doc = query_seg[:, :, None] == key_seg[:, None, :]
    return (causal[None] & same_doc)[:, :, None, :]


def per_device(
    tokens,
    segments,
    ln1_gain,
    ln1_bias,
    qkv_weight,
    qkv_bias,
    out_weight,
    out_bias,
    ln2_gain,
    ln2_bias,
    fc1_weight,
    fc1_bias,
    fc2_weight,
    fc2_bias,
    cotangent,
):
    group_size, block_size, model_width = tokens.shape
    row_count = group_size * block_size
    attention_full = (
        lax.all_gather(ln1_gain, ("dp", "seq"), axis=0, tiled=True),
        lax.all_gather(ln1_bias, ("dp", "seq"), axis=0, tiled=True),
        lax.all_gather(qkv_weight, ("dp", "seq"), axis=0, tiled=True),
        lax.all_gather(qkv_bias, ("dp", "seq"), axis=0, tiled=True),
        lax.all_gather(out_weight, ("dp", "seq"), axis=0, tiled=True),
        lax.all_gather(out_bias, ("dp", "seq"), axis=0, tiled=True),
    )
    gain_one, bias_one, weight_qkv, bias_qkv, weight_out, bias_out = attention_full
    flat_in = tokens.reshape(row_count, model_width).astype(jnp.float32)
    normed_one, norm_back_one = jax.vjp(
        layer_norm, flat_in, gain_one.astype(jnp.float32), bias_one.astype(jnp.float32)
    )
    act_one = normed_one.astype(jnp.bfloat16)
    mixed_qkv = jnp.dot(act_one, weight_qkv, preferred_element_type=jnp.float32) + bias_qkv.astype(
        jnp.float32
    )
    mixed_qkv = mixed_qkv.reshape(group_size, block_size, 3, HEADS, HD)
    first_pos = lax.axis_index("seq") * block_size
    local_pos = first_pos + jnp.arange(block_size, dtype=jnp.int32)
    cosines, sines = base_tables(local_pos.astype(jnp.float32))

    def turn_all(query_raw, key_raw):
        return (base_rotate(query_raw, cosines, sines) * 0.0625, base_rotate(key_raw, cosines, sines))

    (query_turned, key_turned), turn_back = jax.vjp(
        turn_all, mixed_qkv[:, :, 0], mixed_qkv[:, :, 1]
    )
    query_low = query_turned.astype(jnp.bfloat16)
    key_low = key_turned.astype(jnp.bfloat16)
    value_low = mixed_qkv[:, :, 2].astype(jnp.bfloat16)
    start_top = jnp.full((group_size, block_size, HEADS), masked_value, jnp.float32)
    key_piece = lax.all_gather(key_low, "seq", axis=1, tiled=True)
    value_piece = lax.all_gather(value_low, "seq", axis=1, tiled=True)
    seg_piece = lax.all_gather(segments, "seq", axis=1, tiled=True)
    key_pos = jnp.arange(seg_piece.shape[1], dtype=jnp.int32)
    allowed = visible(segments, local_pos, seg_piece, key_pos)
    scores = jnp.einsum("gqhd,gkhd->gqhk", query_low, key_piece, preferred_element_type=jnp.float32)
    scores = jnp.where(allowed, scores, masked_value)
    new_top = jnp.maximum(start_top, jnp.max(scores, axis=-1))
    weights = jnp.where(allowed, jnp.exp(scores - new_top[..., None]), 0.0)
    new_total = jnp.sum(weights, axis=-1)
    new_out = jnp.einsum(
        "gqhk,gkhd->gqhd",
        weights.astype(jnp.bfloat16),
        value_piece,
        preferred_element_type=jnp.float32,
    )
    attended = new_out / new_total[..., None]
    log_total = new_top + jnp.log(new_total)
    attended_low = attended.astype(jnp.bfloat16).reshape(row_count, model_width)
    attn_out = jnp.dot(
        attended_low, weight_out, preferred_element_type=jnp.float32
    ) + bias_out.astype(jnp.float32)
    mlp_full = (
        lax.all_gather(ln2_gain, ("dp", "seq"), axis=0, tiled=True),
        lax.all_gather(ln2_bias, ("dp", "seq"), axis=0, tiled=True),
        lax.all_gather(fc1_weight, ("dp", "seq"), axis=0, tiled=True),
        lax.all_gather(fc1_bias, ("dp", "seq"), axis=0, tiled=True),
        lax.all_gather(fc2_weight, ("dp", "seq"), axis=0, tiled=True),
        lax.all_gather(fc2_bias, ("dp", "seq"), axis=0, tiled=True),
    )
    gain_two, bias_two, weight_up, bias_up, weight_down, bias_down = mlp_full
    normed_two, norm_back_two = jax.vjp(
        layer_norm, flat_in, gain_two.astype(jnp.float32), bias_two.astype(jnp.float32)
    )
    act_two = normed_two.astype(jnp.bfloat16)
    hidden = jnp.dot(act_two, weight_up, preferred_element_type=jnp.float32) + bias_up.astype(
        jnp.float32
    )
    activated, gelu_back = jax.vjp(gelu_exact, hidden)
    act_hidden = activated.astype(jnp.bfloat16)
    mlp_out = jnp.dot(
        act_hidden, weight_down, preferred_element_type=jnp.float32
    ) + bias_down.astype(jnp.float32)
    mixed = (
        (flat_in + attn_out + mlp_out)
        .astype(jnp.bfloat16)
        .reshape(group_size, block_size, model_width)
    )
    back_up, back_down = (
        lax.all_gather(fc1_weight, ("dp", "seq"), axis=0, tiled=True),
        lax.all_gather(fc2_weight, ("dp", "seq"), axis=0, tiled=True),
    )
    back_qkv, back_out = (
        lax.all_gather(qkv_weight, ("dp", "seq"), axis=0, tiled=True),
        lax.all_gather(out_weight, ("dp", "seq"), axis=0, tiled=True),
    )
    grad_out = cotangent.reshape(row_count, model_width)
    grad_float = grad_out.astype(jnp.float32)
    grad_down_weight = jnp.dot(act_hidden.T, grad_out, preferred_element_type=jnp.float32)
    grad_down_bias = jnp.sum(grad_float, axis=0)
    grad_activated = jnp.dot(grad_out, back_down.T, preferred_element_type=jnp.float32)
    (grad_hidden,) = gelu_back(grad_activated)
    grad_hidden_low = grad_hidden.astype(jnp.bfloat16)
    grad_up_weight = jnp.dot(act_two.T, grad_hidden_low, preferred_element_type=jnp.float32)
    grad_up_bias = jnp.sum(grad_hidden_low.astype(jnp.float32), axis=0)
    grad_act_two = jnp.dot(grad_hidden_low, back_up.T, preferred_element_type=jnp.float32)
    grad_in_two, grad_gain_two, grad_bias_two = norm_back_two(grad_act_two)
    mlp_shards = (
        lax.psum_scatter(grad_gain_two, ("dp", "seq"), scatter_dimension=0, tiled=True),
        lax.psum_scatter(grad_bias_two, ("dp", "seq"), scatter_dimension=0, tiled=True),
        lax.psum_scatter(grad_up_weight, ("dp", "seq"), scatter_dimension=0, tiled=True),
        lax.psum_scatter(grad_up_bias, ("dp", "seq"), scatter_dimension=0, tiled=True),
        lax.psum_scatter(grad_down_weight, ("dp", "seq"), scatter_dimension=0, tiled=True),
        lax.psum_scatter(grad_down_bias, ("dp", "seq"), scatter_dimension=0, tiled=True),
    )
    grad_out_weight = jnp.dot(attended_low.T, grad_out, preferred_element_type=jnp.float32)
    grad_out_bias = jnp.sum(grad_float, axis=0)
    grad_attended = jnp.dot(grad_out, back_out.T, preferred_element_type=jnp.float32)
    grad_low = grad_attended.reshape(group_size, block_size, HEADS, HD).astype(jnp.bfloat16)
    delta = jnp.sum(grad_low.astype(jnp.float32) * attended, axis=-1)
    key_piece = lax.all_gather(key_low, "seq", axis=1, tiled=True)
    value_piece = lax.all_gather(value_low, "seq", axis=1, tiled=True)
    seg_piece = lax.all_gather(segments, "seq", axis=1, tiled=True)
    key_pos = jnp.arange(seg_piece.shape[1], dtype=jnp.int32)
    allowed = visible(segments, local_pos, seg_piece, key_pos)
    scores = jnp.einsum("gqhd,gkhd->gqhk", query_low, key_piece, preferred_element_type=jnp.float32)
    chances = jnp.where(allowed, jnp.exp(scores - log_total[..., None]), 0.0)
    grad_chances = jnp.einsum(
        "gqhd,gkhd->gqhk", grad_low, value_piece, preferred_element_type=jnp.float32
    )
    grad_scores = (chances * (grad_chances - delta[..., None])).astype(jnp.bfloat16)
    grad_query = jnp.einsum(
        "gqhk,gkhd->gqhd", grad_scores, key_piece, preferred_element_type=jnp.float32
    )
    query_piece = lax.all_gather(query_low, "seq", axis=1, tiled=True)
    grad_piece = lax.all_gather(grad_low, "seq", axis=1, tiled=True)
    lse_piece = lax.all_gather(log_total.astype(jnp.bfloat16), "seq", axis=1, tiled=True).astype(
        jnp.float32
    )
    delta_piece = lax.all_gather(delta.astype(jnp.bfloat16), "seq", axis=1, tiled=True).astype(
        jnp.float32
    )
    seg_piece = lax.all_gather(segments, "seq", axis=1, tiled=True)
    query_pos = jnp.arange(seg_piece.shape[1], dtype=jnp.int32)
    allowed = visible(seg_piece, query_pos, segments, local_pos)
    scores = jnp.einsum("gqhd,gkhd->gqhk", query_piece, key_low, preferred_element_type=jnp.float32)
    chances = jnp.where(allowed, jnp.exp(scores - lse_piece[..., None]), 0.0)
    new_value = jnp.einsum(
        "gqhk,gqhd->gkhd",
        chances.astype(jnp.bfloat16),
        grad_piece,
        preferred_element_type=jnp.float32,
    )
    grad_chances = jnp.einsum(
        "gqhd,gkhd->gqhk", grad_piece, value_low, preferred_element_type=jnp.float32
    )
    grad_scores = (chances * (grad_chances - delta_piece[..., None])).astype(jnp.bfloat16)
    new_key = jnp.einsum(
        "gqhk,gqhd->gkhd", grad_scores, query_piece, preferred_element_type=jnp.float32
    )
    grad_query_raw, grad_key_raw = turn_back((grad_query, new_key))
    grad_qkv_low = (
        jnp.stack([grad_query_raw, grad_key_raw, new_value], axis=2)
        .reshape(row_count, 3 * model_width)
        .astype(jnp.bfloat16)
    )
    grad_qkv_weight = jnp.dot(act_one.T, grad_qkv_low, preferred_element_type=jnp.float32)
    grad_qkv_bias = jnp.sum(grad_qkv_low.astype(jnp.float32), axis=0)
    grad_act_one = jnp.dot(grad_qkv_low, back_qkv.T, preferred_element_type=jnp.float32)
    grad_in_one, grad_gain_one, grad_bias_one = norm_back_one(grad_act_one)
    attention_shards = (
        lax.psum_scatter(grad_gain_one, ("dp", "seq"), scatter_dimension=0, tiled=True),
        lax.psum_scatter(grad_bias_one, ("dp", "seq"), scatter_dimension=0, tiled=True),
        lax.psum_scatter(grad_qkv_weight, ("dp", "seq"), scatter_dimension=0, tiled=True),
        lax.psum_scatter(grad_qkv_bias, ("dp", "seq"), scatter_dimension=0, tiled=True),
        lax.psum_scatter(grad_out_weight, ("dp", "seq"), scatter_dimension=0, tiled=True),
        lax.psum_scatter(grad_out_bias, ("dp", "seq"), scatter_dimension=0, tiled=True),
    )
    grad_tokens = (
        (grad_float + grad_in_one + grad_in_two)
        .astype(jnp.bfloat16)
        .reshape(group_size, block_size, model_width)
    )
    return (
        mixed,
        grad_tokens,
        attention_shards[0],
        attention_shards[1],
        attention_shards[2],
        attention_shards[3],
        attention_shards[4],
        attention_shards[5],
        mlp_shards[0],
        mlp_shards[1],
        mlp_shards[2],
        mlp_shards[3],
        mlp_shards[4],
        mlp_shards[5],
    )


GROUP = ("z", "y")
PEERS = ("x", "c")
EVERY = ("z", "y", "x", "c")
TURNS = 2 * CORES
ORDER = (0, 1, 7, 2, 6, 3, 5, 4)
LIMIT = 56 * 1024 * 1024
SMALL = 26 * 1024 * 1024
bf16, f32 = jnp.bfloat16, jnp.float32


def whole_ref():
    return pl.BlockSpec(memory_space=pltpu.VMEM)


def in_place():
    return pl.BlockSpec(memory_space=pl.ANY)


def call(
    kernel, results, inputs, operands, outputs, grid=(), prefetch=0, aliases=None, scratch=(), limit=LIMIT
):
    return pl.pallas_call(
        kernel,
        out_shape=[jax.ShapeDtypeStruct(*result) for result in results],
        grid_spec=pltpu.PrefetchScalarGridSpec(
            num_scalar_prefetch=prefetch, grid=grid, in_specs=inputs, out_specs=outputs, scratch_shapes=scratch
        ),
        input_output_aliases=aliases or {},
        compiler_params=pltpu.CompilerParams(vmem_limit_bytes=limit),
        cost_estimate=pl.CostEstimate(flops=1, bytes_accessed=1, transcendentals=0),
    )(*operands)


class Line:
    def __init__(self):
        self.last = ()

    def __call__(self, function, *operands, wait=()):
        operands = lax.optimization_barrier((operands, self.last, wait))[0]
        results = function(*operands)
        self.last = tuple(jax.tree.leaves(results))
        return results

    def hold(self, values):
        return lax.optimization_barrier((values, self.last))[0]


def after(value, *others):
    return lax.optimization_barrier((value, *others))[0]


def ring_perm(shift):
    depth, width = lax.axis_size("z"), lax.axis_size("y")
    places = [z * width for z in range(depth)] + [z * width + 1 for z in reversed(range(depth))]
    count = len(places)
    return [(places[i], places[(i + shift) % count]) for i in range(count)]


class Gather:
    def __init__(self, block):
        self.held = {0: [block]}
        self.ahead = self.behind = block
        self.done = 0

    def step(self, line, *others):
        half = len(ORDER) // 2
        ahead, behind = line.hold((self.ahead, self.behind, *others))[:2]
        self.done += 1
        if self.done < half:
            self.behind = lax.ppermute(behind, GROUP, ring_perm(1))
            self.ahead = lax.ppermute(ahead, GROUP, ring_perm(-1))
            self.held[len(ORDER) - self.done] = [self.behind]
            self.held[self.done] = [self.ahead]
        else:
            cut = behind.shape[0] // 2
            self.held[half] = [
                lax.ppermute(behind[:cut], GROUP, ring_perm(1)),
                lax.ppermute(ahead[cut:], GROUP, ring_perm(-1)),
            ]


def swap(values, axis):
    return lax.ppermute(values, axis, [(0, 1), (1, 0)])


def dot_f32(left, right, dims=((1,), (0,))):
    return lax.dot_general(left, right, (dims, ((), ())), preferred_element_type=f32)


def tile_spec(shape, index):
    return pl.BlockSpec(shape, lambda i, *scalars: index(i))


def same(shape):
    return tile_spec(shape, lambda i: (0,) * len(shape))


def spread_kernel(up, qkv, result):
    share, _, columns = result.shape
    tile = columns - 3 * HD
    for t in range(share):
        for i in range(3):
            at = (i * share + t) * HD
            result[t, :, i * HD : (i + 1) * HD] = qkv[:, at : at + HD]
        result[t, :, 3 * HD :] = up[:, t * tile : (t + 1) * tile]


def spread(up, qkv, share):
    rows, columns = up.shape
    return call(
        spread_kernel,
        [((share, rows, 3 * HD + columns // share), bf16)],
        [whole_ref()] * 2,
        (up, qkv),
        [whole_ref()],
    )[0]


def assemble_kernel(mine, *refs):
    sources, result = refs[:TURNS], refs[TURNS]
    for entry in range(result.shape[0]):
        for turn in range(TURNS):
            result[entry, pl.ds(mine[0] ^ turn, 1)] = sources[turn][entry : entry + 1]


def assemble(pieces, mine, step=2):
    entries, rows, columns = pieces[0].shape
    step = min(step, entries)
    return call(
        assemble_kernel,
        [((entries, TURNS, rows, columns), pieces[0].dtype)],
        [tile_spec((step, rows, columns), lambda i: (i, 0, 0))] * TURNS,
        (mine, *pieces),
        [tile_spec((step, TURNS, rows, columns), lambda i: (i, 0, 0, 0))],
        grid=(entries // step,),
        prefetch=1,
    )[0].reshape(entries * TURNS * rows, columns)


def settle_kernel(depth, peer, *refs):
    sources, result = refs[:-1], refs[-1]
    share = sources[0].shape[0]
    for shift, source in enumerate(sources):
        at = ((depth[0] + len(sources) - shift) % len(sources)) * share
        for j in range(share):
            result[pl.ds(at + (j ^ peer[0]), 1)] = source[j : j + 1]


def settle(depth, peer, *sources):
    shape = (len(sources) * sources[0].shape[0], *sources[0].shape[1:])
    return call(
        settle_kernel,
        [(shape, sources[0].dtype)],
        [same(source.shape) for source in sources],
        (depth, peer, *sources),
        [same(shape)],
        grid=(1,),
        prefetch=2,
    )[0]


def norm_kernel(count, affine, *refs):
    pieces, (one, two, mean_ref, scale_ref, one_turned, two_turned) = refs[:count], refs[-6:]
    values = stacked(pieces).astype(f32)
    mean = jnp.mean(values, axis=-1, keepdims=True)
    centered = values - mean
    scale = lax.rsqrt(jnp.mean(centered * centered, axis=-1, keepdims=True) + epsilon)
    normal = centered * scale
    for at, result, turned in ((0, one, one_turned), (2, two, two_turned)):
        act = (normal * affine[at : at + 1] + affine[at + 1 : at + 2]).astype(bf16)
        result[...] = act
        turned[...] = act.T.reshape(turned.shape)
    mean_ref[...] = mean
    scale_ref[...] = scale


def norm_block(at, pieces, affine, kept, slim):
    block, model = sum(piece.shape[0] for piece in pieces), pieces[0].shape[1]
    rows = len(ORDER) * block
    turned = (model // (TURNS * slim), 2, CORES, slim)
    results = [
        ((rows, model), bf16),
        ((rows, model), bf16),
        ((rows, 1), f32),
        ((rows, 1), f32),
        ((*turned, rows), bf16),
        ((*turned, rows), bf16),
    ]
    outputs = [pl.BlockSpec((block, shape[1]), lambda i: (at, 0)) for shape, _ in results[:4]]
    outputs += [pl.BlockSpec((*turned, block), lambda i: (0, 0, 0, 0, at))] * 2
    operands = [affine, *pieces]
    inputs = [whole_ref()] * len(operands)
    aliases = {}
    if kept is not None:
        aliases = {len(operands) + i: i for i in range(len(results))}
        operands += kept
        inputs += [in_place()] * len(results)
    return call(
        functools.partial(norm_kernel, len(pieces)), results, inputs, operands, outputs, grid=(1,), aliases=aliases
    )


def rotary_tables(places):
    half_rot = ROT // 2
    frequencies = 10000.0 ** (
        -(jnp.arange(half_rot, dtype=jnp.int32).astype(f32) * 2.0 / ROT)
    )
    turned = places.astype(f32)[:, None] * frequencies[None, :]
    cosines, sines = jnp.cos(turned), jnp.sin(turned)
    rest = jnp.zeros((places.shape[0], 128 - ROT), f32)
    none = jnp.zeros_like(sines)
    return (
        jnp.concatenate([cosines, cosines, rest + 1.0], axis=1),
        jnp.concatenate([sines, none, rest], axis=1),
        jnp.concatenate([none, sines, rest], axis=1),
    )


def rotate(values, tables, sign):
    cosines, first, second = tables
    half_rot = ROT // 2
    low = values[:, :128]
    ahead = pltpu.roll(low, 128 - half_rot, 1)
    behind = pltpu.roll(low, half_rot, 1)
    low = low * cosines + sign * (behind * second - ahead * first)
    return jnp.concatenate([low, values[:, 128:]], axis=1)


def qkv_kernel(depth_of, far_of, core, act, weight, bias, cosines, first, second, *results):
    qkv = jnp.dot(act[...], weight[...], preferred_element_type=f32) + bias[...]
    tables = (cosines[...], first[...], second[...])
    query = (rotate(qkv[:, :HD], tables, 1.0) * 0.0625).astype(bf16)
    key = rotate(qkv[:, HD : 2 * HD], tables, 1.0).astype(bf16)
    value = qkv[:, 2 * HD :].astype(bf16)
    parts = act.shape[0] // results[0].shape[2]
    start = pl.program_id(0) * parts
    spill(jnp.concatenate([query, key, value], axis=1), depth_of, far_of, core, start, results)


def spill(values, depth_of, far_of, core, start, results):
    block = results[0].shape[2]
    for part in range(values.shape[0] // block):
        at = start + part
        rows = values[None, None, part * block : (part + 1) * block]
        owner, low = depth_of[at] // 2, depth_of[at] % 2
        for result, mine in zip(results, (True, False)):

            @pl.when((owner == core[0]) == mine)
            def _():
                result[pl.ds(low, 1), pl.ds(far_of[at], 1)] = rows


def project(act, weight, bias, tables, depth_of, far_of, core, block):
    rows, model = act.shape
    columns = weight.shape[1]
    step = 4 * block
    return call(
        qkv_kernel,
        [((2, 2, block, columns), bf16)] * 2,
        [tile_spec((step, model), lambda i: (i, 0)), same((model, columns)), same((1, columns))]
        + [tile_spec((step, 128), lambda i: (i, 0))] * 3,
        (depth_of, far_of, core, act, weight, bias, *tables),
        [same((2, 2, block, columns))] * 2,
        grid=(rows // step,),
        prefetch=3,
    )


def place_kernel(depth_of, far_of, core, mine, came, result, *turned):
    block = result.shape[1]
    for at in range(result.shape[0]):
        for source, own in ((mine, True), (came, False)):

            @pl.when((depth_of[at] // 2 == core[0]) == own)
            def _():
                values = source[pl.ds(depth_of[at] % 2, 1), pl.ds(far_of[at], 1)][0, 0]
                result[at] = values
                for other in turned:
                    other[:, at * block : (at + 1) * block] = values.T


def place(mine, came, depth_of, far_of, core, turn=False):
    low, far, block, columns = mine.shape
    count = 2 * low * far
    shapes = [(count, block, columns)] + [(columns, count * block)] * turn
    placed, *turned = call(
        place_kernel,
        [(shape, bf16) for shape in shapes],
        [same(mine.shape)] * 2,
        (depth_of, far_of, core, mine, came),
        [same(shape) for shape in shapes],
        grid=(1,),
        prefetch=3,
        limit=SMALL,
    )
    return (placed.reshape(count * block, columns), *turned)


def pairs(ref, rows):
    return [(far, slice(at, at + rows)) for far in range(ref.shape[1]) for at in range(0, ref.shape[2], rows)]


def gathered(mine, came, even, seq, start, rows):
    parts = []
    for far, at in pairs(mine, rows):
        own, other = (ref[seq, far, at, start : start + HD] for ref in (mine, came))
        parts += [jnp.where(even, own, other), jnp.where(even, other, own)]
    return jnp.concatenate(parts, axis=0)


def scattered(mine, sent, even, seq, start, rows, values):
    for i, (far, at) in enumerate(pairs(mine, rows)):
        first, second = (values[(2 * i + k) * rows : (2 * i + k + 1) * rows] for k in range(2))
        mine[seq, far, at, start : start + HD] = jnp.where(even, first, second)
        sent[seq, far, at, start : start + HD] = jnp.where(even, second, first)


def chances_of(query, key, segments):
    scores = dot_f32(query, key, ((1,), (1,)))
    col_seg = jnp.broadcast_to(segments, scores.shape)
    row_seg = col_seg.T
    row_pos = lax.broadcasted_iota(jnp.int32, scores.shape, 0)
    col_pos = lax.broadcasted_iota(jnp.int32, scores.shape, 1)
    scores = jnp.where((col_pos <= row_pos) & (col_seg == row_seg), scores, masked_value)
    weights = jnp.exp(scores - jnp.max(scores, axis=-1, keepdims=True))
    return weights / jnp.sum(weights, axis=-1, keepdims=True)


def forward_kernel(rows, core, segments, mine, came, kept, sent):
    even = core[0] == 0
    for seq in range(mine.shape[0]):
        query, key, value = (gathered(mine, came, even, seq, i * HD, rows) for i in range(3))
        chances = chances_of(query, key, segments[seq])
        scattered(kept, sent, even, seq, 0, rows, dot_f32(chances.astype(bf16), value).astype(bf16))


def backward_kernel(
    rows, core, segments, cosines, first, second, mine, came, grad_mine, grad_came, kept, sent
):
    even = core[0] == 0
    tables = (cosines[...], first[...], second[...])
    for seq in range(mine.shape[0]):
        query, key, value = (gathered(mine, came, even, seq, i * HD, rows) for i in range(3))
        grad = gathered(grad_mine, grad_came, even, seq, 0, rows)
        chances = chances_of(query, key, segments[seq])
        chances_low = chances.astype(bf16)
        grad_chances = dot_f32(grad, value, ((1,), (1,)))
        delta = jnp.sum(chances_low.astype(f32) * grad_chances, axis=-1, keepdims=True)
        grad_scores = (chances * (grad_chances - delta)).astype(bf16)
        grad_query = dot_f32(grad_scores, key)
        grad_key = dot_f32(grad_scores, query, ((0,), (0,)))
        grad_value = dot_f32(chances_low, grad, ((0,), (0,)))
        for i, part in enumerate(
            (rotate(grad_query * 0.0625, tables, -1.0), rotate(grad_key, tables, -1.0), grad_value)
        ):
            scattered(kept, sent, even, seq, i * HD, rows, part.astype(bf16))


def attend(kernel, rows, columns, core, given, *arrays):
    operands = (*given, *arrays)
    shape = (*arrays[0].shape[:3], columns)
    return call(
        functools.partial(kernel, rows),
        [(shape, bf16)] * 2,
        [same(a.shape) for a in operands],
        (core, *operands),
        [same(shape)] * 2,
        grid=(1,),
        prefetch=1,
        limit=SMALL,
    )


def widen_kernel(act, weight, bias, activated, slope, turned):
    hidden = jnp.dot(act[...], weight[...], preferred_element_type=f32) + bias[...]
    cdf = 0.5 * (1.0 + lax.erf(hidden * math.sqrt(0.5)))
    result = (hidden * cdf).astype(bf16)
    activated[...] = result
    turned[...] = result.T
    slope[...] = (cdf + hidden * jnp.exp(-0.5 * hidden * hidden) * (1.0 / math.sqrt(2.0 * math.pi))).astype(bf16)


def widen(act, weight, bias, tile=256):
    rows, model = act.shape
    columns = weight.shape[1]
    return call(
        widen_kernel,
        [((rows, columns), bf16), ((rows, columns), bf16), ((columns, rows), bf16)],
        [
            same((rows, model)),
            tile_spec((model, tile), lambda i: (0, i)),
            tile_spec((1, tile), lambda i: (0, i)),
        ],
        (act, weight, bias),
        [tile_spec((rows, tile), lambda i: (0, i))] * 2 + [tile_spec((tile, rows), lambda i: (i, 0))],
        grid=(columns // tile,),
    )


def stacked(refs):
    return jnp.concatenate([ref[...] for ref in refs], axis=0)


def narrow_kernel(weight, slope, *refs):
    blocks, (result, sums) = refs[:-2], refs[-2:]
    grad = dot_f32(stacked(blocks), weight[...], ((1,), (1,))) * slope[...].astype(f32)
    grad = grad.astype(bf16)
    result[...] = grad
    sums[...] = jnp.sum(grad.astype(f32), axis=0, keepdims=True)


def narrow(blocks, weight, slope, tile=512):
    rows, columns = slope.shape
    model = weight.shape[1]
    return call(
        narrow_kernel,
        [((rows, columns), bf16), ((1, columns), f32)],
        [tile_spec((tile, model), lambda i: (i, 0)), tile_spec((rows, tile), lambda i: (0, i))]
        + [same(piece.shape) for piece in blocks],
        (weight, slope, *blocks),
        [tile_spec((rows, tile), lambda i: (0, i)), tile_spec((1, tile), lambda i: (0, i))],
        grid=(columns // tile,),
        limit=SMALL,
    )


def head_kernel(depth_of, far_of, core, weight, *refs):
    blocks, results, total = refs[:-3], refs[-3:-1], refs[-1]
    part = dot_f32(stacked(blocks), weight[...], ((1,), (1,)))
    step = pl.program_id(0)

    @pl.when(step == 0)
    def _():
        total[...] = part

    @pl.when(step > 0)
    def _():
        total[...] += part

    @pl.when(step == pl.num_programs(0) - 1)
    def _():
        spill(total[...].astype(bf16), depth_of, far_of, core, 0, results)


def head_grads(blocks, weight, depth_of, far_of, core, block, tile=512):
    rows = sum(piece.shape[0] for piece in blocks)
    return call(
        head_kernel,
        [((2, 2, block, HD), bf16)] * 2,
        [tile_spec((piece.shape[0], tile), lambda i: (0, i)) for piece in (weight, *blocks)],
        (depth_of, far_of, core, weight, *blocks),
        [same((2, 2, block, HD))] * 2,
        grid=(weight.shape[1] // tile,),
        prefetch=3,
        scratch=[pltpu.VMEM((rows, HD), f32)],
        limit=SMALL,
    )


def across(total, half, near, far, slots=False):
    first, second = total[:, 0], total[:, 1]
    low = half[0] == 0
    near[...] = jnp.where(low, first, second).astype(bf16).reshape(near.shape)
    other = jnp.where(low, second, first).astype(bf16)
    if slots:
        far[pl.ds(1 - half[0], 1)] = other[None]
    else:
        far[...] = other.reshape(far.shape)


def rows_kernel(near, slots, core, half, act, grad, *refs):
    entries, _, _, rows, tokens = act.shape
    total = dot_f32(act[...].reshape(entries * 2 * rows, tokens), grad[...])
    total = total.reshape(entries, 2, rows, grad.shape[1])
    if near:
        came, kept, sent = refs
        across(total + came[...].astype(f32), half, kept, sent, slots)
    else:
        refs[0][...] = total.astype(bf16)


def rows_grad(turned, grad, core, half, came=None, step=4, slots=False):
    entries, _, _, rows, tokens = turned.shape
    columns = grad.shape[1]
    near = came is not None
    spec = tile_spec((step, 2, rows, columns), lambda i: (i, 0, 0, 0))
    inputs = [
        pl.BlockSpec(
            (step, 2, 1, rows, tokens), lambda i, c, x: (i, 0, c[0] if near else 1 - c[0], 0, 0)
        ),
        same((tokens, columns)),
    ]
    if near:
        results = [((entries, rows, columns), bf16)] * 2
        outputs = [tile_spec((step, rows, columns), lambda i: (i, 0, 0))] * 2
        if slots:
            results[1] = ((2, entries, rows, columns), bf16)
            outputs[1] = tile_spec((2, step, rows, columns), lambda i: (0, i, 0, 0))
    else:
        results, outputs = [((entries, 2, rows, columns), bf16)], [spec]
    return call(
        functools.partial(rows_kernel, near, slots),
        results,
        inputs + [spec] * near,
        (core, half, turned, grad) + (came,) * near,
        outputs,
        grid=(entries // step,),
        prefetch=2,
        limit=SMALL,
    )


def down_kernel(near, core, half, attended, activated, *refs):
    count = 3 if near else 1
    blocks, refs = refs[:-count], refs[-count:]
    parts = [ref[x, 0] for x in range(2) for ref in (attended, activated)]
    total = dot_f32(jnp.concatenate(parts, axis=0), stacked(blocks))
    total = total.reshape(1, 2, total.shape[0] // 2, total.shape[1])
    if near:
        came, kept, sent = refs
        across(total + came[...][None].astype(f32), half, kept, sent)
    else:
        refs[0][...] = total[0].astype(bf16)


def down_grad(attended, activated, blocks, core, half, came=None, tile=512):
    tokens = attended.shape[3]
    model = blocks[0].shape[1]
    rows = attended.shape[2] + activated.shape[2]
    near = came is not None
    spec = tile_spec((2, rows, tile), lambda i: (0, 0, i))
    inputs = [
        pl.BlockSpec(
            (2, 1, turned.shape[2], tokens), lambda i, c, x: (0, c[0] if near else 1 - c[0], 0, 0)
        )
        for turned in (attended, activated)
    ]
    inputs += [tile_spec((piece.shape[0], tile), lambda i: (0, i)) for piece in blocks]
    if near:
        results = [((rows, model), bf16)] * 2
        outputs = [tile_spec((rows, tile), lambda i: (0, i))] * 2
    else:
        results, outputs = [((2, rows, model), bf16)], [spec]
    return call(
        functools.partial(down_kernel, near),
        results,
        inputs + [spec] * near,
        (core, half, attended, activated, *blocks) + (came,) * near,
        outputs,
        grid=(model // tile,),
        prefetch=2,
        limit=SMALL,
    )


def join_kernel(pieces, given, result, *sums):
    share = given.shape[0]
    width = result.shape[1] // (share * pieces)
    for t in range(share):
        for i in range(pieces):
            at = (i * share + t) * width
            result[:, at : at + width] = given[t, :, i * width : (i + 1) * width].astype(f32)
    for ref in sums:
        rows, columns = ref.shape
        ref[...] = jnp.sum(given[:, :rows, pieces * width : pieces * width + columns].astype(f32), axis=0)


def join(given, pieces, extra=None):
    share, rows, columns = given.shape
    results = [((rows, share * (columns - (extra[1] if extra else 0))), f32)]
    results += [(extra, f32)] if extra else []
    return call(
        functools.partial(join_kernel, pieces), results, [whole_ref()], (given,), [whole_ref()] * len(results), limit=SMALL)


def widen_rows_kernel(mine, came, extra, result):
    columns = mine.shape[2]
    result[:, :, :columns] = (mine[...].astype(f32) + came[...].astype(f32)).astype(bf16)
    result[:, :, columns:] = jnp.zeros((*result.shape[:2], result.shape[2] - columns), bf16)
    result[:, : extra.shape[1], columns:] = extra[...].astype(bf16)


def total_with(mine, came, extra):
    shape = (*mine.shape[:2], mine.shape[2] + extra.shape[2])
    operands = (mine, came, extra)
    return call(widen_rows_kernel, [(shape, bf16)], [whole_ref()] * 3, operands, [whole_ref()], limit=SMALL)[0]


def share_part(pull, first, count, block, lefts, rights, pieces, extras=(), tile=512):
    model = rights[0].shape[0 if pull else 1]
    depths = [right.shape[1 if pull else 0] for right in rights]
    operands, inputs = [], []
    for left, depth in zip(lefts, depths):
        for b in range(count):
            operands.append(left)
            inputs.append(tile_spec((block, depth), lambda i, b=b: (first + b, 0)))
    for right, depth in zip(rights, depths):
        operands.append(right)
        inputs.append(
            tile_spec((tile, depth), lambda i: (i, 0)) if pull else tile_spec((depth, tile), lambda i: (0, i))
        )
    given = 0
    if pull:
        gains, values, mean, scale = extras
        given = len(values)
        for row in (*gains, *values):
            operands.append(row)
            inputs.append(tile_spec((row.shape[0], tile), lambda i: (0, i)))
        for stat in (mean, scale):
            for b in range(count):
                operands.append(stat)
                inputs.append(tile_spec((block, 1), lambda i, b=b: (first + b, 0)))

    def kernel(*refs):
        refs = list(refs)

        def take(number):
            taken = refs[:number]
            del refs[:number]
            return taken

        left_a, left_b = stacked(take(count)), stacked(take(count))
        (right_a,), (right_b,) = take(1), take(1)
        dims = ((1,), (1,)) if pull else ((1,), (0,))
        part_a = dot_f32(left_a, right_a[...], dims)
        part_b = dot_f32(left_b, right_b[...], dims)
        if pull:
            (gains_ref,) = take(1)
            tokens = stacked(take(given)).astype(f32)
            normal = (tokens - stacked(take(count))) * stacked(take(count))
            (sums,) = take(1)
            sums[...] = jnp.concatenate(
                [
                    jnp.sum(part, axis=0, keepdims=True)
                    for part in (part_a * normal, part_a, part_b * normal, part_b)
                ]
                + [jnp.zeros((4, tile), f32)],
                axis=0,
            )
            total = part_a * gains_ref[0:1] + part_b * gains_ref[2:3]
        else:
            total = part_a + part_b
        for (start, rows, dtype), result in zip(pieces, refs):
            result[...] = total[start : start + rows].astype(dtype)

    results = [((rows, model), dtype) for _, rows, dtype in pieces]
    outputs = [tile_spec((rows, tile), lambda i: (0, i)) for _, rows, _ in pieces]
    if pull:
        results = [((8, model), f32)] + results
        outputs = [tile_spec((8, tile), lambda i: (0, i))] + outputs
    return call(
        kernel, results, inputs, operands, outputs, grid=(model // tile,), limit=LIMIT if pull else SMALL
    )


def early_pieces(block):
    cut = block // 2
    return [(2 * block, cut, bf16), (2 * block + cut, cut, bf16), (0, block, bf16), (block, block, bf16)]


def late_pieces(block):
    return [(i * block, block, bf16) for i in range(5)]


def all_pieces(block):
    return late_pieces(block) + [(5 * block + start, rows, dtype) for start, rows, dtype in early_pieces(block)]


def add_kernel(one, two, ahead, behind, *results):
    cut = ahead.shape[0]
    rows = one.shape[0]
    for mine, came, result, start in ((one, ahead, results[0], 0), (two, behind, results[1], rows - cut)):
        if cut < rows:
            result[...] = mine[...]
        at = slice(start, start + cut)
        result[at] = (mine[at].astype(f32) + came[...].astype(f32)).astype(bf16)


def add_incoming(one, two, ahead, behind, tile=1024):
    rows, model = one.shape
    return call(
        add_kernel,
        [(one.shape, bf16)] * 2,
        [tile_spec((a.shape[0], tile), lambda i: (0, i)) for a in (one, two, ahead, behind)],
        (one, two, ahead, behind),
        [tile_spec((rows, tile), lambda i: (0, i))] * 2,
        grid=(model // tile,), limit=SMALL)


class Scatter:
    def send(self, one, two):
        self.ahead = lax.ppermute(one, GROUP, ring_perm(1))
        self.behind = lax.ppermute(two, GROUP, ring_perm(-1))

    def step(self, line, one, two, wait=()):
        self.send(*line(add_incoming, one, two, self.ahead, self.behind, wait=wait))


def total_slot_kernel(half, mine, came, result):
    result[...] = (mine[...].astype(f32) + came[...].reshape(mine.shape).astype(f32)).astype(bf16)


def total_slot(half, mine, came, step=2):
    entries, rows, columns = mine.shape
    block = (entries // step, rows, columns)
    return call(
        total_slot_kernel,
        [(mine.shape, bf16)],
        [
            tile_spec(block, lambda i: (i, 0, 0)),
            pl.BlockSpec((1, *block), lambda i, x: (1 - x[0], i, 0, 0)),
        ],
        (half, mine, came),
        [tile_spec(block, lambda i: (i, 0, 0))],
        grid=(step,),
        prefetch=1, limit=SMALL)[0]


def total_kernel(mine, came, *results):
    total = mine[...].astype(f32) + came[...].astype(f32)
    at = 0
    for result in results:
        rows = result.shape[0]
        result[...] = total[at : at + rows].astype(result.dtype)
        at += rows


def total_rows(mine, came, pieces):
    tail = mine.shape[1:]
    steps = 2
    tile = tail[:-1] + (tail[-1] // steps,)

    def spec(rows):
        return tile_spec((rows, *tile), lambda i: (0,) * len(tile) + (i,))

    return call(
        total_kernel,
        [((rows, *tail), dtype) for rows, dtype in pieces],
        [spec(mine.shape[0])] * 2,
        (mine, came),
        [spec(rows) for rows, _ in pieces],
        grid=(steps,), limit=SMALL)


def apart(values, half, kept, sent):
    cut = values.shape[0] // 2
    low = half[0] == 0
    first, second = values[:cut], values[cut:]
    kept[...] = jnp.where(low, first, second).astype(kept.dtype)
    sent[...] = jnp.where(low, second, first).astype(sent.dtype)


def mixed_kernel(half, own, ahead, behind, tokens, bias_one, bias_two, kept, sent):
    total = own[...].astype(f32) + ahead[...].astype(f32) + behind[...].astype(f32) + tokens[...].astype(f32)
    apart(total + bias_one[...] + bias_two[...], half, kept, sent)


def by_rows(kernel, half, operands, tokens):
    rows, model = tokens.shape
    return call(
        kernel,
        [((rows // 2, model), bf16)] * 2,
        [tile_spec((rows, 1), lambda i: (0, 0)) if a.shape[1] == 1 else same(a.shape) for a in operands],
        (half, *operands),
        [same((rows // 2, model))] * 2,
        grid=(1,),
        prefetch=1, limit=SMALL)


def mixed_rows(half, *operands):
    return by_rows(mixed_kernel, half, operands, operands[3])


def vectors_kernel(share, early, late, grad, grad_qkv, up_sum, result):
    result[...] = jnp.zeros_like(result)
    result[:4] = early[:4] + late[:4]
    result[4:5] = jnp.sum(grad[...].astype(f32), axis=0, keepdims=True)
    qkv_sum = jnp.sum(grad_qkv[...].astype(f32), axis=0, keepdims=True)
    for i in range(3):
        at = pl.multiple_of(share[0] * HD, HD)
        result[5 + i : 6 + i, pl.ds(at, HD)] = qkv_sum[:, i * HD : (i + 1) * HD]
    columns = up_sum.shape[1]
    each = result.shape[1] // columns
    at = pl.multiple_of((share[0] % each) * columns, columns)
    result[pl.ds(8 + share[0] // each, 1), pl.ds(at, columns)] = up_sum[...]


def vectors(share, early, late, grad, grad_qkv, up_sum):
    operands = (early, late, grad, grad_qkv, up_sum)
    return call(
        vectors_kernel,
        [((16, early.shape[1]), f32)],
        [same(a.shape) for a in operands],
        (share, *operands),
        [same((16, early.shape[1]))],
        grid=(1,),
        prefetch=1, limit=SMALL)[0]


def sum_kernel(*refs):
    total = refs[0][...]
    for ref in refs[1:-1]:
        total = total + ref[...]
    refs[-1][...] = total


def sum_arrays(*arrays):
    return call(
        sum_kernel, [(arrays[0].shape, f32)], [whole_ref()] * len(arrays), arrays, [whole_ref()], limit=SMALL)[0]


def finish_kernel(half, own, ahead, behind, tokens, grad, mean, scale, kept, sent):
    pulled = own[...].astype(f32) + ahead[...].astype(f32) + behind[...].astype(f32)
    normal = (tokens[...].astype(f32) - mean[...]) * scale[...]
    inner = (
        pulled
        - jnp.mean(pulled, axis=-1, keepdims=True)
        - normal * jnp.mean(pulled * normal, axis=-1, keepdims=True)
    )
    apart(grad[...].astype(f32) + scale[...] * inner, half, kept, sent)


def finish(half, *operands):
    return by_rows(finish_kernel, half, operands, operands[3])


def trade_kernel(half, *refs):
    count = len(refs) // 3
    low = half[0] == 0
    for values, came, result in zip(refs[:count], refs[count : 2 * count], refs[2 * count :]):
        rows = came.shape[0]
        own = values[pl.ds(half[0], 1)][0]
        result[:rows] = jnp.where(low, own, came[...])
        result[rows:] = jnp.where(low, came[...], own)


def trade(half, arrays, came):
    shapes = [(2 * piece.shape[0], piece.shape[1]) for piece in came]
    return call(
        trade_kernel,
        [(shape, bf16) for shape in shapes],
        [same(a.shape) for a in (*arrays, *came)],
        (half, *arrays, *came),
        [same(shape) for shape in shapes],
        grid=(1,),
        prefetch=1,
    )


def in_order_kernel(half, *refs):
    count = len(refs) // 3
    for own, came, result in zip(refs[:count], refs[count : 2 * count], refs[2 * count :]):
        low = half[0] == 0
        result[0] = jnp.where(low, own[...], came[...])
        result[1] = jnp.where(low, came[...], own[...])


def in_order(half, own, came):
    operands = (*own, *came)
    return call(
        in_order_kernel,
        [((2, *a.shape), a.dtype) for a in own],
        [same(a.shape) for a in operands],
        (half, *operands),
        [same((2, *a.shape)) for a in own],
        grid=(1,),
        prefetch=1, limit=SMALL)


def scalar(value):
    return jnp.reshape(value, (1,)).astype(jnp.int32)


def grouped(
    tokens,
    segments,
    ln1_gain,
    ln1_bias,
    qkv_weight,
    qkv_bias,
    out_weight,
    out_bias,
    ln2_gain,
    ln2_bias,
    fc1_weight,
    fc1_bias,
    fc2_weight,
    fc2_bias,
    cotangent,
):
    depth, width = lax.axis_size("z"), lax.axis_size("y")
    share = depth * width
    devices = share * TURNS
    z, y, x, c = (lax.axis_index(name) for name in EVERY)
    t = z * width + y
    mine = x * CORES + c
    r = jnp.where(y == 0, z, 2 * depth - 1 - z)
    seqs, rows, model = tokens.shape
    block = seqs * rows
    slim = ln1_gain.shape[0]
    hidden = fc2_weight.shape[0] * TURNS
    line = Line()

    sent = line(lambda up, qkv: spread(up, qkv, share), fc1_weight, qkv_weight)
    columns = lax.all_to_all(sent, GROUP, 0, 0, tiled=True)

    down_out = (out_weight[None], fc2_weight[None])
    down_out_near = [swap(piece, "c") for piece in line.hold(down_out)]
    came = [
        swap(lax.dynamic_index_in_dim(rows_of, 1 - x, 0, keepdims=False), "x")
        for rows_of in line.hold((tokens, cotangent))
    ]

    pieces = (
        ln1_gain,
        ln1_bias,
        ln2_gain,
        ln2_bias,
        out_bias,
        fc2_bias,
        qkv_bias,
        fc1_bias,
        segments.reshape(-1).astype(bf16),
    )
    ends = [0]
    for piece in pieces:
        ends.append(ends[-1] + piece.shape[0])
    packed = jnp.concatenate(line.hold(pieces))
    packed = jnp.pad(packed, (0, -ends[-1] % 1024)).reshape(1, -1, 128)
    for axis in ("c", "x", "y"):
        packed = jnp.concatenate([packed, swap(packed, axis)], axis=0)
    packed = [packed] + [
        lax.ppermute(packed, "z", [(i, (i + shift) % depth) for i in range(depth)]) for shift in range(1, depth)
    ]
    steps = (r + jnp.array(ORDER, jnp.int32)) % share
    far_of = (steps >= depth).astype(jnp.int32)
    depth_of = jnp.where(far_of == 1, 2 * depth - 1 - steps, steps)
    within = (jnp.arange(2, dtype=jnp.int32) * CORES + c)[:, None] * rows + jnp.arange(rows, dtype=jnp.int32)
    token_pos = far_of[:, None] * (TURNS * rows) + within.reshape(1, -1)
    token_tables = line(rotary_tables, token_pos.reshape(-1))
    seq_tables = line(rotary_tables, jnp.arange(rows * width * TURNS, dtype=jnp.int32))

    my_rows, my_grad = line(trade, scalar(x), (tokens, cotangent), came, wait=packed[0])
    down_out_far = [swap(piece, "x") for piece in line.hold(down_out)]
    packed = line(settle, scalar(z), scalar(y * TURNS + mine), *packed, wait=down_out_near).reshape(devices, -1)
    down_out_last = [swap(piece, "c") for piece in line.hold(down_out_far)]
    in_ring = Gather(my_rows)
    in_ring.step(line, columns, *down_out_last)
    small = [
        packed[:, ends[i] : ends[i + 1]].astype(f32).reshape(1, -1) for i in range(4, len(pieces) - 1)
    ]
    bias_out, bias_down, bias_qkv, bias_up = small
    affine = packed[:, : ends[4]].astype(f32).reshape(devices, 4, slim).transpose(1, 0, 2).reshape(4, model)
    bias_up = lax.dynamic_slice_in_dim(bias_up, t * hidden, hidden, 1)
    bias_qkv = lax.dynamic_index_in_dim(
        bias_qkv.reshape(3, HEADS, HD), t, 1, keepdims=False
    ).reshape(1, 3 * HD)

    all_seg = packed[:, ends[-2] : ends[-1]].reshape(depth, width * TURNS, seqs, rows)
    seq_seg = lax.dynamic_slice_in_dim(all_seg, c * 2, 2, 0)
    seq_seg = lax.dynamic_index_in_dim(seq_seg, x, 2, keepdims=False).reshape(2, -1).astype(f32)
    masks = (seq_seg[:, None, :],)

    def norm(at, kept):
        pieces = in_ring.held[ORDER[at]]
        return line(lambda *given: norm_block(at, *given, slim), pieces, affine, kept)

    kept = norm(0, None)
    qkv_cols, up_cols = after((columns[:, :, : 3 * HD], columns[:, :, 3 * HD :]), columns)
    qkv_far, up_far = swap(qkv_cols, "x"), swap(up_cols, "x")
    qkv_near, up_near = swap(qkv_cols, "c"), swap(up_cols, "c")
    weight_out, weight_down = (
        line(assemble, pieces, scalar(mine))
        for pieces in zip(down_out, down_out_near, down_out_far, down_out_last)
    )
    in_ring.step(line)
    kept = norm(1, kept)
    kept = norm(2, kept)
    in_ring.step(line)
    qkv_last = swap(line.hold(qkv_far), "c")
    kept = norm(3, kept)
    kept = norm(4, kept)
    weight_qkv = line(assemble, (qkv_cols, qkv_near, qkv_far, qkv_last), scalar(mine))
    in_ring.step(line)
    kept = norm(5, kept)
    kept = norm(6, kept)
    grad_ring = Gather(my_grad)
    grad_ring.step(line, *in_ring.held[4])
    up_last = swap(line.hold(up_far), "c")
    act_one, act_two, means, scales, turned_one, turned_two = norm(7, kept)

    lie = (depth_of, far_of, scalar(c))
    qkv_mine, sent = line(
        lambda *given: project(*given, block), act_one, weight_qkv, bias_qkv, token_tables, *lie
    )
    grad_ring.step(line)
    qkv_came = swap(sent, "c")
    weight_up = line(assemble, (up_cols, up_near, up_far, up_last), scalar(mine))
    out_mine, sent = line(
        lambda *given: attend(forward_kernel, rows, HD, *given), scalar(c), masks, qkv_mine, qkv_came
    )
    out_came = swap(sent, "c")
    grad_ring.step(line)
    act_hidden, slope, hidden_turned = line(widen, act_two, weight_up, bias_up)
    grad_ring.step(line)
    attended, attended_turned = line(lambda *given: place(*given, turn=True), out_mine, out_came, *lie)

    out_own, *out_late = line(
        lambda a, b: share_part(False, 0, len(ORDER), block, a, b, all_pieces(block)),
        (attended, act_hidden),
        (weight_out, weight_down),
    )
    out_late, (one, two, *out_early) = out_late[:4], out_late[4:]
    out_ring = Scatter()

    grads = [piece for j in ORDER for piece in grad_ring.held[j]]
    grad_mine, sent = line(lambda *given: head_grads(*given, block), grads, weight_out, *lie)
    grad_came = swap(sent, "c")
    out_ring.send(*line.hold((one, two)))
    grad_hidden, up_sum = line(narrow, grads, weight_down, slope)
    which = (scalar(c), scalar(x))
    (up_far,) = line(rows_grad, turned_two, grad_hidden, *which)
    back_mine, sent = line(
        lambda *given: attend(backward_kernel, rows, 3 * HD, *given),
        scalar(c),
        (*masks, *seq_tables),
        qkv_mine,
        qkv_came,
        grad_mine,
        grad_came,
        wait=(out_ring.ahead, out_ring.behind),
    )
    back_came = swap(sent, "c")
    out_ring.step(line, *out_early)
    up_came = swap(line.hold(up_far), "c")
    down_lefts = (
        attended_turned.reshape(2, CORES, slim, -1),
        hidden_turned.reshape(2, CORES, hidden // TURNS, -1),
    )
    (down_far,) = line(down_grad, *down_lefts, grads, *which)
    (grad_qkv,) = line(place, back_mine, back_came, *lie)
    (qkv_far,) = line(rows_grad, turned_one, grad_qkv, *which)
    grad_up, up_far = line(
        lambda *given: rows_grad(*given, slots=True), turned_two, grad_hidden, *which, up_came
    )
    out_ring.step(line, out_late[2], out_late[3])
    qkv_came = swap(line.hold(qkv_far), "c")
    up_came = lax.all_to_all(line.hold(up_far), "x", 0, 0, tiled=True)

    lefts, rights = (grad_qkv, grad_hidden), (weight_qkv, weight_up)

    def pull(first, count, pieces):
        values = [piece for j in ORDER[first : first + count] for piece in in_ring.held[j]]
        return line(
            lambda left, right, more: share_part(True, first, count, block, left, right, pieces, more),
            lefts,
            rights,
            ((affine,), values, means, scales),
        )

    early_sums, one, two, *early = pull(5, 3, early_pieces(block))
    pull_ring = Scatter()
    pull_ring.send(one, two)
    out_ring.step(line, out_late[0], out_late[1])
    late_sums, pull_own, *late = pull(0, 5, late_pieces(block))
    sums = line(vectors, scalar(t), early_sums, late_sums, my_grad, grad_qkv, up_sum)
    grad_qkv_w, qkv_far = line(rows_grad, turned_one, grad_qkv, *which, qkv_came)
    grad_up = line(total_slot, scalar(x), grad_up, up_came)
    pull_ring.step(line, *early, wait=(out_ring.ahead, out_ring.behind))
    grad_up = lax.all_to_all(line.hold(grad_up), GROUP, 0, 0, tiled=True)
    qkv_came, down_came = swap(line.hold(qkv_far), "x"), swap(line.hold(down_far), "c")
    sums_came = swap(line.hold(sums), "c")
    sums = line(sum_arrays, sums, sums_came)
    grad_down, down_far = line(down_grad, *down_lefts, grads, *which, down_came)
    pull_ring.step(line, late[2], late[3])
    sums_came = swap(line.hold(sums), "x")
    sums = line(sum_arrays, sums, sums_came)

    def slices(values, rows):
        cut = values.reshape(rows, share, TURNS, -1)
        return lax.dynamic_index_in_dim(cut, mine, 2, keepdims=False).transpose(1, 0, 2).reshape(share, -1)

    sums = jnp.concatenate([slices(sums[:5], 5), slices(sums[5:8], 1), slices(sums[8:12], 1)], axis=1)
    sums = jnp.pad(sums.reshape(share, -1, 128), ((0, 0), (0, 2), (0, 0)))
    grad_qkv_w = line(total_with, grad_qkv_w, qkv_came, sums)
    pull_ring.step(line, late[0], late[1])
    grad_qkv_w = lax.all_to_all(line.hold(grad_qkv_w), GROUP, 0, 0, tiled=True)
    down_came = swap(line.hold(down_far), "x")
    (grad_up,) = line(lambda given: join(given, 1), grad_up)
    kept_out, sent_out = line(
        mixed_rows, scalar(x), out_own, out_ring.ahead, out_ring.behind, my_rows, bias_out, bias_down
    )
    grad_out, grad_down = line(
        lambda a, b: total_rows(a, b, [(slim, f32), (hidden // TURNS, f32)]), grad_down, down_came
    )
    grad_qkv_w, sums = line(lambda given: join(given, 3, (8, 128)), grad_qkv_w)
    kept_in, sent_in = line(
        finish, scalar(x), pull_own, pull_ring.ahead, pull_ring.behind, my_rows, my_grad, means, scales
    )
    came_in, came_out = (swap(sent, "x") for sent in line.hold((sent_in, sent_out)))
    mixed, grad_in = line(in_order, scalar(x), (kept_out, kept_in), (came_out, came_in))

    sums = sums.reshape(-1)
    norm_sums = [sums[i * slim : (i + 1) * slim] for i in range(5)]
    qkv_end = 5 * slim + qkv_bias.shape[0]
    return (
        mixed,
        grad_in,
        norm_sums[0],
        norm_sums[1],
        grad_qkv_w,
        sums[5 * slim : qkv_end],
        grad_out,
        norm_sums[4],
        norm_sums[2],
        norm_sums[3],
        grad_up,
        sums[qkv_end : qkv_end + fc1_bias.shape[0]],
        grad_down,
        norm_sums[4],
    )


def specs(batch, block):
    every = batch + block
    one, two, three = P(every), P(every, None), P(batch, block, None)
    arguments = (three, P(batch, block), one, one, two, one, two, one, one, one, two, one, two, one, three)
    results = (three, three, one, one, two, one, two, one, one, one, two, one, two, one)
    return arguments, results


def solution(mesh):
    depth, ring = mesh.shape["dp"], mesh.shape["seq"]
    width = ring // TURNS
    if width == 2 and depth == TURNS and depth * width == HEADS:
        chips = Mesh(mesh.devices.reshape(depth, width, 2, CORES), EVERY)
        arguments, results = specs(("z",), ("y", "x", "c"))
        return jax.shard_map(
            grouped, mesh=chips, in_specs=arguments, out_specs=results, check_vma=False
        )
    arguments, results = specs(("dp",), ("seq",))
    return jax.shard_map(
        per_device, mesh=mesh, in_specs=arguments, out_specs=results, check_vma=False
    )
```

```python
import functools
import math

import jax
import jax.numpy as jnp
from jax import lax
from jax.experimental import pallas as pl
from jax.experimental.pallas import tpu as pltpu
from jax.sharding import Mesh, PartitionSpec as P

HEADS = 8
HD = 256
ROT = 64
CORES = 2


epsilon = 1e-05
masked_value = -1e30


def layer_norm(values, gain, shift):
    average = jnp.mean(values, axis=-1, keepdims=True)
    centered = values - average
    variance = jnp.mean(centered * centered, axis=-1, keepdims=True)
    return centered * lax.rsqrt(variance + epsilon) * gain + shift


def base_tables(places):
    half_rot = ROT // 2
    frequencies = 10000.0 ** (
        -(jnp.arange(half_rot, dtype=jnp.int32).astype(jnp.float32) * 2.0 / ROT)
    )
    angles = places[:, None] * frequencies[None, :]
    return (jnp.cos(angles)[:, None, :], jnp.sin(angles)[:, None, :])


def base_rotate(values, cosines, sines):
    half_rot = ROT // 2
    first_half = values[..., :half_rot]
    second_half = values[..., half_rot:ROT]
    return jnp.concatenate(
        [
            first_half * cosines - second_half * sines,
            second_half * cosines + first_half * sines,
            values[..., ROT:],
        ],
        axis=-1,
    )


def gelu_exact(values):
    return jax.nn.gelu(values, approximate=False)


def visible(query_seg, query_pos, key_seg, key_pos):
    causal = key_pos[None, :] <= query_pos[:, None]
    same_doc = query_seg[:, :, None] == key_seg[:, None, :]
    return (causal[None] & same_doc)[:, :, None, :]


def per_device(
    tokens,
    segments,
    ln1_gain,
    ln1_bias,
    qkv_weight,
    qkv_bias,
    out_weight,
    out_bias,
    ln2_gain,
    ln2_bias,
    fc1_weight,
    fc1_bias,
    fc2_weight,
    fc2_bias,
    cotangent,
):
    group_size, block_size, model_width = tokens.shape
    row_count = group_size * block_size
    attention_full = (
        lax.all_gather(ln1_gain, ("dp", "seq"), axis=0, tiled=True),
        lax.all_gather(ln1_bias, ("dp", "seq"), axis=0, tiled=True),
        lax.all_gather(qkv_weight, ("dp", "seq"), axis=0, tiled=True),
        lax.all_gather(qkv_bias, ("dp", "seq"), axis=0, tiled=True),
        lax.all_gather(out_weight, ("dp", "seq"), axis=0, tiled=True),
        lax.all_gather(out_bias, ("dp", "seq"), axis=0, tiled=True),
    )
    gain_one, bias_one, weight_qkv, bias_qkv, weight_out, bias_out = attention_full
    flat_in = tokens.reshape(row_count, model_width).astype(jnp.float32)
    normed_one, norm_back_one = jax.vjp(
        layer_norm, flat_in, gain_one.astype(jnp.float32), bias_one.astype(jnp.float32)
    )
    act_one = normed_one.astype(jnp.bfloat16)
    mixed_qkv = jnp.dot(act_one, weight_qkv, preferred_element_type=jnp.float32) + bias_qkv.astype(
        jnp.float32
    )
    mixed_qkv = mixed_qkv.reshape(group_size, block_size, 3, HEADS, HD)
    first_pos = lax.axis_index("seq") * block_size
    local_pos = first_pos + jnp.arange(block_size, dtype=jnp.int32)
    cosines, sines = base_tables(local_pos.astype(jnp.float32))

    def turn_all(query_raw, key_raw):
        return (base_rotate(query_raw, cosines, sines) * 0.0625, base_rotate(key_raw, cosines, sines))

    (query_turned, key_turned), turn_back = jax.vjp(
        turn_all, mixed_qkv[:, :, 0], mixed_qkv[:, :, 1]
    )
    query_low = query_turned.astype(jnp.bfloat16)
    key_low = key_turned.astype(jnp.bfloat16)
    value_low = mixed_qkv[:, :, 2].astype(jnp.bfloat16)
    start_top = jnp.full((group_size, block_size, HEADS), masked_value, jnp.float32)
    key_piece = lax.all_gather(key_low, "seq", axis=1, tiled=True)
    value_piece = lax.all_gather(value_low, "seq", axis=1, tiled=True)
    seg_piece = lax.all_gather(segments, "seq", axis=1, tiled=True)
    key_pos = jnp.arange(seg_piece.shape[1], dtype=jnp.int32)
    allowed = visible(segments, local_pos, seg_piece, key_pos)
    scores = jnp.einsum("gqhd,gkhd->gqhk", query_low, key_piece, preferred_element_type=jnp.float32)
    scores = jnp.where(allowed, scores, masked_value)
    new_top = jnp.maximum(start_top, jnp.max(scores, axis=-1))
    weights = jnp.where(allowed, jnp.exp(scores - new_top[..., None]), 0.0)
    new_total = jnp.sum(weights, axis=-1)
    new_out = jnp.einsum(
        "gqhk,gkhd->gqhd",
        weights.astype(jnp.bfloat16),
        value_piece,
        preferred_element_type=jnp.float32,
    )
    attended = new_out / new_total[..., None]
    log_total = new_top + jnp.log(new_total)
    attended_low = attended.astype(jnp.bfloat16).reshape(row_count, model_width)
    attn_out = jnp.dot(
        attended_low, weight_out, preferred_element_type=jnp.float32
    ) + bias_out.astype(jnp.float32)
    mlp_full = (
        lax.all_gather(ln2_gain, ("dp", "seq"), axis=0, tiled=True),
        lax.all_gather(ln2_bias, ("dp", "seq"), axis=0, tiled=True),
        lax.all_gather(fc1_weight, ("dp", "seq"), axis=0, tiled=True),
        lax.all_gather(fc1_bias, ("dp", "seq"), axis=0, tiled=True),
        lax.all_gather(fc2_weight, ("dp", "seq"), axis=0, tiled=True),
        lax.all_gather(fc2_bias, ("dp", "seq"), axis=0, tiled=True),
    )
    gain_two, bias_two, weight_up, bias_up, weight_down, bias_down = mlp_full
    normed_two, norm_back_two = jax.vjp(
        layer_norm, flat_in, gain_two.astype(jnp.float32), bias_two.astype(jnp.float32)
    )
    act_two = normed_two.astype(jnp.bfloat16)
    hidden = jnp.dot(act_two, weight_up, preferred_element_type=jnp.float32) + bias_up.astype(
        jnp.float32
    )
    activated, gelu_back = jax.vjp(gelu_exact, hidden)
    act_hidden = activated.astype(jnp.bfloat16)
    mlp_out = jnp.dot(
        act_hidden, weight_down, preferred_element_type=jnp.float32
    ) + bias_down.astype(jnp.float32)
    mixed = (
        (flat_in + attn_out + mlp_out)
        .astype(jnp.bfloat16)
        .reshape(group_size, block_size, model_width)
    )
    back_up, back_down = (
        lax.all_gather(fc1_weight, ("dp", "seq"), axis=0, tiled=True),
        lax.all_gather(fc2_weight, ("dp", "seq"), axis=0, tiled=True),
    )
    back_qkv, back_out = (
        lax.all_gather(qkv_weight, ("dp", "seq"), axis=0, tiled=True),
        lax.all_gather(out_weight, ("dp", "seq"), axis=0, tiled=True),
    )
    grad_out = cotangent.reshape(row_count, model_width)
    grad_float = grad_out.astype(jnp.float32)
    grad_down_weight = jnp.dot(act_hidden.T, grad_out, preferred_element_type=jnp.float32)
    grad_down_bias = jnp.sum(grad_float, axis=0)
    grad_activated = jnp.dot(grad_out, back_down.T, preferred_element_type=jnp.float32)
    (grad_hidden,) = gelu_back(grad_activated)
    grad_hidden_low = grad_hidden.astype(jnp.bfloat16)
    grad_up_weight = jnp.dot(act_two.T, grad_hidden_low, preferred_element_type=jnp.float32)
    grad_up_bias = jnp.sum(grad_hidden_low.astype(jnp.float32), axis=0)
    grad_act_two = jnp.dot(grad_hidden_low, back_up.T, preferred_element_type=jnp.float32)
    grad_in_two, grad_gain_two, grad_bias_two = norm_back_two(grad_act_two)
    mlp_shards = (
        lax.psum_scatter(grad_gain_two, ("dp", "seq"), scatter_dimension=0, tiled=True),
        lax.psum_scatter(grad_bias_two, ("dp", "seq"), scatter_dimension=0, tiled=True),
        lax.psum_scatter(grad_up_weight, ("dp", "seq"), scatter_dimension=0, tiled=True),
        lax.psum_scatter(grad_up_bias, ("dp", "seq"), scatter_dimension=0, tiled=True),
        lax.psum_scatter(grad_down_weight, ("dp", "seq"), scatter_dimension=0, tiled=True),
        lax.psum_scatter(grad_down_bias, ("dp", "seq"), scatter_dimension=0, tiled=True),
    )
    grad_out_weight = jnp.dot(attended_low.T, grad_out, preferred_element_type=jnp.float32)
    grad_out_bias = jnp.sum(grad_float, axis=0)
    grad_attended = jnp.dot(grad_out, back_out.T, preferred_element_type=jnp.float32)
    grad_low = grad_attended.reshape(group_size, block_size, HEADS, HD).astype(jnp.bfloat16)
    delta = jnp.sum(grad_low.astype(jnp.float32) * attended, axis=-1)
    key_piece = lax.all_gather(key_low, "seq", axis=1, tiled=True)
    value_piece = lax.all_gather(value_low, "seq", axis=1, tiled=True)
    seg_piece = lax.all_gather(segments, "seq", axis=1, tiled=True)
    key_pos = jnp.arange(seg_piece.shape[1], dtype=jnp.int32)
    allowed = visible(segments, local_pos, seg_piece, key_pos)
    scores = jnp.einsum("gqhd,gkhd->gqhk", query_low, key_piece, preferred_element_type=jnp.float32)
    chances = jnp.where(allowed, jnp.exp(scores - log_total[..., None]), 0.0)
    grad_chances = jnp.einsum(
        "gqhd,gkhd->gqhk", grad_low, value_piece, preferred_element_type=jnp.float32
    )
    grad_scores = (chances * (grad_chances - delta[..., None])).astype(jnp.bfloat16)
    grad_query = jnp.einsum(
        "gqhk,gkhd->gqhd", grad_scores, key_piece, preferred_element_type=jnp.float32
    )
    query_piece = lax.all_gather(query_low, "seq", axis=1, tiled=True)
    grad_piece = lax.all_gather(grad_low, "seq", axis=1, tiled=True)
    lse_piece = lax.all_gather(log_total.astype(jnp.bfloat16), "seq", axis=1, tiled=True).astype(
        jnp.float32
    )
    delta_piece = lax.all_gather(delta.astype(jnp.bfloat16), "seq", axis=1, tiled=True).astype(
        jnp.float32
    )
    seg_piece = lax.all_gather(segments, "seq", axis=1, tiled=True)
    query_pos = jnp.arange(seg_piece.shape[1], dtype=jnp.int32)
    allowed = visible(seg_piece, query_pos, segments, local_pos)
    scores = jnp.einsum("gqhd,gkhd->gqhk", query_piece, key_low, preferred_element_type=jnp.float32)
    chances = jnp.where(allowed, jnp.exp(scores - lse_piece[..., None]), 0.0)
    new_value = jnp.einsum(
        "gqhk,gqhd->gkhd",
        chances.astype(jnp.bfloat16),
        grad_piece,
        preferred_element_type=jnp.float32,
    )
    grad_chances = jnp.einsum(
        "gqhd,gkhd->gqhk", grad_piece, value_low, preferred_element_type=jnp.float32
    )
    grad_scores = (chances * (grad_chances - delta_piece[..., None])).astype(jnp.bfloat16)
    new_key = jnp.einsum(
        "gqhk,gqhd->gkhd", grad_scores, query_piece, preferred_element_type=jnp.float32
    )
    grad_query_raw, grad_key_raw = turn_back((grad_query, new_key))
    grad_qkv_low = (
        jnp.stack([grad_query_raw, grad_key_raw, new_value], axis=2)
        .reshape(row_count, 3 * model_width)
        .astype(jnp.bfloat16)
    )
    grad_qkv_weight = jnp.dot(act_one.T, grad_qkv_low, preferred_element_type=jnp.float32)
    grad_qkv_bias = jnp.sum(grad_qkv_low.astype(jnp.float32), axis=0)
    grad_act_one = jnp.dot(grad_qkv_low, back_qkv.T, preferred_element_type=jnp.float32)
    grad_in_one, grad_gain_one, grad_bias_one = norm_back_one(grad_act_one)
    attention_shards = (
        lax.psum_scatter(grad_gain_one, ("dp", "seq"), scatter_dimension=0, tiled=True),
        lax.psum_scatter(grad_bias_one, ("dp", "seq"), scatter_dimension=0, tiled=True),
        lax.psum_scatter(grad_qkv_weight, ("dp", "seq"), scatter_dimension=0, tiled=True),
        lax.psum_scatter(grad_qkv_bias, ("dp", "seq"), scatter_dimension=0, tiled=True),
        lax.psum_scatter(grad_out_weight, ("dp", "seq"), scatter_dimension=0, tiled=True),
        lax.psum_scatter(grad_out_bias, ("dp", "seq"), scatter_dimension=0, tiled=True),
    )
    grad_tokens = (
        (grad_float + grad_in_one + grad_in_two)
        .astype(jnp.bfloat16)
        .reshape(group_size, block_size, model_width)
    )
    return (
        mixed,
        grad_tokens,
        attention_shards[0],
        attention_shards[1],
        attention_shards[2],
        attention_shards[3],
        attention_shards[4],
        attention_shards[5],
        mlp_shards[0],
        mlp_shards[1],
        mlp_shards[2],
        mlp_shards[3],
        mlp_shards[4],
        mlp_shards[5],
    )


GROUP = ("z", "y")
PEERS = ("x", "c")
EVERY = ("z", "y", "x", "c")
TURNS = 2 * CORES
ORDER = (0, 1, 7, 2, 6, 3, 5, 4)
LIMIT = 56 * 1024 * 1024
SMALL = 26 * 1024 * 1024
bf16, f32 = jnp.bfloat16, jnp.float32


def whole_ref():
    return pl.BlockSpec(memory_space=pltpu.VMEM)


def in_place():
    return pl.BlockSpec(memory_space=pl.ANY)


def call(
    kernel, results, inputs, operands, outputs, grid=(), prefetch=0, aliases=None, scratch=(), limit=LIMIT
):
    return pl.pallas_call(
        kernel,
        out_shape=[jax.ShapeDtypeStruct(*result) for result in results],
        grid_spec=pltpu.PrefetchScalarGridSpec(
            num_scalar_prefetch=prefetch, grid=grid, in_specs=inputs, out_specs=outputs, scratch_shapes=scratch
        ),
        input_output_aliases=aliases or {},
        compiler_params=pltpu.CompilerParams(vmem_limit_bytes=limit),
        cost_estimate=pl.CostEstimate(flops=1, bytes_accessed=1, transcendentals=0),
    )(*operands)


class Line:
    def __init__(self):
        self.last = ()

    def __call__(self, function, *operands, wait=()):
        operands = lax.optimization_barrier((operands, self.last, wait))[0]
        results = function(*operands)
        self.last = tuple(jax.tree.leaves(results))
        return results

    def hold(self, values):
        return lax.optimization_barrier((values, self.last))[0]


def after(value, *others):
    return lax.optimization_barrier((value, *others))[0]


def ring_perm(shift):
    depth, width = lax.axis_size("z"), lax.axis_size("y")
    places = [z * width for z in range(depth)] + [z * width + 1 for z in reversed(range(depth))]
    count = len(places)
    return [(places[i], places[(i + shift) % count]) for i in range(count)]


class Gather:
    def __init__(self, block):
        self.held = {0: [block]}
        self.ahead = self.behind = block
        self.done = 0

    def step(self, line, *others):
        half = len(ORDER) // 2
        ahead, behind = line.hold((self.ahead, self.behind, *others))[:2]
        self.done += 1
        if self.done < half:
            self.behind = lax.ppermute(behind, GROUP, ring_perm(1))
            self.ahead = lax.ppermute(ahead, GROUP, ring_perm(-1))
            self.held[len(ORDER) - self.done] = [self.behind]
            self.held[self.done] = [self.ahead]
        else:
            cut = behind.shape[0] // 2
            self.held[half] = [
                lax.ppermute(behind[:cut], GROUP, ring_perm(1)),
                lax.ppermute(ahead[cut:], GROUP, ring_perm(-1)),
            ]


def swap(values, axis):
    return lax.ppermute(values, axis, [(0, 1), (1, 0)])


def dot_f32(left, right, dims=((1,), (0,))):
    return lax.dot_general(left, right, (dims, ((), ())), preferred_element_type=f32)


def tile_spec(shape, index):
    return pl.BlockSpec(shape, lambda i, *scalars: index(i))


def same(shape):
    return tile_spec(shape, lambda i: (0,) * len(shape))


def spread_kernel(up, qkv, result):
    share, _, columns = result.shape
    tile = columns - 3 * HD
    for t in range(share):
        for i in range(3):
            at = (i * share + t) * HD
            result[t, :, i * HD : (i + 1) * HD] = qkv[:, at : at + HD]
        result[t, :, 3 * HD :] = up[:, t * tile : (t + 1) * tile]


def spread(up, qkv, share):
    rows, columns = up.shape
    return call(
        spread_kernel,
        [((share, rows, 3 * HD + columns // share), bf16)],
        [whole_ref()] * 2,
        (up, qkv),
        [whole_ref()],
    )[0]


def assemble_kernel(mine, *refs):
    sources, result = refs[:TURNS], refs[TURNS]
    for entry in range(result.shape[0]):
        for turn in range(TURNS):
            result[entry, pl.ds(mine[0] ^ turn, 1)] = sources[turn][entry : entry + 1]


def assemble(pieces, mine, step=2):
    entries, rows, columns = pieces[0].shape
    step = min(step, entries)
    return call(
        assemble_kernel,
        [((entries, TURNS, rows, columns), pieces[0].dtype)],
        [tile_spec((step, rows, columns), lambda i: (i, 0, 0))] * TURNS,
        (mine, *pieces),
        [tile_spec((step, TURNS, rows, columns), lambda i: (i, 0, 0, 0))],
        grid=(entries // step,),
        prefetch=1,
    )[0].reshape(entries * TURNS * rows, columns)


def settle_kernel(depth, peer, *refs):
    sources, result = refs[:-1], refs[-1]
    share = sources[0].shape[0]
    for shift, source in enumerate(sources):
        at = ((depth[0] + len(sources) - shift) % len(sources)) * share
        for j in range(share):
            result[pl.ds(at + (j ^ peer[0]), 1)] = source[j : j + 1]


def settle(depth, peer, *sources):
    shape = (len(sources) * sources[0].shape[0], *sources[0].shape[1:])
    return call(
        settle_kernel,
        [(shape, sources[0].dtype)],
        [same(source.shape) for source in sources],
        (depth, peer, *sources),
        [same(shape)],
        grid=(1,),
        prefetch=2,
    )[0]


def norm_kernel(count, affine, *refs):
    pieces, (one, two, mean_ref, scale_ref, one_turned, two_turned) = refs[:count], refs[-6:]
    values = stacked(pieces).astype(f32)
    mean = jnp.mean(values, axis=-1, keepdims=True)
    centered = values - mean
    scale = lax.rsqrt(jnp.mean(centered * centered, axis=-1, keepdims=True) + epsilon)
    normal = centered * scale
    for at, result, turned in ((0, one, one_turned), (2, two, two_turned)):
        act = (normal * affine[at : at + 1] + affine[at + 1 : at + 2]).astype(bf16)
        result[...] = act
        turned[...] = act.T.reshape(turned.shape)
    mean_ref[...] = mean
    scale_ref[...] = scale


def norm_block(at, pieces, affine, kept, slim):
    block, model = sum(piece.shape[0] for piece in pieces), pieces[0].shape[1]
    rows = len(ORDER) * block
    turned = (model // (TURNS * slim), 2, CORES, slim)
    results = [
        ((rows, model), bf16),
        ((rows, model), bf16),
        ((rows, 1), f32),
        ((rows, 1), f32),
        ((*turned, rows), bf16),
        ((*turned, rows), bf16),
    ]
    outputs = [pl.BlockSpec((block, shape[1]), lambda i: (at, 0)) for shape, _ in results[:4]]
    outputs += [pl.BlockSpec((*turned, block), lambda i: (0, 0, 0, 0, at))] * 2
    operands = [affine, *pieces]
    inputs = [whole_ref()] * len(operands)
    aliases = {}
    if kept is not None:
        aliases = {len(operands) + i: i for i in range(len(results))}
        operands += kept
        inputs += [in_place()] * len(results)
    return call(
        functools.partial(norm_kernel, len(pieces)), results, inputs, operands, outputs, grid=(1,), aliases=aliases
    )


def rotary_tables(places):
    half_rot = ROT // 2
    frequencies = 10000.0 ** (
        -(jnp.arange(half_rot, dtype=jnp.int32).astype(f32) * 2.0 / ROT)
    )
    turned = places.astype(f32)[:, None] * frequencies[None, :]
    cosines, sines = jnp.cos(turned), jnp.sin(turned)
    rest = jnp.zeros((places.shape[0], 128 - ROT), f32)
    none = jnp.zeros_like(sines)
    return (
        jnp.concatenate([cosines, cosines, rest + 1.0], axis=1),
        jnp.concatenate([sines, none, rest], axis=1),
        jnp.concatenate([none, sines, rest], axis=1),
    )


def rotate(values, tables, sign):
    cosines, first, second = tables
    half_rot = ROT // 2
    low = values[:, :128]
    ahead = pltpu.roll(low, 128 - half_rot, 1)
    behind = pltpu.roll(low, half_rot, 1)
    low = low * cosines + sign * (behind * second - ahead * first)
    return jnp.concatenate([low, values[:, 128:]], axis=1)


def qkv_kernel(depth_of, far_of, core, act, weight, bias, cosines, first, second, *results):
    qkv = jnp.dot(act[...], weight[...], preferred_element_type=f32) + bias[...]
    tables = (cosines[...], first[...], second[...])
    query = (rotate(qkv[:, :HD], tables, 1.0) * 0.0625).astype(bf16)
    key = rotate(qkv[:, HD : 2 * HD], tables, 1.0).astype(bf16)
    value = qkv[:, 2 * HD :].astype(bf16)
    parts = act.shape[0] // results[0].shape[2]
    start = pl.program_id(0) * parts
    spill(jnp.concatenate([query, key, value], axis=1), depth_of, far_of, core, start, results)


def spill(values, depth_of, far_of, core, start, results):
    block = results[0].shape[2]
    for part in range(values.shape[0] // block):
        at = start + part
        rows = values[None, None, part * block : (part + 1) * block]
        owner, low = depth_of[at] // 2, depth_of[at] % 2
        for result, mine in zip(results, (True, False)):

            @pl.when((owner == core[0]) == mine)
            def _():
                result[pl.ds(low, 1), pl.ds(far_of[at], 1)] = rows


def project(act, weight, bias, tables, depth_of, far_of, core, block):
    rows, model = act.shape
    columns = weight.shape[1]
    step = 4 * block
    return call(
        qkv_kernel,
        [((2, 2, block, columns), bf16)] * 2,
        [tile_spec((step, model), lambda i: (i, 0)), same((model, columns)), same((1, columns))]
        + [tile_spec((step, 128), lambda i: (i, 0))] * 3,
        (depth_of, far_of, core, act, weight, bias, *tables),
        [same((2, 2, block, columns))] * 2,
        grid=(rows // step,),
        prefetch=3, limit=SMALL)


def place_kernel(depth_of, far_of, core, mine, came, result, *turned):
    block = result.shape[1]
    for at in range(result.shape[0]):
        for source, own in ((mine, True), (came, False)):

            @pl.when((depth_of[at] // 2 == core[0]) == own)
            def _():
                values = source[pl.ds(depth_of[at] % 2, 1), pl.ds(far_of[at], 1)][0, 0]
                result[at] = values
                for other in turned:
                    other[:, at * block : (at + 1) * block] = values.T


def place(mine, came, depth_of, far_of, core, turn=False):
    low, far, block, columns = mine.shape
    count = 2 * low * far
    shapes = [(count, block, columns)] + [(columns, count * block)] * turn
    placed, *turned = call(
        place_kernel,
        [(shape, bf16) for shape in shapes],
        [same(mine.shape)] * 2,
        (depth_of, far_of, core, mine, came),
        [same(shape) for shape in shapes],
        grid=(1,),
        prefetch=3,
        limit=SMALL,
    )
    return (placed.reshape(count * block, columns), *turned)


def pairs(ref, rows):
    return [(far, slice(at, at + rows)) for far in range(ref.shape[1]) for at in range(0, ref.shape[2], rows)]


def gathered(mine, came, even, seq, start, rows):
    parts = []
    for far, at in pairs(mine, rows):
        own, other = (ref[seq, far, at, start : start + HD] for ref in (mine, came))
        parts += [jnp.where(even, own, other), jnp.where(even, other, own)]
    return jnp.concatenate(parts, axis=0)


def scattered(mine, sent, even, seq, start, rows, values):
    for i, (far, at) in enumerate(pairs(mine, rows)):
        first, second = (values[(2 * i + k) * rows : (2 * i + k + 1) * rows] for k in range(2))
        mine[seq, far, at, start : start + HD] = jnp.where(even, first, second)
        sent[seq, far, at, start : start + HD] = jnp.where(even, second, first)


def chances_of(query, key, segments):
    scores = dot_f32(query, key, ((1,), (1,)))
    col_seg = jnp.broadcast_to(segments, scores.shape)
    row_seg = col_seg.T
    row_pos = lax.broadcasted_iota(jnp.int32, scores.shape, 0)
    col_pos = lax.broadcasted_iota(jnp.int32, scores.shape, 1)
    scores = jnp.where((col_pos <= row_pos) & (col_seg == row_seg), scores, masked_value)
    weights = jnp.exp(scores - jnp.max(scores, axis=-1, keepdims=True))
    return weights / jnp.sum(weights, axis=-1, keepdims=True)


def forward_kernel(rows, core, segments, mine, came, kept, sent):
    even = core[0] == 0
    for seq in range(mine.shape[0]):
        query, key, value = (gathered(mine, came, even, seq, i * HD, rows) for i in range(3))
        chances = chances_of(query, key, segments[seq])
        scattered(kept, sent, even, seq, 0, rows, dot_f32(chances.astype(bf16), value).astype(bf16))


def backward_kernel(
    rows, core, segments, cosines, first, second, mine, came, grad_mine, grad_came, kept, sent
):
    even = core[0] == 0
    tables = (cosines[...], first[...], second[...])
    for seq in range(mine.shape[0]):
        query, key, value = (gathered(mine, came, even, seq, i * HD, rows) for i in range(3))
        grad = gathered(grad_mine, grad_came, even, seq, 0, rows)
        chances = chances_of(query, key, segments[seq])
        chances_low = chances.astype(bf16)
        grad_chances = dot_f32(grad, value, ((1,), (1,)))
        delta = jnp.sum(chances_low.astype(f32) * grad_chances, axis=-1, keepdims=True)
        grad_scores = (chances * (grad_chances - delta)).astype(bf16)
        grad_query = dot_f32(grad_scores, key)
        grad_key = dot_f32(grad_scores, query, ((0,), (0,)))
        grad_value = dot_f32(chances_low, grad, ((0,), (0,)))
        for i, part in enumerate(
            (rotate(grad_query * 0.0625, tables, -1.0), rotate(grad_key, tables, -1.0), grad_value)
        ):
            scattered(kept, sent, even, seq, i * HD, rows, part.astype(bf16))


def attend(kernel, rows, columns, core, given, *arrays):
    operands = (*given, *arrays)
    shape = (*arrays[0].shape[:3], columns)
    return call(
        functools.partial(kernel, rows),
        [(shape, bf16)] * 2,
        [same(a.shape) for a in operands],
        (core, *operands),
        [same(shape)] * 2,
        grid=(1,),
        prefetch=1,
        limit=SMALL,
    )


def widen_kernel(act, weight, bias, activated, slope, turned):
    hidden = jnp.dot(act[...], weight[...], preferred_element_type=f32) + bias[...]
    cdf = 0.5 * (1.0 + lax.erf(hidden * math.sqrt(0.5)))
    result = (hidden * cdf).astype(bf16)
    activated[...] = result
    turned[...] = result.T
    slope[...] = (cdf + hidden * jnp.exp(-0.5 * hidden * hidden) * (1.0 / math.sqrt(2.0 * math.pi))).astype(bf16)


def widen(act, weight, bias, tile=256):
    rows, model = act.shape
    columns = weight.shape[1]
    return call(
        widen_kernel,
        [((rows, columns), bf16), ((rows, columns), bf16), ((columns, rows), bf16)],
        [
            same((rows, model)),
            tile_spec((model, tile), lambda i: (0, i)),
            tile_spec((1, tile), lambda i: (0, i)),
        ],
        (act, weight, bias),
        [tile_spec((rows, tile), lambda i: (0, i))] * 2 + [tile_spec((tile, rows), lambda i: (i, 0))],
        grid=(columns // tile,), limit=SMALL)


def stacked(refs):
    return jnp.concatenate([ref[...] for ref in refs], axis=0)


def narrow_kernel(weight, slope, *refs):
    blocks, (result, sums) = refs[:-2], refs[-2:]
    grad = dot_f32(stacked(blocks), weight[...], ((1,), (1,))) * slope[...].astype(f32)
    grad = grad.astype(bf16)
    result[...] = grad
    sums[...] = jnp.sum(grad.astype(f32), axis=0, keepdims=True)


def narrow(blocks, weight, slope, tile=512):
    rows, columns = slope.shape
    model = weight.shape[1]
    return call(
        narrow_kernel,
        [((rows, columns), bf16), ((1, columns), f32)],
        [tile_spec((tile, model), lambda i: (i, 0)), tile_spec((rows, tile), lambda i: (0, i))]
        + [same(piece.shape) for piece in blocks],
        (weight, slope, *blocks),
        [tile_spec((rows, tile), lambda i: (0, i)), tile_spec((1, tile), lambda i: (0, i))],
        grid=(columns // tile,),
        limit=SMALL,
    )


def head_kernel(depth_of, far_of, core, weight, *refs):
    blocks, results, total = refs[:-3], refs[-3:-1], refs[-1]
    part = dot_f32(stacked(blocks), weight[...], ((1,), (1,)))
    step = pl.program_id(0)

    @pl.when(step == 0)
    def _():
        total[...] = part

    @pl.when(step > 0)
    def _():
        total[...] += part

    @pl.when(step == pl.num_programs(0) - 1)
    def _():
        spill(total[...].astype(bf16), depth_of, far_of, core, 0, results)


def head_grads(blocks, weight, depth_of, far_of, core, block, tile=512):
    rows = sum(piece.shape[0] for piece in blocks)
    return call(
        head_kernel,
        [((2, 2, block, HD), bf16)] * 2,
        [tile_spec((piece.shape[0], tile), lambda i: (0, i)) for piece in (weight, *blocks)],
        (depth_of, far_of, core, weight, *blocks),
        [same((2, 2, block, HD))] * 2,
        grid=(weight.shape[1] // tile,),
        prefetch=3,
        scratch=[pltpu.VMEM((rows, HD), f32)],
        limit=SMALL,
    )


def across(total, half, near, far, slots=False):
    first, second = total[:, 0], total[:, 1]
    low = half[0] == 0
    near[...] = jnp.where(low, first, second).astype(bf16).reshape(near.shape)
    other = jnp.where(low, second, first).astype(bf16)
    if slots:
        far[pl.ds(1 - half[0], 1)] = other[None]
    else:
        far[...] = other.reshape(far.shape)


def rows_kernel(near, slots, core, half, act, grad, *refs):
    entries, _, _, rows, tokens = act.shape
    total = dot_f32(act[...].reshape(entries * 2 * rows, tokens), grad[...])
    total = total.reshape(entries, 2, rows, grad.shape[1])
    if near:
        came, kept, sent = refs
        across(total + came[...].astype(f32), half, kept, sent, slots)
    else:
        refs[0][...] = total.astype(bf16)


def rows_grad(turned, grad, core, half, came=None, step=4, slots=False):
    entries, _, _, rows, tokens = turned.shape
    columns = grad.shape[1]
    near = came is not None
    spec = tile_spec((step, 2, rows, columns), lambda i: (i, 0, 0, 0))
    inputs = [
        pl.BlockSpec(
            (step, 2, 1, rows, tokens), lambda i, c, x: (i, 0, c[0] if near else 1 - c[0], 0, 0)
        ),
        same((tokens, columns)),
    ]
    if near:
        results = [((entries, rows, columns), bf16)] * 2
        outputs = [tile_spec((step, rows, columns), lambda i: (i, 0, 0))] * 2
        if slots:
            results[1] = ((2, entries, rows, columns), bf16)
            outputs[1] = tile_spec((2, step, rows, columns), lambda i: (0, i, 0, 0))
    else:
        results, outputs = [((entries, 2, rows, columns), bf16)], [spec]
    return call(
        functools.partial(rows_kernel, near, slots),
        results,
        inputs + [spec] * near,
        (core, half, turned, grad) + (came,) * near,
        outputs,
        grid=(entries // step,),
        prefetch=2,
        limit=SMALL,
    )


def down_kernel(near, core, half, attended, activated, *refs):
    count = 3 if near else 1
    blocks, refs = refs[:-count], refs[-count:]
    parts = [ref[x, 0] for x in range(2) for ref in (attended, activated)]
    total = dot_f32(jnp.concatenate(parts, axis=0), stacked(blocks))
    total = total.reshape(1, 2, total.shape[0] // 2, total.shape[1])
    if near:
        came, kept, sent = refs
        across(total + came[...][None].astype(f32), half, kept, sent)
    else:
        refs[0][...] = total[0].astype(bf16)


def down_grad(attended, activated, blocks, core, half, came=None, tile=512):
    tokens = attended.shape[3]
    model = blocks[0].shape[1]
    rows = attended.shape[2] + activated.shape[2]
    near = came is not None
    spec = tile_spec((2, rows, tile), lambda i: (0, 0, i))
    inputs = [
        pl.BlockSpec(
            (2, 1, turned.shape[2], tokens), lambda i, c, x: (0, c[0] if near else 1 - c[0], 0, 0)
        )
        for turned in (attended, activated)
    ]
    inputs += [tile_spec((piece.shape[0], tile), lambda i: (0, i)) for piece in blocks]
    if near:
        results = [((rows, model), bf16)] * 2
        outputs = [tile_spec((rows, tile), lambda i: (0, i))] * 2
    else:
        results, outputs = [((2, rows, model), bf16)], [spec]
    return call(
        functools.partial(down_kernel, near),
        results,
        inputs + [spec] * near,
        (core, half, attended, activated, *blocks) + (came,) * near,
        outputs,
        grid=(model // tile,),
        prefetch=2,
        limit=SMALL,
    )


def join_kernel(pieces, given, result, *sums):
    share = given.shape[0]
    width = result.shape[1] // (share * pieces)
    for t in range(share):
        for i in range(pieces):
            at = (i * share + t) * width
            result[:, at : at + width] = given[t, :, i * width : (i + 1) * width].astype(f32)
    for ref in sums:
        rows, columns = ref.shape
        ref[...] = jnp.sum(given[:, :rows, pieces * width : pieces * width + columns].astype(f32), axis=0)


def join(given, pieces, extra=None):
    share, rows, columns = given.shape
    results = [((rows, share * (columns - (extra[1] if extra else 0))), f32)]
    results += [(extra, f32)] if extra else []
    return call(
        functools.partial(join_kernel, pieces), results, [whole_ref()], (given,), [whole_ref()] * len(results), limit=SMALL)


def widen_rows_kernel(mine, came, extra, result):
    columns = mine.shape[2]
    result[:, :, :columns] = (mine[...].astype(f32) + came[...].astype(f32)).astype(bf16)
    result[:, :, columns:] = jnp.zeros((*result.shape[:2], result.shape[2] - columns), bf16)
    result[:, : extra.shape[1], columns:] = extra[...].astype(bf16)


def total_with(mine, came, extra):
    shape = (*mine.shape[:2], mine.shape[2] + extra.shape[2])
    operands = (mine, came, extra)
    return call(widen_rows_kernel, [(shape, bf16)], [whole_ref()] * 3, operands, [whole_ref()], limit=SMALL)[0]


def share_part(pull, first, count, block, lefts, rights, pieces, extras=(), tile=512):
    model = rights[0].shape[0 if pull else 1]
    depths = [right.shape[1 if pull else 0] for right in rights]
    operands, inputs = [], []
    for left, depth in zip(lefts, depths):
        for b in range(count):
            operands.append(left)
            inputs.append(tile_spec((block, depth), lambda i, b=b: (first + b, 0)))
    for right, depth in zip(rights, depths):
        operands.append(right)
        inputs.append(
            tile_spec((tile, depth), lambda i: (i, 0)) if pull else tile_spec((depth, tile), lambda i: (0, i))
        )
    given = 0
    if pull:
        gains, values, mean, scale = extras
        given = len(values)
        for row in (*gains, *values):
            operands.append(row)
            inputs.append(tile_spec((row.shape[0], tile), lambda i: (0, i)))
        for stat in (mean, scale):
            for b in range(count):
                operands.append(stat)
                inputs.append(tile_spec((block, 1), lambda i, b=b: (first + b, 0)))

    def kernel(*refs):
        refs = list(refs)

        def take(number):
            taken = refs[:number]
            del refs[:number]
            return taken

        left_a, left_b = stacked(take(count)), stacked(take(count))
        (right_a,), (right_b,) = take(1), take(1)
        dims = ((1,), (1,)) if pull else ((1,), (0,))
        part_a = dot_f32(left_a, right_a[...], dims)
        part_b = dot_f32(left_b, right_b[...], dims)
        if pull:
            (gains_ref,) = take(1)
            tokens = stacked(take(given)).astype(f32)
            normal = (tokens - stacked(take(count))) * stacked(take(count))
            (sums,) = take(1)
            sums[...] = jnp.concatenate(
                [
                    jnp.sum(part, axis=0, keepdims=True)
                    for part in (part_a * normal, part_a, part_b * normal, part_b)
                ]
                + [jnp.zeros((4, tile), f32)],
                axis=0,
            )
            total = part_a * gains_ref[0:1] + part_b * gains_ref[2:3]
        else:
            total = part_a + part_b
        for (start, rows, dtype), result in zip(pieces, refs):
            result[...] = total[start : start + rows].astype(dtype)

    results = [((rows, model), dtype) for _, rows, dtype in pieces]
    outputs = [tile_spec((rows, tile), lambda i: (0, i)) for _, rows, _ in pieces]
    if pull:
        results = [((8, model), f32)] + results
        outputs = [tile_spec((8, tile), lambda i: (0, i))] + outputs
    return call(
        kernel, results, inputs, operands, outputs, grid=(model // tile,), limit=LIMIT if pull else SMALL
    )


def early_pieces(block):
    cut = block // 2
    return [(2 * block, cut, bf16), (2 * block + cut, cut, bf16), (0, block, bf16), (block, block, bf16)]


def late_pieces(block):
    return [(i * block, block, bf16) for i in range(5)]


def all_pieces(block):
    return late_pieces(block) + [(5 * block + start, rows, dtype) for start, rows, dtype in early_pieces(block)]


def add_kernel(one, two, ahead, behind, *results):
    cut = ahead.shape[0]
    rows = one.shape[0]
    for mine, came, result, start in ((one, ahead, results[0], 0), (two, behind, results[1], rows - cut)):
        if cut < rows:
            result[...] = mine[...]
        at = slice(start, start + cut)
        result[at] = (mine[at].astype(f32) + came[...].astype(f32)).astype(bf16)


def add_incoming(one, two, ahead, behind, tile=1024):
    rows, model = one.shape
    return call(
        add_kernel,
        [(one.shape, bf16)] * 2,
        [tile_spec((a.shape[0], tile), lambda i: (0, i)) for a in (one, two, ahead, behind)],
        (one, two, ahead, behind),
        [tile_spec((rows, tile), lambda i: (0, i))] * 2,
        grid=(model // tile,), limit=SMALL)


class Scatter:
    def send(self, one, two):
        self.ahead = lax.ppermute(one, GROUP, ring_perm(1))
        self.behind = lax.ppermute(two, GROUP, ring_perm(-1))

    def step(self, line, one, two, wait=()):
        self.send(*line(add_incoming, one, two, self.ahead, self.behind, wait=wait))


def total_slot_kernel(half, mine, came, result):
    result[...] = (mine[...].astype(f32) + came[...].reshape(mine.shape).astype(f32)).astype(bf16)


def total_slot(half, mine, came, step=2):
    entries, rows, columns = mine.shape
    block = (entries // step, rows, columns)
    return call(
        total_slot_kernel,
        [(mine.shape, bf16)],
        [
            tile_spec(block, lambda i: (i, 0, 0)),
            pl.BlockSpec((1, *block), lambda i, x: (1 - x[0], i, 0, 0)),
        ],
        (half, mine, came),
        [tile_spec(block, lambda i: (i, 0, 0))],
        grid=(step,),
        prefetch=1, limit=SMALL)[0]


def total_kernel(mine, came, *results):
    total = mine[...].astype(f32) + came[...].astype(f32)
    at = 0
    for result in results:
        rows = result.shape[0]
        result[...] = total[at : at + rows].astype(result.dtype)
        at += rows


def total_rows(mine, came, pieces):
    tail = mine.shape[1:]
    steps = 2
    tile = tail[:-1] + (tail[-1] // steps,)

    def spec(rows):
        return tile_spec((rows, *tile), lambda i: (0,) * len(tile) + (i,))

    return call(
        total_kernel,
        [((rows, *tail), dtype) for rows, dtype in pieces],
        [spec(mine.shape[0])] * 2,
        (mine, came),
        [spec(rows) for rows, _ in pieces],
        grid=(steps,), limit=SMALL)


def apart(values, half, kept, sent):
    cut = values.shape[0] // 2
    low = half[0] == 0
    first, second = values[:cut], values[cut:]
    kept[...] = jnp.where(low, first, second).astype(kept.dtype)
    sent[...] = jnp.where(low, second, first).astype(sent.dtype)


def mixed_kernel(half, own, ahead, behind, tokens, bias_one, bias_two, kept, sent):
    total = own[...].astype(f32) + ahead[...].astype(f32) + behind[...].astype(f32) + tokens[...].astype(f32)
    apart(total + bias_one[...] + bias_two[...], half, kept, sent)


def by_rows(kernel, half, operands, tokens):
    rows, model = tokens.shape
    return call(
        kernel,
        [((rows // 2, model), bf16)] * 2,
        [tile_spec((rows, 1), lambda i: (0, 0)) if a.shape[1] == 1 else same(a.shape) for a in operands],
        (half, *operands),
        [same((rows // 2, model))] * 2,
        grid=(1,),
        prefetch=1, limit=SMALL)


def mixed_rows(half, *operands):
    return by_rows(mixed_kernel, half, operands, operands[3])


def vectors_kernel(share, early, late, grad, grad_qkv, up_sum, result):
    result[...] = jnp.zeros_like(result)
    result[:4] = early[:4] + late[:4]
    result[4:5] = jnp.sum(grad[...].astype(f32), axis=0, keepdims=True)
    qkv_sum = jnp.sum(grad_qkv[...].astype(f32), axis=0, keepdims=True)
    for i in range(3):
        at = pl.multiple_of(share[0] * HD, HD)
        result[5 + i : 6 + i, pl.ds(at, HD)] = qkv_sum[:, i * HD : (i + 1) * HD]
    columns = up_sum.shape[1]
    each = result.shape[1] // columns
    at = pl.multiple_of((share[0] % each) * columns, columns)
    result[pl.ds(8 + share[0] // each, 1), pl.ds(at, columns)] = up_sum[...]


def vectors(share, early, late, grad, grad_qkv, up_sum):
    operands = (early, late, grad, grad_qkv, up_sum)
    return call(
        vectors_kernel,
        [((16, early.shape[1]), f32)],
        [same(a.shape) for a in operands],
        (share, *operands),
        [same((16, early.shape[1]))],
        grid=(1,),
        prefetch=1, limit=SMALL)[0]


def sum_kernel(*refs):
    total = refs[0][...]
    for ref in refs[1:-1]:
        total = total + ref[...]
    refs[-1][...] = total


def sum_arrays(*arrays):
    return call(
        sum_kernel, [(arrays[0].shape, f32)], [whole_ref()] * len(arrays), arrays, [whole_ref()], limit=SMALL)[0]


def finish_kernel(half, own, ahead, behind, tokens, grad, mean, scale, kept, sent):
    pulled = own[...].astype(f32) + ahead[...].astype(f32) + behind[...].astype(f32)
    normal = (tokens[...].astype(f32) - mean[...]) * scale[...]
    inner = (
        pulled
        - jnp.mean(pulled, axis=-1, keepdims=True)
        - normal * jnp.mean(pulled * normal, axis=-1, keepdims=True)
    )
    apart(grad[...].astype(f32) + scale[...] * inner, half, kept, sent)


def finish(half, *operands):
    return by_rows(finish_kernel, half, operands, operands[3])


def trade_kernel(half, *refs):
    count = len(refs) // 3
    low = half[0] == 0
    for values, came, result in zip(refs[:count], refs[count : 2 * count], refs[2 * count :]):
        rows = came.shape[0]
        own = values[pl.ds(half[0], 1)][0]
        result[:rows] = jnp.where(low, own, came[...])
        result[rows:] = jnp.where(low, came[...], own)


def trade(half, arrays, came):
    shapes = [(2 * piece.shape[0], piece.shape[1]) for piece in came]
    return call(
        trade_kernel,
        [(shape, bf16) for shape in shapes],
        [same(a.shape) for a in (*arrays, *came)],
        (half, *arrays, *came),
        [same(shape) for shape in shapes],
        grid=(1,),
        prefetch=1,
    )


def in_order_kernel(half, *refs):
    count = len(refs) // 3
    for own, came, result in zip(refs[:count], refs[count : 2 * count], refs[2 * count :]):
        low = half[0] == 0
        result[0] = jnp.where(low, own[...], came[...])
        result[1] = jnp.where(low, came[...], own[...])


def in_order(half, own, came):
    operands = (*own, *came)
    return call(
        in_order_kernel,
        [((2, *a.shape), a.dtype) for a in own],
        [same(a.shape) for a in operands],
        (half, *operands),
        [same((2, *a.shape)) for a in own],
        grid=(1,),
        prefetch=1, limit=SMALL)


def scalar(value):
    return jnp.reshape(value, (1,)).astype(jnp.int32)


def grouped(
    tokens,
    segments,
    ln1_gain,
    ln1_bias,
    qkv_weight,
    qkv_bias,
    out_weight,
    out_bias,
    ln2_gain,
    ln2_bias,
    fc1_weight,
    fc1_bias,
    fc2_weight,
    fc2_bias,
    cotangent,
):
    depth, width = lax.axis_size("z"), lax.axis_size("y")
    share = depth * width
    devices = share * TURNS
    z, y, x, c = (lax.axis_index(name) for name in EVERY)
    t = z * width + y
    mine = x * CORES + c
    r = jnp.where(y == 0, z, 2 * depth - 1 - z)
    seqs, rows, model = tokens.shape
    block = seqs * rows
    slim = ln1_gain.shape[0]
    hidden = fc2_weight.shape[0] * TURNS
    line = Line()

    sent = line(lambda up, qkv: spread(up, qkv, share), fc1_weight, qkv_weight)
    columns = lax.all_to_all(sent, GROUP, 0, 0, tiled=True)

    down_out = (out_weight[None], fc2_weight[None])
    down_out_near = [swap(piece, "c") for piece in line.hold(down_out)]
    came = [
        swap(lax.dynamic_index_in_dim(rows_of, 1 - x, 0, keepdims=False), "x")
        for rows_of in line.hold((tokens, cotangent))
    ]

    pieces = (
        ln1_gain,
        ln1_bias,
        ln2_gain,
        ln2_bias,
        out_bias,
        fc2_bias,
        qkv_bias,
        fc1_bias,
        segments.reshape(-1).astype(bf16),
    )
    ends = [0]
    for piece in pieces:
        ends.append(ends[-1] + piece.shape[0])
    packed = jnp.concatenate(line.hold(pieces))
    packed = jnp.pad(packed, (0, -ends[-1] % 1024)).reshape(1, -1, 128)
    for axis in ("c", "x", "y"):
        packed = jnp.concatenate([packed, swap(packed, axis)], axis=0)
    packed = [packed] + [
        lax.ppermute(packed, "z", [(i, (i + shift) % depth) for i in range(depth)]) for shift in range(1, depth)
    ]
    steps = (r + jnp.array(ORDER, jnp.int32)) % share
    far_of = (steps >= depth).astype(jnp.int32)
    depth_of = jnp.where(far_of == 1, 2 * depth - 1 - steps, steps)
    within = (jnp.arange(2, dtype=jnp.int32) * CORES + c)[:, None] * rows + jnp.arange(rows, dtype=jnp.int32)
    token_pos = far_of[:, None] * (TURNS * rows) + within.reshape(1, -1)
    token_tables = line(rotary_tables, token_pos.reshape(-1))
    seq_tables = line(rotary_tables, jnp.arange(rows * width * TURNS, dtype=jnp.int32))

    my_rows, my_grad = line(trade, scalar(x), (tokens, cotangent), came, wait=packed[0])
    down_out_far = [swap(piece, "x") for piece in line.hold(down_out)]
    packed = line(settle, scalar(z), scalar(y * TURNS + mine), *packed, wait=down_out_near).reshape(devices, -1)
    down_out_last = [swap(piece, "c") for piece in line.hold(down_out_far)]
    in_ring = Gather(my_rows)
    in_ring.step(line, columns, *down_out_last)
    small = [
        packed[:, ends[i] : ends[i + 1]].astype(f32).reshape(1, -1) for i in range(4, len(pieces) - 1)
    ]
    bias_out, bias_down, bias_qkv, bias_up = small
    affine = packed[:, : ends[4]].astype(f32).reshape(devices, 4, slim).transpose(1, 0, 2).reshape(4, model)
    bias_up = lax.dynamic_slice_in_dim(bias_up, t * hidden, hidden, 1)
    bias_qkv = lax.dynamic_index_in_dim(
        bias_qkv.reshape(3, HEADS, HD), t, 1, keepdims=False
    ).reshape(1, 3 * HD)

    all_seg = packed[:, ends[-2] : ends[-1]].reshape(depth, width * TURNS, seqs, rows)
    seq_seg = lax.dynamic_slice_in_dim(all_seg, c * 2, 2, 0)
    seq_seg = lax.dynamic_index_in_dim(seq_seg, x, 2, keepdims=False).reshape(2, -1).astype(f32)
    masks = (seq_seg[:, None, :],)

    def norm(at, kept):
        pieces = in_ring.held[ORDER[at]]
        return line(lambda *given: norm_block(at, *given, slim), pieces, affine, kept)

    kept = norm(0, None)
    qkv_cols, up_cols = after((columns[:, :, : 3 * HD], columns[:, :, 3 * HD :]), columns)
    qkv_far, up_far = swap(qkv_cols, "x"), swap(up_cols, "x")
    qkv_near, up_near = swap(qkv_cols, "c"), swap(up_cols, "c")
    weight_out, weight_down = (
        line(assemble, pieces, scalar(mine))
        for pieces in zip(down_out, down_out_near, down_out_far, down_out_last)
    )
    in_ring.step(line)
    kept = norm(1, kept)
    kept = norm(2, kept)
    in_ring.step(line)
    qkv_last = swap(line.hold(qkv_far), "c")
    kept = norm(3, kept)
    kept = norm(4, kept)
    weight_qkv = line(assemble, (qkv_cols, qkv_near, qkv_far, qkv_last), scalar(mine))
    in_ring.step(line)
    kept = norm(5, kept)
    kept = norm(6, kept)
    grad_ring = Gather(my_grad)
    grad_ring.step(line, *in_ring.held[4])
    up_last = swap(line.hold(up_far), "c")
    act_one, act_two, means, scales, turned_one, turned_two = norm(7, kept)

    lie = (depth_of, far_of, scalar(c))
    qkv_mine, sent = line(
        lambda *given: project(*given, block), act_one, weight_qkv, bias_qkv, token_tables, *lie
    )
    grad_ring.step(line)
    qkv_came = swap(sent, "c")
    weight_up = line(assemble, (up_cols, up_near, up_far, up_last), scalar(mine))
    out_mine, sent = line(
        lambda *given: attend(forward_kernel, rows, HD, *given), scalar(c), masks, qkv_mine, qkv_came
    )
    out_came = swap(sent, "c")
    grad_ring.step(line)
    act_hidden, slope, hidden_turned = line(widen, act_two, weight_up, bias_up)
    grad_ring.step(line)
    attended, attended_turned = line(lambda *given: place(*given, turn=True), out_mine, out_came, *lie)

    out_own, *out_late = line(
        lambda a, b: share_part(False, 0, len(ORDER), block, a, b, all_pieces(block)),
        (attended, act_hidden),
        (weight_out, weight_down),
    )
    out_late, (one, two, *out_early) = out_late[:4], out_late[4:]
    out_ring = Scatter()

    grads = [piece for j in ORDER for piece in grad_ring.held[j]]
    grad_mine, sent = line(lambda *given: head_grads(*given, block), grads, weight_out, *lie)
    grad_came = swap(sent, "c")
    out_ring.send(*line.hold((one, two)))
    grad_hidden, up_sum = line(narrow, grads, weight_down, slope)
    which = (scalar(c), scalar(x))
    (up_far,) = line(rows_grad, turned_two, grad_hidden, *which)
    back_mine, sent = line(
        lambda *given: attend(backward_kernel, rows, 3 * HD, *given),
        scalar(c),
        (*masks, *seq_tables),
        qkv_mine,
        qkv_came,
        grad_mine,
        grad_came,
        wait=(out_ring.ahead, out_ring.behind),
    )
    back_came = swap(sent, "c")
    out_ring.step(line, *out_early)
    up_came = swap(line.hold(up_far), "c")
    down_lefts = (
        attended_turned.reshape(2, CORES, slim, -1),
        hidden_turned.reshape(2, CORES, hidden // TURNS, -1),
    )
    (down_far,) = line(down_grad, *down_lefts, grads, *which)
    (grad_qkv,) = line(place, back_mine, back_came, *lie)
    (qkv_far,) = line(rows_grad, turned_one, grad_qkv, *which)
    grad_up, up_far = line(
        lambda *given: rows_grad(*given, slots=True), turned_two, grad_hidden, *which, up_came
    )
    out_ring.step(line, out_late[2], out_late[3])
    qkv_came = swap(line.hold(qkv_far), "c")
    up_came = lax.all_to_all(line.hold(up_far), "x", 0, 0, tiled=True)

    lefts, rights = (grad_qkv, grad_hidden), (weight_qkv, weight_up)

    def pull(first, count, pieces):
        values = [piece for j in ORDER[first : first + count] for piece in in_ring.held[j]]
        return line(
            lambda left, right, more: share_part(True, first, count, block, left, right, pieces, more),
            lefts,
            rights,
            ((affine,), values, means, scales),
        )

    early_sums, one, two, *early = pull(5, 3, early_pieces(block))
    pull_ring = Scatter()
    pull_ring.send(one, two)
    out_ring.step(line, out_late[0], out_late[1])
    late_sums, pull_own, *late = pull(0, 5, late_pieces(block))
    sums = line(vectors, scalar(t), early_sums, late_sums, my_grad, grad_qkv, up_sum)
    grad_qkv_w, qkv_far = line(rows_grad, turned_one, grad_qkv, *which, qkv_came)
    grad_up = line(total_slot, scalar(x), grad_up, up_came)
    pull_ring.step(line, *early, wait=(out_ring.ahead, out_ring.behind))
    grad_up = lax.all_to_all(line.hold(grad_up), GROUP, 0, 0, tiled=True)
    qkv_came, down_came = swap(line.hold(qkv_far), "x"), swap(line.hold(down_far), "c")
    sums_came = swap(line.hold(sums), "c")
    sums = line(sum_arrays, sums, sums_came)
    grad_down, down_far = line(down_grad, *down_lefts, grads, *which, down_came)
    pull_ring.step(line, late[2], late[3])
    sums_came = swap(line.hold(sums), "x")
    sums = line(sum_arrays, sums, sums_came)

    def slices(values, rows):
        cut = values.reshape(rows, share, TURNS, -1)
        return lax.dynamic_index_in_dim(cut, mine, 2, keepdims=False).transpose(1, 0, 2).reshape(share, -1)

    sums = jnp.concatenate([slices(sums[:5], 5), slices(sums[5:8], 1), slices(sums[8:12], 1)], axis=1)
    sums = jnp.pad(sums.reshape(share, -1, 128), ((0, 0), (0, 2), (0, 0)))
    grad_qkv_w = line(total_with, grad_qkv_w, qkv_came, sums)
    pull_ring.step(line, late[0], late[1])
    grad_qkv_w = lax.all_to_all(line.hold(grad_qkv_w), GROUP, 0, 0, tiled=True)
    down_came = swap(line.hold(down_far), "x")
    (grad_up,) = line(lambda given: join(given, 1), grad_up)
    kept_out, sent_out = line(
        mixed_rows, scalar(x), out_own, out_ring.ahead, out_ring.behind, my_rows, bias_out, bias_down
    )
    grad_out, grad_down = line(
        lambda a, b: total_rows(a, b, [(slim, f32), (hidden // TURNS, f32)]), grad_down, down_came
    )
    grad_qkv_w, sums = line(lambda given: join(given, 3, (8, 128)), grad_qkv_w)
    kept_in, sent_in = line(
        finish, scalar(x), pull_own, pull_ring.ahead, pull_ring.behind, my_rows, my_grad, means, scales
    )
    came_in, came_out = (swap(sent, "x") for sent in line.hold((sent_in, sent_out)))
    mixed, grad_in = line(in_order, scalar(x), (kept_out, kept_in), (came_out, came_in))

    sums = sums.reshape(-1)
    norm_sums = [sums[i * slim : (i + 1) * slim] for i in range(5)]
    qkv_end = 5 * slim + qkv_bias.shape[0]
    return (
        mixed,
        grad_in,
        norm_sums[0],
        norm_sums[1],
        grad_qkv_w,
        sums[5 * slim : qkv_end],
        grad_out,
        norm_sums[4],
        norm_sums[2],
        norm_sums[3],
        grad_up,
        sums[qkv_end : qkv_end + fc1_bias.shape[0]],
        grad_down,
        norm_sums[4],
    )


def specs(batch, block):
    every = batch + block
    one, two, three = P(every), P(every, None), P(batch, block, None)
    arguments = (three, P(batch, block), one, one, two, one, two, one, one, one, two, one, two, one, three)
    results = (three, three, one, one, two, one, two, one, one, one, two, one, two, one)
    return arguments, results


def solution(mesh):
    depth, ring = mesh.shape["dp"], mesh.shape["seq"]
    width = ring // TURNS
    if width == 2 and depth == TURNS and depth * width == HEADS:
        chips = Mesh(mesh.devices.reshape(depth, width, 2, CORES), EVERY)
        arguments, results = specs(("z",), ("y", "x", "c"))
        return jax.shard_map(
            grouped, mesh=chips, in_specs=arguments, out_specs=results, check_vma=False
        )
    arguments, results = specs(("dp",), ("seq",))
    return jax.shard_map(
        per_device, mesh=mesh, in_specs=arguments, out_specs=results, check_vma=False
    )
```
